32 devices in a mesh: tm: 8 (over y, x, core), space: 4 (over z).
Axes of the slice: x: 2, y: 2, z: 4, core: 2. Of those that a mesh axis runs over, the one named last changes fastest.
Arguments:
- state: float32 [64, 96, 128], P('tm', 'space'), may hold values from -6 to 6
- forcing: float32 [64, 96, 128], P('tm', 'space'), may hold values from -6 to 6
- initial: float32 [96, 128], P('space'), may hold values from -6 to 6
- blocks: bfloat16 [5, 96, 128, 128], P(None, 'space'), may hold values from -0.25 to 0.25
- precond: bfloat16 [96, 128, 128], P('space'), may hold values from -0.5 to 0.5
- couple: int32 [96, 5], P('space'), may hold values from -2 to 2
Outputs:
- corrected: float32 [64, 96, 128], P('tm', 'space')
The draws below stay inside these ranges and needn't reach their ends.
Inputs may be any that keep to these rules, and one draw needn't show every extreme that they name: Row j, slot s couples to block row j + couple[j, s].
All inputs are finite; a program needn't handle non-finite values.
Results may differ from the reference program's by a relative error of at most 0.002.
Values may be sent and summed in bfloat16 or wider, within the bound.
A program may use at most 64 MiB of HBM per device.

```python
import math
import jax
import jax.numpy as jnp

BS = 128
SWEEPS = 2
NT = 64
NB = 96


def touch_ends(drawn, own_key, smallest, high):
    dims = drawn.shape
    place = [jax.random.randint(jax.random.fold_in(own_key, axis), (), 0, dims[axis]) for axis in range(len(dims))]
    drawn = drawn.at[tuple(place)].set(smallest)
    longest = dims.index(max(dims))
    place[longest] = (place[longest] + 1) % dims[longest]
    return drawn.at[tuple(place)].set(high)


def block_scale(own_key, shape, pieces, smallest, high):
    def one(axis_at, shards_of):
        draws = jax.random.uniform(jax.random.fold_in(jax.random.fold_in(own_key, 6), axis_at), (shards_of,), jnp.float32, smallest / len(pieces), high / len(pieces))
        return jnp.repeat(jnp.exp(draws), shape[axis_at] // shards_of).reshape((-1,) + (1,) * (len(shape) - axis_at - 1))

    factor_of = one(*pieces[0])
    for cut in pieces[1:]:
        factor_of = factor_of * one(*cut)
    return factor_of


def noise(stream_key, shape, scale, bound, pieces=(), kind=jnp.bfloat16):
    drawn = jax.random.normal(stream_key, shape, jnp.float32) * scale
    if len(pieces) > 0:
        drawn = block_scale(stream_key, shape, pieces, -0.22, 0.18) * drawn
    return jnp.clip(drawn, min=-bound, max=bound).astype(kind)


def setup_inputs(seed: int = 0) -> dict:
    splits = jax.random.split(jax.random.key(seed), 7)
    return {
        "state": noise(splits[0], (NT, NB, BS), 1.0, 6.0, ((0, 8), (1, 4)), jnp.float32),
        "forcing": noise(splits[1], (NT, NB, BS), 1.0, 6.0, ((0, 8), (1, 4)), jnp.float32),
        "initial": noise(splits[2], (NB, BS), 1.0, 6.0, ((0, 4),), jnp.float32),
        "blocks": noise(splits[3], (5, NB, BS, BS), (5 * BS) ** -0.5, 0.25, ((1, 4),)),
        "precond": noise(splits[4], (NB, BS, BS), BS ** -0.5, 0.5, ((0, 4),)),
        "couple": touch_ends(jax.random.randint(splits[5], (NB, 5), -2, 3), jax.random.fold_in(splits[5], 1), -2, 2).astype(jnp.int32),
    }


alpha_rate = 0.5
time_step = 0.5
relaxation = 0.7


def neighbour_rows(padded, couple, column, width):
    chosen = padded[:, 2:2 + width]
    for offset in range(-2, 3):
        picked = (couple[:, column] == offset)[None, :, None]
        chosen = jnp.where(picked, padded[:, 2 + offset:2 + offset + width], chosen)
    return chosen


def apply_blocks(vectors, blocks, couple):
    rounded = vectors.astype(jnp.bfloat16)
    width = rounded.shape[1]
    padded = jnp.pad(rounded, ((0, 0), (2, 2), (0, 0)))
    total = jnp.zeros(vectors.shape, jnp.float32)
    for column in range(5):
        chosen = neighbour_rows(padded, couple, column, width)
        total = total + jnp.einsum('fbj,bij->fbi', chosen.astype(jnp.float32), blocks[column].astype(jnp.float32))
    return total


def precondition(vectors, precond):
    rounded = vectors.astype(jnp.bfloat16).astype(jnp.float32)
    return jnp.einsum('fbj,bij->fbi', rounded, precond.astype(jnp.float32))


def reference(state, forcing, initial, blocks, precond, couple):
    total_steps = state.shape[0]
    previous = jnp.concatenate([initial[None], state[:-1]], 0)
    squares = (0.5 * state * state).astype(jnp.bfloat16)
    flux = apply_blocks(squares.astype(jnp.float32), blocks, couple)
    residual = forcing - state + previous - time_step * flux
    steps_index = jnp.arange(total_steps).astype(jnp.float32)
    log_rate = math.log(alpha_rate) / total_steps
    scaled = residual * jnp.exp(steps_index * log_rate)[:, None, None]
    spectrum = jnp.fft.fft(scaled, axis=0)
    spec_re = jnp.real(spectrum).astype(jnp.float32)
    spec_im = jnp.imag(spectrum).astype(jnp.float32)
    theta = 2.0 * math.pi * steps_index / total_steps
    rate = math.exp(log_rate)
    lam_re = (1.0 - rate * jnp.cos(theta))[:, None, None]
    lam_im = (rate * jnp.sin(theta))[:, None, None]
    denom = (1.0 + lam_re) ** 2 + lam_im ** 2
    coef_re = (1.0 + lam_re) / denom
    coef_im = -lam_im / denom
    sol_re = jnp.zeros(state.shape, jnp.float32)
    sol_im = jnp.zeros(state.shape, jnp.float32)
    for sweep in range(SWEEPS):
        applied = apply_blocks(jnp.concatenate([sol_re, sol_im], 0), blocks, couple)
        res_re = spec_re - (lam_re * sol_re - lam_im * sol_im) - time_step * applied[:total_steps]
        res_im = spec_im - (lam_re * sol_im + lam_im * sol_re) - time_step * applied[total_steps:]
        gres = precondition(jnp.concatenate([res_re, res_im], 0), precond)
        g_re = gres[:total_steps]
        g_im = gres[total_steps:]
        sol_re = sol_re + relaxation * (coef_re * g_re - coef_im * g_im)
        sol_im = sol_im + relaxation * (coef_re * g_im + coef_im * g_re)
    inverse = jnp.real(jnp.fft.ifft(sol_re + 1j * sol_im, axis=0))
    change = inverse * jnp.exp(-steps_index * log_rate)[:, None, None]
    return state + change
```

```python
import functools
import math

import jax
import jax.numpy as jnp
import numpy as np
from jax import lax
from jax.experimental import pallas as pl
from jax.experimental.pallas import tpu as pltpu
from jax.sharding import PartitionSpec as P

SWEEPS = 2


alpha_rate = 0.5
time_step = 0.5
relaxation = 0.7


def from_behind(block, axis, distance):
    devices = range(lax.axis_size(axis))
    route = [(i - distance, i) for i in devices if i - distance in devices]
    return lax.ppermute(block, axis, route)


def extended(block, sides, width):
    for axis, dim in sides:
        count = lax.axis_size(axis)
        forward = [(i, i + 1) for i in range(count - 1)]
        backward = [(target, source) for source, target in forward]
        low = lax.ppermute(
            lax.slice_in_dim(block, block.shape[dim] - width, None, axis=dim), axis, forward
        )
        high = lax.ppermute(lax.slice_in_dim(block, 0, width, axis=dim), axis, backward)
        block = jnp.concatenate([low, block, high], axis=dim)
    return block


def from_partner(block, axis, stride):
    count = lax.axis_size(axis)
    route = []
    for low in range(count):
        high = low | 1 << stride
        if high != low and high < count:
            route += [(low, high), (high, low)]
    return lax.ppermute(block, axis, route)


def apply_padded(padded, blocks, couple):
    width = padded.shape[1] - 4
    total = None
    for column in range(5):
        chosen = padded[:, 2 : 2 + width]
        for offset in range(-2, 3):
            picked = (couple[:, column] == offset)[None, :, None]
            chosen = jnp.where(picked, padded[:, 2 + offset : 2 + offset + width], chosen)
        term = jnp.einsum(
            "fbj,bij->fbi", chosen, blocks[column], preferred_element_type=jnp.float32
        )
        total = term if total is None else total + term
    return total


def on_device_steps(state, forcing, initial, blocks, precond, couple):
    local_steps = state.shape[0]
    devices_tm = lax.axis_size("tm")
    position = lax.axis_index("tm")
    total_steps = local_steps * devices_tm
    level_count = devices_tm.bit_length() - 1
    highest = lax.Precision.HIGHEST
    last_step = from_behind(state[-1:], "tm", 1)
    first_prev = jnp.where(position == 0, initial[None], last_step)
    previous = jnp.concatenate([first_prev, state[:-1]], 0)
    squares = (0.5 * state * state).astype(jnp.bfloat16)
    padded = extended(squares, (("space", 1),), 2)
    flux = apply_padded(padded, blocks, couple)
    residual = forcing - state + previous - time_step * flux
    steps_global = position * local_steps + jnp.arange(local_steps, dtype=jnp.int32)
    log_rate = math.log(alpha_rate) / total_steps
    scaled = residual * jnp.exp(steps_global.astype(jnp.float32) * log_rate)[:, None, None]
    cur_re = scaled
    cur_im = jnp.zeros_like(scaled)
    for level in range(level_count):
        bit_number = level_count - 1 - level
        half = 1 << bit_number
        other = from_partner(jnp.stack([cur_re, cur_im]), "tm", bit_number)
        upper = position >> bit_number & 1 == 1
        angle = -2.0 * math.pi * (position % half).astype(jnp.float32) / (2 * half)
        tw_re = jnp.cos(angle)
        tw_im = jnp.sin(angle)
        diff_re = other[0] - cur_re
        diff_im = other[1] - cur_im
        new_re = jnp.where(upper, diff_re * tw_re - diff_im * tw_im, cur_re + other[0])
        new_im = jnp.where(upper, diff_re * tw_im + diff_im * tw_re, cur_im + other[1])
        cur_re, cur_im = (new_re, new_im)
    freq_base = jnp.zeros((), jnp.int32)
    for level in range(level_count):
        freq_base = freq_base + (position >> level & 1) * (1 << level_count - 1 - level)
    part_re, part_im = (cur_re, cur_im)
    local_index = jnp.arange(local_steps, dtype=jnp.int32)
    freq = freq_base + devices_tm * local_index
    product = freq[:, None] * local_index[None, :] % total_steps
    angle_table = 2.0 * math.pi * product.astype(jnp.float32) / total_steps
    table_re = jnp.cos(angle_table)
    table_im = -jnp.sin(angle_table)
    spec_re = jnp.einsum("qm,mbc->qbc", table_re, part_re, precision=highest) - jnp.einsum(
        "qm,mbc->qbc", table_im, part_im, precision=highest
    )
    spec_im = jnp.einsum("qm,mbc->qbc", table_re, part_im, precision=highest) + jnp.einsum(
        "qm,mbc->qbc", table_im, part_re, precision=highest
    )
    theta = 2.0 * math.pi * freq.astype(jnp.float32) / total_steps
    rate = math.exp(log_rate)
    lam_re = (1.0 - rate * jnp.cos(theta))[:, None, None]
    lam_im = (rate * jnp.sin(theta))[:, None, None]
    denom = (1.0 + lam_re) ** 2 + lam_im**2
    coef_re = (1.0 + lam_re) / denom
    coef_im = -lam_im / denom
    sol_re = None
    sol_im = None
    for sweep in range(SWEEPS):
        if sweep == 0:
            res_re, res_im = (spec_re, spec_im)
        else:
            stacked = jnp.concatenate([sol_re, sol_im], 0).astype(jnp.bfloat16)
            padded_sol = extended(stacked, (("space", 1),), 2)
            applied = apply_padded(padded_sol, blocks, couple)
            res_re = (
                spec_re - (lam_re * sol_re - lam_im * sol_im) - time_step * applied[:local_steps]
            )
            res_im = (
                spec_im - (lam_re * sol_im + lam_im * sol_re) - time_step * applied[local_steps:]
            )
        rounded = jnp.concatenate([res_re, res_im], 0).astype(jnp.bfloat16)
        gres = jnp.einsum("fbj,bij->fbi", rounded, precond, preferred_element_type=jnp.float32)
        g_re = gres[:local_steps]
        g_im = gres[local_steps:]
        step_re = relaxation * (coef_re * g_re - coef_im * g_im)
        step_im = relaxation * (coef_re * g_im + coef_im * g_re)
        if sweep == 0:
            sol_re, sol_im = (step_re, step_im)
        else:
            sol_re = sol_re + step_re
            sol_im = sol_im + step_im
    back_re = (
        jnp.einsum("qm,qbc->mbc", table_re, sol_re, precision=highest)
        + jnp.einsum("qm,qbc->mbc", table_im, sol_im, precision=highest)
    ) / local_steps
    back_im = (
        jnp.einsum("qm,qbc->mbc", table_re, sol_im, precision=highest)
        - jnp.einsum("qm,qbc->mbc", table_im, sol_re, precision=highest)
    ) / local_steps
    cur_re, cur_im = (back_re, back_im)
    for bit_number in range(level_count):
        half = 1 << bit_number
        other = from_partner(jnp.stack([cur_re, cur_im]), "tm", bit_number)
        upper = position >> bit_number & 1 == 1
        angle = -2.0 * math.pi * (position % half).astype(jnp.float32) / (2 * half)
        conj_re = jnp.cos(angle)
        conj_im = -jnp.sin(angle)
        other_tw_re = other[0] * conj_re - other[1] * conj_im
        other_tw_im = other[0] * conj_im + other[1] * conj_re
        mine_tw_re = cur_re * conj_re - cur_im * conj_im
        mine_tw_im = cur_re * conj_im + cur_im * conj_re
        new_re = jnp.where(upper, 0.5 * (other[0] - mine_tw_re), 0.5 * (cur_re + other_tw_re))
        new_im = jnp.where(upper, 0.5 * (other[1] - mine_tw_im), 0.5 * (cur_im + other_tw_im))
        cur_re, cur_im = (new_re, new_im)
    change = cur_re * jnp.exp(-steps_global.astype(jnp.float32) * log_rate)[:, None, None]
    return state + change


MESH = pl.DeviceIdType.MESH
NT_DIMS = (((1,), (1,)), ((), ()))
HIGHEST = lax.Precision.HIGHEST


def tables(steps):
    half = steps // 2
    rate = math.exp(math.log(alpha_rate) / steps)
    step = np.arange(steps)
    freq = np.arange(half)
    angle = 2.0 * np.pi * ((freq[:, None] * step[None, :]) % steps) / steps
    cosine, sine = np.cos(angle), np.sin(angle)
    nyquist = 1.0 - 2.0 * (step % 2)
    forward = np.concatenate([cosine, nyquist[None], -sine[1:]], 0) * rate**step
    inverse = np.concatenate([2.0 * cosine, nyquist[None], -2.0 * sine[1:]], 0)
    inverse[0] = 1.0
    inverse = inverse.T / steps * (rate ** (-step))[:, None]
    theta = 2.0 * np.pi * np.arange(half + 1) / steps
    lam = 1.0 - rate * np.exp(-1j * theta)
    lam[half] = lam[half].real
    coef = relaxation / (1.0 + lam)

    def columns(factor):
        real = np.concatenate([factor.real[:half], factor.real[half:], factor.real[1:half]])
        imag = np.concatenate([[0.0], factor.imag[1:half]])
        return real, np.concatenate([-imag, imag])

    coef_own, coef_swap = columns(coef)
    lam_own, lam_swap = columns(lam * coef)
    swap = np.roll(np.eye(steps), half, 1)
    inverse = inverse @ (np.diag(coef_own) + np.diag(coef_swap) @ swap)
    factors = np.zeros((steps, steps))
    lanes = -(-steps // 128) * 128
    for place, column in enumerate((coef_own, coef_swap, lam_own, lam_swap)):
        factors[:, place] = column
    stacked = np.stack([forward, inverse, factors])
    return np.pad(stacked, ((0, 0), (0, 0), (0, lanes - steps))).astype(np.float32)


def kernel(
    sizes,
    state_h,
    forcing_h,
    initial_h,
    blocks_h,
    precond_h,
    couple_s,
    table_h,
    out_ref,
    state_v,
    forcing_v,
    initial_v,
    wb,
    wp,
    table_v,
    chunk,
    edge,
    diff,
    rq,
    rd,
    redge,
    xsq,
    xsol,
    back,
    rback,
    local_sem,
    q_send,
    q_recv,
    d_send,
    d_recv,
    edge_send,
    edge_recv,
    halo_send,
    halo_recv,
    b_send,
    b_recv,
):
    nt, ns, steps, width, own = sizes
    total = nt * steps
    half = total // 2
    t = lax.axis_index("tm")
    s = lax.axis_index("space")
    first, last = t == 0, t == nt - 1
    below, above = s > 0, s < ns - 1
    lower, upper = jnp.maximum(s - 1, 0), jnp.minimum(s + 1, ns - 1)
    low_edge = jnp.logical_and(first, below)
    high_edge = jnp.logical_and(last, above)

    barrier = pltpu.get_barrier_semaphore()
    for o in range(1, nt):
        pl.semaphore_signal(
            barrier, inc=1, device_id=(lax.rem(t + o, nt), s), device_id_type=MESH
        )

    @pl.when(low_edge)
    def _():
        for o in range(nt):
            pl.semaphore_signal(barrier, inc=1, device_id=(o, lower), device_id_type=MESH)

    @pl.when(high_edge)
    def _():
        for o in range(nt):
            pl.semaphore_signal(barrier, inc=1, device_id=(o, upper), device_id_type=MESH)

    start = t * own
    loads = [
        pltpu.make_async_copy(source, target, local_sem.at[place])
        for place, (source, target) in enumerate(
            (
                (state_h, state_v),
                (forcing_h, forcing_v),
                (initial_h, initial_v),
                (blocks_h.at[:, pl.ds(start, own)], wb),
                (table_h, table_v),
                (precond_h.at[pl.ds(start, own)], wp),
            )
        )
    ]
    for load in loads:
        load.start()

    loads[0].wait()
    state = state_v[...]
    by_block = jnp.swapaxes(state, 0, 1)
    squares = 0.5 * by_block * by_block
    blank = jnp.zeros((steps, squares.shape[2]), jnp.float32)
    for target in range(nt):
        parts = []
        for j in range(own * target - 2, own * (target + 1) + 2):
            parts.append(squares[j] if 0 <= j < width else blank)
        tail = state[steps - 1, own * target : own * (target + 1)]
        tail_hi = tail.astype(jnp.bfloat16).astype(jnp.float32)
        parts += [tail_hi, tail - tail_hi]
        if steps > 2 * own:
            parts.append(blank[: steps - 2 * own])
        chunk[target] = jnp.concatenate(parts, 0).astype(jnp.bfloat16)
    edge[0] = jnp.concatenate([squares[width - 2], squares[width - 1]], 0).astype(jnp.bfloat16)
    edge[1] = jnp.concatenate([squares[0], squares[1]], 0).astype(jnp.bfloat16)

    signals = nt - 1 + jnp.where(below, 1, 0) + jnp.where(above, 1, 0)
    pl.semaphore_wait(barrier, signals)

    q_copies = []
    for o in range(1, nt):
        target = lax.rem(t + o, nt)
        q_copies.append(
            pltpu.make_async_remote_copy(
                src_ref=chunk.at[target],
                dst_ref=rq.at[t],
                send_sem=q_send.at[o],
                recv_sem=q_recv.at[o],
                device_id=(target, s),
                device_id_type=MESH,
            )
        )
    for copy in q_copies:
        copy.start()
    edge_up = pltpu.make_async_remote_copy(
        src_ref=edge.at[0],
        dst_ref=redge.at[t],
        send_sem=edge_send.at[0],
        recv_sem=edge_recv.at[t],
        device_id=(0, upper),
        device_id_type=MESH,
    )
    edge_down = pltpu.make_async_remote_copy(
        src_ref=edge.at[1],
        dst_ref=redge.at[t],
        send_sem=edge_send.at[1],
        recv_sem=edge_recv.at[t],
        device_id=(nt - 1, lower),
        device_id_type=MESH,
    )

    @pl.when(above)
    def _():
        edge_up.start()

    @pl.when(below)
    def _():
        edge_down.start()

    loads[1].wait()
    loads[2].wait()
    forcing = forcing_v[...]
    initial = jnp.where(first, initial_v[...], 0.0)
    previous = jnp.concatenate([initial[None], state[:-1]], 0)
    diff[...] = jnp.swapaxes(forcing - state + previous, 0, 1)
    d_copies = []
    for o in range(1, nt):
        target = lax.rem(t + o, nt)
        d_copies.append(
            pltpu.make_async_remote_copy(
                src_ref=diff.at[pl.ds(target * own, own)],
                dst_ref=rd.at[t],
                send_sem=d_send.at[o],
                recv_sem=d_recv.at[o],
                device_id=(target, s),
                device_id_type=MESH,
            )
        )
    for copy in d_copies:
        copy.start()
    rq[t] = chunk[t]
    rd[t] = diff[pl.ds(start, own)]

    for copy in q_copies:
        copy.wait_recv()
    got = [rq[source].astype(jnp.float32) for source in range(nt)]
    for e in range(own + 4):
        xsq[e] = jnp.concatenate(
            [part[e * steps : (e + 1) * steps] for part in got], 0
        ).astype(jnp.bfloat16)
    lead = (own + 4) * steps
    tails = [
        part[lead : lead + own] + part[lead + own : lead + 2 * own] for part in got[:-1]
    ]

    def take_edge(place):
        for source in range(nt):
            pltpu.make_async_remote_copy(
                src_ref=edge.at[0],
                dst_ref=redge.at[source],
                send_sem=edge_send.at[0],
                recv_sem=edge_recv.at[source],
                device_id=(0, 0),
                device_id_type=MESH,
            ).wait_recv()
        edges = [redge[source].astype(jnp.float32) for source in range(nt)]
        for e in range(2):
            xsq[place + e] = jnp.concatenate(
                [part[e * steps : (e + 1) * steps] for part in edges], 0
            ).astype(jnp.bfloat16)

    @pl.when(low_edge)
    def _():
        take_edge(0)

    @pl.when(high_edge)
    def _():
        take_edge(own + 2)

    loads[3].wait()

    def coupled(field, e):
        slots = wb.shape[0]
        rows = [field[e + 2 + couple_s[start + e, slot]] for slot in range(slots)]
        weights = [wb[slot, e] for slot in range(slots)]
        return lax.dot_general(
            jnp.concatenate(rows, 1),
            jnp.concatenate(weights, 1),
            NT_DIMS,
            preferred_element_type=jnp.float32,
        )

    def conditioned(rounded):
        size = wp.shape[1]
        return jnp.concatenate(
            [
                lax.dot_general(
                    rounded[:, e * size : (e + 1) * size],
                    wp[e],
                    NT_DIMS,
                    preferred_element_type=jnp.float32,
                )
                for e in range(own)
            ],
            1,
        )

    flux = [coupled(xsq, e) for e in range(own)]
    for copy in d_copies:
        copy.wait_recv()
    leading = lax.broadcasted_iota(jnp.int32, blank.shape, 0) == 0
    residual = []
    for e in range(own):
        parts = [rd[0, e]]
        for source in range(1, nt):
            carried = jnp.broadcast_to(tails[source - 1][e : e + 1], blank.shape)
            parts.append(rd[source, e] + jnp.where(leading, carried, 0.0))
        residual.append(jnp.concatenate(parts, 0) - time_step * flux[e])
    loads[4].wait()
    spectrum = jnp.dot(
        table_v[0][:, :total],
        jnp.concatenate(residual, 1),
        precision=HIGHEST,
        preferred_element_type=jnp.float32,
    )

    loads[5].wait()
    first_step = conditioned(spectrum.astype(jnp.bfloat16))
    swapped = jnp.concatenate([first_step[half:], first_step[:half]], 0)
    factors = table_v[2]
    sol = factors[:, 0:1] * first_step + factors[:, 1:2] * swapped
    size = wp.shape[1]
    for e in range(own):
        xsol[2 + e] = sol[:, e * size : (e + 1) * size].astype(jnp.bfloat16)

    has_down = jnp.logical_or(t > 0, below)
    has_up = jnp.logical_or(t < nt - 1, above)
    halo_down = pltpu.make_async_remote_copy(
        src_ref=xsol.at[pl.ds(2, 2)],
        dst_ref=xsol.at[pl.ds(own + 2, 2)],
        send_sem=halo_send.at[0],
        recv_sem=halo_recv.at[0],
        device_id=(jnp.where(first, nt - 1, t - 1), jnp.where(first, lower, s)),
        device_id_type=MESH,
    )
    halo_up = pltpu.make_async_remote_copy(
        src_ref=xsol.at[pl.ds(own, 2)],
        dst_ref=xsol.at[pl.ds(0, 2)],
        send_sem=halo_send.at[1],
        recv_sem=halo_recv.at[1],
        device_id=(jnp.where(last, 0, t + 1), jnp.where(last, upper, s)),
        device_id_type=MESH,
    )

    @pl.when(has_down)
    def _():
        halo_down.start()

    @pl.when(has_up)
    def _():
        halo_up.start()

    @pl.when(jnp.logical_not(has_down))
    def _():
        xsol[0:2] = jnp.zeros((2,) + xsol.shape[1:], jnp.bfloat16)

    @pl.when(jnp.logical_not(has_up))
    def _():
        xsol[own + 2 : own + 4] = jnp.zeros((2,) + xsol.shape[1:], jnp.bfloat16)

    left = spectrum - (factors[:, 2:3] * first_step + factors[:, 3:4] * swapped)

    @pl.when(has_down)
    def _():
        halo_up.wait_recv()

    @pl.when(has_up)
    def _():
        halo_down.wait_recv()

    applied = jnp.concatenate([coupled(xsol, e) for e in range(own)], 1)
    left = left - time_step * applied
    steps_sum = first_step + conditioned(left.astype(jnp.bfloat16))
    change = jnp.dot(
        table_v[1][:, :total], steps_sum, precision=HIGHEST, preferred_element_type=jnp.float32
    )
    for e in range(own):
        back[e] = change[:, e * size : (e + 1) * size]
    b_copies = []
    for o in range(1, nt):
        target = lax.rem(t + o, nt)
        b_copies.append(
            pltpu.make_async_remote_copy(
                src_ref=back.at[:, pl.ds(pl.multiple_of(target * steps, steps), steps)],
                dst_ref=rback.at[pl.ds(start, own)],
                send_sem=b_send.at[o],
                recv_sem=b_recv.at[o],
                device_id=(target, s),
                device_id_type=MESH,
            )
        )
    for copy in b_copies:
        copy.start()
    rback[pl.ds(start, own)] = back[:, pl.ds(pl.multiple_of(t * steps, steps), steps)]
    for copy in b_copies:
        copy.wait_recv()
    out_ref[...] = jnp.swapaxes(rback[...], 0, 1)

    for copy in q_copies + d_copies + b_copies:
        copy.wait_send()

    @pl.when(above)
    def _():
        edge_up.wait_send()

    @pl.when(below)
    def _():
        edge_down.wait_send()

    @pl.when(has_down)
    def _():
        halo_down.wait_send()

    @pl.when(has_up)
    def _():
        halo_up.wait_send()


def on_device_blocks(state, forcing, initial, blocks, precond, couple):
    nt, ns = lax.axis_size("tm"), lax.axis_size("space")
    steps, width, size = state.shape
    own = width // nt
    total = nt * steps
    slots = blocks.shape[0]
    table = jnp.asarray(tables(total))
    anywhere = pl.BlockSpec(memory_space=pl.ANY)
    rows = (own + 5) * steps
    f32, b16 = jnp.float32, jnp.bfloat16
    dma = pltpu.SemaphoreType.DMA
    change = pl.pallas_call(
        functools.partial(kernel, (nt, ns, steps, width, own)),
        out_shape=jax.ShapeDtypeStruct(state.shape, f32),
        in_specs=[anywhere] * 5 + [pl.BlockSpec(memory_space=pltpu.SMEM), anywhere],
        out_specs=pl.BlockSpec(memory_space=pltpu.VMEM),
        scratch_shapes=[
            pltpu.VMEM(state.shape, f32),
            pltpu.VMEM(state.shape, f32),
            pltpu.VMEM(initial.shape, f32),
            pltpu.VMEM((slots, own, size, size), b16),
            pltpu.VMEM((own, size, size), b16),
            pltpu.VMEM(table.shape, f32),
            pltpu.VMEM((nt, rows, size), b16),
            pltpu.VMEM((2, 2 * steps, size), b16),
            pltpu.VMEM((width, steps, size), f32),
            pltpu.VMEM((nt, rows, size), b16),
            pltpu.VMEM((nt, own, steps, size), f32),
            pltpu.VMEM((nt, 2 * steps, size), b16),
            pltpu.VMEM((own + 4, total, size), b16),
            pltpu.VMEM((own + 4, total, size), b16),
            pltpu.VMEM((own, total, size), f32),
            pltpu.VMEM((width, steps, size), f32),
            dma((6,)),
            dma((nt,)),
            dma((nt,)),
            dma((nt,)),
            dma((nt,)),
            dma((2,)),
            dma((nt,)),
            dma((2,)),
            dma((2,)),
            dma((nt,)),
            dma((nt,)),
        ],
        compiler_params=pltpu.CompilerParams(
            collective_id=0, has_side_effects=True, vmem_limit_bytes=24 * 1024 * 1024
        ),
    )(state, forcing, initial, blocks, precond, couple, table)
    return state + change


def on_device(state, forcing, initial, blocks, precond, couple):
    nt = lax.axis_size("tm")
    steps, width, _ = state.shape
    own = width // nt
    even_cut = width % nt == 0 and own >= 2 and 2 * own <= steps and steps % 8 == 0
    if nt > 1 and even_cut and (own + 5) * steps % 16 == 0:
        return on_device_blocks(state, forcing, initial, blocks, precond, couple)
    return on_device_steps(state, forcing, initial, blocks, precond, couple)


def solution(mesh):
    placed = (
        P("tm", "space", None),
        P("tm", "space", None),
        P("space", None),
        P(None, "space", None, None),
        P("space", None, None),
        P("space", None),
    )
    return jax.shard_map(
        on_device, mesh=mesh, in_specs=placed, out_specs=P("tm", "space", None), check_vma=False
    )
```

```python
import functools
import math

import jax
import jax.numpy as jnp
import numpy as np
from jax import lax
from jax.experimental import pallas as pl
from jax.experimental.pallas import tpu as pltpu
from jax.sharding import PartitionSpec as P

SWEEPS = 2


alpha_rate = 0.5
time_step = 0.5
relaxation = 0.7


def from_behind(block, axis, distance):
    devices = range(lax.axis_size(axis))
    route = [(i - distance, i) for i in devices if i - distance in devices]
    return lax.ppermute(block, axis, route)


def extended(block, sides, width):
    for axis, dim in sides:
        count = lax.axis_size(axis)
        forward = [(i, i + 1) for i in range(count - 1)]
        backward = [(target, source) for source, target in forward]
        low = lax.ppermute(
            lax.slice_in_dim(block, block.shape[dim] - width, None, axis=dim), axis, forward
        )
        high = lax.ppermute(lax.slice_in_dim(block, 0, width, axis=dim), axis, backward)
        block = jnp.concatenate([low, block, high], axis=dim)
    return block


def from_partner(block, axis, stride):
    count = lax.axis_size(axis)
    route = []
    for low in range(count):
        high = low | 1 << stride
        if high != low and high < count:
            route += [(low, high), (high, low)]
    return lax.ppermute(block, axis, route)


def apply_padded(padded, blocks, couple):
    width = padded.shape[1] - 4
    total = None
    for column in range(5):
        chosen = padded[:, 2 : 2 + width]
        for offset in range(-2, 3):
            picked = (couple[:, column] == offset)[None, :, None]
            chosen = jnp.where(picked, padded[:, 2 + offset : 2 + offset + width], chosen)
        term = jnp.einsum(
            "fbj,bij->fbi", chosen, blocks[column], preferred_element_type=jnp.float32
        )
        total = term if total is None else total + term
    return total


def on_device_steps(state, forcing, initial, blocks, precond, couple):
    local_steps = state.shape[0]
    devices_tm = lax.axis_size("tm")
    position = lax.axis_index("tm")
    total_steps = local_steps * devices_tm
    level_count = devices_tm.bit_length() - 1
    highest = lax.Precision.HIGHEST
    last_step = from_behind(state[-1:], "tm", 1)
    first_prev = jnp.where(position == 0, initial[None], last_step)
    previous = jnp.concatenate([first_prev, state[:-1]], 0)
    squares = (0.5 * state * state).astype(jnp.bfloat16)
    padded = extended(squares, (("space", 1),), 2)
    flux = apply_padded(padded, blocks, couple)
    residual = forcing - state + previous - time_step * flux
    steps_global = position * local_steps + jnp.arange(local_steps, dtype=jnp.int32)
    log_rate = math.log(alpha_rate) / total_steps
    scaled = residual * jnp.exp(steps_global.astype(jnp.float32) * log_rate)[:, None, None]
    cur_re = scaled
    cur_im = jnp.zeros_like(scaled)
    for level in range(level_count):
        bit_number = level_count - 1 - level
        half = 1 << bit_number
        other = from_partner(jnp.stack([cur_re, cur_im]), "tm", bit_number)
        upper = position >> bit_number & 1 == 1
        angle = -2.0 * math.pi * (position % half).astype(jnp.float32) / (2 * half)
        tw_re = jnp.cos(angle)
        tw_im = jnp.sin(angle)
        diff_re = other[0] - cur_re
        diff_im = other[1] - cur_im
        new_re = jnp.where(upper, diff_re * tw_re - diff_im * tw_im, cur_re + other[0])
        new_im = jnp.where(upper, diff_re * tw_im + diff_im * tw_re, cur_im + other[1])
        cur_re, cur_im = (new_re, new_im)
    freq_base = jnp.zeros((), jnp.int32)
    for level in range(level_count):
        freq_base = freq_base + (position >> level & 1) * (1 << level_count - 1 - level)
    part_re, part_im = (cur_re, cur_im)
    local_index = jnp.arange(local_steps, dtype=jnp.int32)
    freq = freq_base + devices_tm * local_index
    product = freq[:, None] * local_index[None, :] % total_steps
    angle_table = 2.0 * math.pi * product.astype(jnp.float32) / total_steps
    table_re = jnp.cos(angle_table)
    table_im = -jnp.sin(angle_table)
    spec_re = jnp.einsum("qm,mbc->qbc", table_re, part_re, precision=highest) - jnp.einsum(
        "qm,mbc->qbc", table_im, part_im, precision=highest
    )
    spec_im = jnp.einsum("qm,mbc->qbc", table_re, part_im, precision=highest) + jnp.einsum(
        "qm,mbc->qbc", table_im, part_re, precision=highest
    )
    theta = 2.0 * math.pi * freq.astype(jnp.float32) / total_steps
    rate = math.exp(log_rate)
    lam_re = (1.0 - rate * jnp.cos(theta))[:, None, None]
    lam_im = (rate * jnp.sin(theta))[:, None, None]
    denom = (1.0 + lam_re) ** 2 + lam_im**2
    coef_re = (1.0 + lam_re) / denom
    coef_im = -lam_im / denom
    sol_re = None
    sol_im = None
    for sweep in range(SWEEPS):
        if sweep == 0:
            res_re, res_im = (spec_re, spec_im)
        else:
            stacked = jnp.concatenate([sol_re, sol_im], 0).astype(jnp.bfloat16)
            padded_sol = extended(stacked, (("space", 1),), 2)
            applied = apply_padded(padded_sol, blocks, couple)
            res_re = (
                spec_re - (lam_re * sol_re - lam_im * sol_im) - time_step * applied[:local_steps]
            )
            res_im = (
                spec_im - (lam_re * sol_im + lam_im * sol_re) - time_step * applied[local_steps:]
            )
        rounded = jnp.concatenate([res_re, res_im], 0).astype(jnp.bfloat16)
        gres = jnp.einsum("fbj,bij->fbi", rounded, precond, preferred_element_type=jnp.float32)
        g_re = gres[:local_steps]
        g_im = gres[local_steps:]
        step_re = relaxation * (coef_re * g_re - coef_im * g_im)
        step_im = relaxation * (coef_re * g_im + coef_im * g_re)
        if sweep == 0:
            sol_re, sol_im = (step_re, step_im)
        else:
            sol_re = sol_re + step_re
            sol_im = sol_im + step_im
    back_re = (
        jnp.einsum("qm,qbc->mbc", table_re, sol_re, precision=highest)
        + jnp.einsum("qm,qbc->mbc", table_im, sol_im, precision=highest)
    ) / local_steps
    back_im = (
        jnp.einsum("qm,qbc->mbc", table_re, sol_im, precision=highest)
        - jnp.einsum("qm,qbc->mbc", table_im, sol_re, precision=highest)
    ) / local_steps
    cur_re, cur_im = (back_re, back_im)
    for bit_number in range(level_count):
        half = 1 << bit_number
        other = from_partner(jnp.stack([cur_re, cur_im]), "tm", bit_number)
        upper = position >> bit_number & 1 == 1
        angle = -2.0 * math.pi * (position % half).astype(jnp.float32) / (2 * half)
        conj_re = jnp.cos(angle)
        conj_im = -jnp.sin(angle)
        other_tw_re = other[0] * conj_re - other[1] * conj_im
        other_tw_im = other[0] * conj_im + other[1] * conj_re
        mine_tw_re = cur_re * conj_re - cur_im * conj_im
        mine_tw_im = cur_re * conj_im + cur_im * conj_re
        new_re = jnp.where(upper, 0.5 * (other[0] - mine_tw_re), 0.5 * (cur_re + other_tw_re))
        new_im = jnp.where(upper, 0.5 * (other[1] - mine_tw_im), 0.5 * (cur_im + other_tw_im))
        cur_re, cur_im = (new_re, new_im)
    change = cur_re * jnp.exp(-steps_global.astype(jnp.float32) * log_rate)[:, None, None]
    return state + change


MESH = pl.DeviceIdType.MESH
NT_DIMS = (((1,), (1,)), ((), ()))
HIGHEST = lax.Precision.HIGHEST


def tables(steps):
    half = steps // 2
    rate = math.exp(math.log(alpha_rate) / steps)
    step = np.arange(steps)
    freq = np.arange(half)
    angle = 2.0 * np.pi * ((freq[:, None] * step[None, :]) % steps) / steps
    cosine, sine = np.cos(angle), np.sin(angle)
    nyquist = 1.0 - 2.0 * (step % 2)
    forward = np.concatenate([cosine, nyquist[None], -sine[1:]], 0) * rate**step
    inverse = np.concatenate([2.0 * cosine, nyquist[None], -2.0 * sine[1:]], 0)
    inverse[0] = 1.0
    inverse = inverse.T / steps * (rate ** (-step))[:, None]
    theta = 2.0 * np.pi * np.arange(half + 1) / steps
    lam = 1.0 - rate * np.exp(-1j * theta)
    lam[half] = lam[half].real
    coef = relaxation / (1.0 + lam)

    def columns(factor):
        real = np.concatenate([factor.real[:half], factor.real[half:], factor.real[1:half]])
        imag = np.concatenate([[0.0], factor.imag[1:half]])
        return real, np.concatenate([-imag, imag])

    coef_own, coef_swap = columns(coef)
    lam_own, lam_swap = columns(lam * coef)
    swap = np.roll(np.eye(steps), half, 1)
    inverse = inverse @ (np.diag(coef_own) + np.diag(coef_swap) @ swap)
    lanes = -(-steps // 128) * 128
    factors = np.zeros((steps, lanes), np.float32)
    for place, column in enumerate((coef_own, coef_swap, lam_own, lam_swap)):
        factors[:, place] = column
    matrices = np.stack([np.tile(matrix, 2) for matrix in (forward, inverse)])
    return matrices.astype(np.float32), factors


def halves(field, axis):
    high = field.astype(jnp.bfloat16)
    low = (field - high.astype(jnp.float32)).astype(jnp.bfloat16)
    return jnp.concatenate([high, low], axis)


def transformed(matrix, field):
    both = halves(field, 0)
    return jnp.dot(
        halves(matrix, 1),
        jnp.concatenate([both, both], 0),
        preferred_element_type=jnp.float32,
    )


def bits_of(number, count):
    return [lax.rem(lax.div(number, 1 << i), 2) for i in range(count)]


def number_of(bits):
    return sum(bit * (1 << i) for i, bit in enumerate(bits))


def flipped(position, mask, count):
    bits = bits_of(position, count)
    return position + sum((1 - 2 * bits[i]) * (1 << i) for i in range(count) if mask >> i & 1)


def rank_at(position, s, count):
    bits = bits_of(position, count)
    for i in reversed(range(count - 1)):
        bits[i] = lax.rem(bits[i] + bits[i + 1], 2)
    rank = number_of(bits)
    return rank + lax.rem(s, 2) * ((1 << count) - 1 - 2 * rank)


def position_at(rank, s, count):
    rank = rank + lax.rem(s, 2) * ((1 << count) - 1 - 2 * rank)
    bits = bits_of(rank, count)
    for i in range(count - 1):
        bits[i] = lax.rem(bits[i] + bits[i + 1], 2)
    return number_of(bits)


def kernel(
    sizes,
    state_h,
    forcing_h,
    initial_h,
    blocks_h,
    precond_h,
    couple_s,
    matrix_h,
    factor_h,
    out_ref,
    state_v,
    forcing_v,
    initial_v,
    wb,
    wp,
    matrix_v,
    factor_v,
    chunk,
    edge,
    diff,
    rq,
    rd,
    redge,
    xsq,
    xsol,
    back,
    rback,
    local_sem,
    q_send,
    q_recv,
    d_send,
    d_recv,
    edge_send,
    edge_recv,
    halo_send,
    halo_recv,
    b_send,
    b_recv,
):
    nt, ns, steps, width, own = sizes
    total = nt * steps
    half = total // 2
    t = lax.axis_index("tm")
    s = lax.axis_index("space")
    level = nt.bit_length() - 1
    rank = rank_at(t, s, level)
    first, last = rank == 0, rank == nt - 1
    targets = [flipped(t, o, level) for o in range(nt)]
    ranks = [rank_at(target, s, level) for target in targets]
    order = range(nt - 1, 0, -1)
    below, above = s > 0, s < ns - 1
    lower, upper = jnp.maximum(s - 1, 0), jnp.minimum(s + 1, ns - 1)
    low_edge = jnp.logical_and(first, below)
    high_edge = jnp.logical_and(last, above)

    barrier = pltpu.get_barrier_semaphore()
    for o in order:
        pl.semaphore_signal(barrier, inc=1, device_id=(targets[o], s), device_id_type=MESH)

    @pl.when(low_edge)
    def _():
        for o in range(nt):
            pl.semaphore_signal(barrier, inc=1, device_id=(o, lower), device_id_type=MESH)

    @pl.when(high_edge)
    def _():
        for o in range(nt):
            pl.semaphore_signal(barrier, inc=1, device_id=(o, upper), device_id_type=MESH)

    start = rank * own
    loads = [
        pltpu.make_async_copy(source, target, local_sem.at[place])
        for place, (source, target) in enumerate(
            (
                (state_h, state_v),
                (forcing_h, forcing_v),
                (initial_h, initial_v),
                (blocks_h.at[:, pl.ds(start, own)], wb),
                (matrix_h, matrix_v),
                (factor_h, factor_v),
                (precond_h.at[pl.ds(start, own)], wp),
            )
        )
    ]
    for load in loads:
        load.start()

    loads[0].wait()
    state = state_v[...]
    by_block = jnp.swapaxes(state, 0, 1)
    squares = 0.5 * by_block * by_block
    blank = jnp.zeros((steps, squares.shape[2]), jnp.float32)
    for target in range(nt):
        parts = []
        for j in range(own * target - 2, own * (target + 1) + 2):
            parts.append(squares[j] if 0 <= j < width else blank)
        tail = state[steps - 1, own * target : own * (target + 1)]
        tail_hi = tail.astype(jnp.bfloat16).astype(jnp.float32)
        parts += [tail_hi, tail - tail_hi]
        if steps > 2 * own:
            parts.append(blank[: steps - 2 * own])
        chunk[target] = jnp.concatenate(parts, 0).astype(jnp.bfloat16)
    edge[0] = jnp.concatenate([squares[width - 2], squares[width - 1]], 0).astype(jnp.bfloat16)
    edge[1] = jnp.concatenate([squares[0], squares[1]], 0).astype(jnp.bfloat16)

    signals = nt - 1 + jnp.where(below, 1, 0) + jnp.where(above, 1, 0)
    pl.semaphore_wait(barrier, signals)

    edge_up = pltpu.make_async_remote_copy(
        src_ref=edge.at[0],
        dst_ref=redge.at[t],
        send_sem=edge_send.at[0],
        recv_sem=edge_recv.at[t],
        device_id=(position_at(0, upper, level), upper),
        device_id_type=MESH,
    )
    edge_down = pltpu.make_async_remote_copy(
        src_ref=edge.at[1],
        dst_ref=redge.at[t],
        send_sem=edge_send.at[1],
        recv_sem=edge_recv.at[t],
        device_id=(position_at(nt - 1, lower, level), lower),
        device_id_type=MESH,
    )

    @pl.when(above)
    def _():
        edge_up.start()

    @pl.when(below)
    def _():
        edge_down.start()

    q_copies = []
    for o in order:
        target = targets[o]
        q_copies.append(
            pltpu.make_async_remote_copy(
                src_ref=chunk.at[ranks[o]],
                dst_ref=rq.at[t],
                send_sem=q_send.at[o],
                recv_sem=q_recv.at[o],
                device_id=(target, s),
                device_id_type=MESH,
            )
        )
    for copy in q_copies:
        copy.start()

    loads[1].wait()
    loads[2].wait()
    forcing = forcing_v[...]
    initial = jnp.where(t == 0, initial_v[...], 0.0)
    previous = jnp.concatenate([initial[None], state[:-1]], 0)
    diff[...] = jnp.swapaxes(forcing - state + previous, 0, 1)
    d_copies = []
    for o in order:
        target = targets[o]
        d_copies.append(
            pltpu.make_async_remote_copy(
                src_ref=diff.at[pl.ds(ranks[o] * own, own)],
                dst_ref=rd.at[t],
                send_sem=d_send.at[o],
                recv_sem=d_recv.at[o],
                device_id=(target, s),
                device_id_type=MESH,
            )
        )
    for copy in d_copies:
        copy.start()
    rq[t] = chunk[rank]
    rd[t] = diff[pl.ds(start, own)]

    for copy in q_copies:
        copy.wait_recv()
    got = [rq[source].astype(jnp.float32) for source in range(nt)]
    for e in range(own + 4):
        xsq[e] = jnp.concatenate(
            [part[e * steps : (e + 1) * steps] for part in got], 0
        ).astype(jnp.bfloat16)
    lead = (own + 4) * steps
    tails = [
        part[lead : lead + own] + part[lead + own : lead + 2 * own] for part in got[:-1]
    ]

    def take_edge(place):
        for source in range(nt):
            pltpu.make_async_remote_copy(
                src_ref=edge.at[0],
                dst_ref=redge.at[source],
                send_sem=edge_send.at[0],
                recv_sem=edge_recv.at[source],
                device_id=(0, 0),
                device_id_type=MESH,
            ).wait_recv()
        edges = [redge[source].astype(jnp.float32) for source in range(nt)]
        for e in range(2):
            xsq[place + e] = jnp.concatenate(
                [part[e * steps : (e + 1) * steps] for part in edges], 0
            ).astype(jnp.bfloat16)

    @pl.when(low_edge)
    def _():
        take_edge(0)

    @pl.when(high_edge)
    def _():
        take_edge(own + 2)

    loads[3].wait()

    def coupled(field, e):
        slots = wb.shape[0]
        rows = [field[e + 2 + couple_s[slot, start + e]] for slot in range(slots)]
        weights = [wb[slot, e] for slot in range(slots)]
        return lax.dot_general(
            jnp.concatenate(rows, 1),
            jnp.concatenate(weights, 1),
            NT_DIMS,
            preferred_element_type=jnp.float32,
        )

    def conditioned(rounded):
        size = wp.shape[1]
        return jnp.concatenate(
            [
                lax.dot_general(
                    rounded[:, e * size : (e + 1) * size],
                    wp[e],
                    NT_DIMS,
                    preferred_element_type=jnp.float32,
                )
                for e in range(own)
            ],
            1,
        )

    flux = [coupled(xsq, e) for e in range(own)]
    for copy in d_copies:
        copy.wait_recv()
    leading = lax.broadcasted_iota(jnp.int32, blank.shape, 0) == 0
    residual = []
    for e in range(own):
        parts = [rd[0, e]]
        for source in range(1, nt):
            carried = jnp.broadcast_to(tails[source - 1][e : e + 1], blank.shape)
            parts.append(rd[source, e] + jnp.where(leading, carried, 0.0))
        residual.append(jnp.concatenate(parts, 0) - time_step * flux[e])
    loads[4].wait()
    spectrum = transformed(matrix_v[0], jnp.concatenate(residual, 1))

    loads[5].wait()
    loads[6].wait()
    first_step = conditioned(spectrum.astype(jnp.bfloat16))
    swapped = jnp.concatenate([first_step[half:], first_step[:half]], 0)
    factors = factor_v[...]
    sol = factors[:, 0:1] * first_step + factors[:, 1:2] * swapped
    size = wp.shape[1]
    for e in range(own):
        xsol[2 + e] = sol[:, e * size : (e + 1) * size].astype(jnp.bfloat16)

    has_down = jnp.logical_or(rank > 0, below)
    has_up = jnp.logical_or(rank < nt - 1, above)
    down_s = jnp.where(first, lower, s)
    down_t = position_at(jnp.where(first, nt - 1, rank - 1), down_s, level)
    up_s = jnp.where(last, upper, s)
    up_t = position_at(jnp.where(last, 0, rank + 1), up_s, level)
    halo_down = pltpu.make_async_remote_copy(
        src_ref=xsol.at[pl.ds(2, 2)],
        dst_ref=xsol.at[pl.ds(own + 2, 2)],
        send_sem=halo_send.at[0],
        recv_sem=halo_recv.at[0],
        device_id=(down_t, down_s),
        device_id_type=MESH,
    )
    halo_up = pltpu.make_async_remote_copy(
        src_ref=xsol.at[pl.ds(own, 2)],
        dst_ref=xsol.at[pl.ds(0, 2)],
        send_sem=halo_send.at[1],
        recv_sem=halo_recv.at[1],
        device_id=(up_t, up_s),
        device_id_type=MESH,
    )

    @pl.when(has_down)
    def _():
        halo_down.start()

    @pl.when(has_up)
    def _():
        halo_up.start()

    @pl.when(jnp.logical_not(has_down))
    def _():
        xsol[0:2] = jnp.zeros((2,) + xsol.shape[1:], jnp.bfloat16)

    @pl.when(jnp.logical_not(has_up))
    def _():
        xsol[own + 2 : own + 4] = jnp.zeros((2,) + xsol.shape[1:], jnp.bfloat16)

    left = spectrum - (factors[:, 2:3] * first_step + factors[:, 3:4] * swapped)

    @pl.when(has_down)
    def _():
        halo_up.wait_recv()

    @pl.when(has_up)
    def _():
        halo_down.wait_recv()

    applied = jnp.concatenate([coupled(xsol, e) for e in range(own)], 1)
    left = left - time_step * applied
    steps_sum = first_step + conditioned(left.astype(jnp.bfloat16))
    change = transformed(matrix_v[1], steps_sum)
    for e in range(own):
        back[e] = change[:, e * size : (e + 1) * size]
    b_copies = []
    for o in order:
        target = targets[o]
        b_copies.append(
            pltpu.make_async_remote_copy(
                src_ref=back.at[:, pl.ds(pl.multiple_of(target * steps, steps), steps)],
                dst_ref=rback.at[pl.ds(start, own)],
                send_sem=b_send.at[o],
                recv_sem=b_recv.at[o],
                device_id=(target, s),
                device_id_type=MESH,
            )
        )
    for copy in b_copies:
        copy.start()
    rback[pl.ds(start, own)] = back[:, pl.ds(pl.multiple_of(t * steps, steps), steps)]
    for copy in b_copies:
        copy.wait_recv()
    out_ref[...] = jnp.swapaxes(rback[...], 0, 1)

    for copy in q_copies + d_copies + b_copies:
        copy.wait_send()

    @pl.when(above)
    def _():
        edge_up.wait_send()

    @pl.when(below)
    def _():
        edge_down.wait_send()

    @pl.when(has_down)
    def _():
        halo_down.wait_send()

    @pl.when(has_up)
    def _():
        halo_up.wait_send()


def on_device_blocks(state, forcing, initial, blocks, precond, couple):
    nt, ns = lax.axis_size("tm"), lax.axis_size("space")
    steps, width, size = state.shape
    own = width // nt
    total = nt * steps
    slots = blocks.shape[0]
    matrix, factor = (jnp.asarray(table) for table in tables(total))
    far = pl.BlockSpec(memory_space=pltpu.HBM)
    rows = (own + 5) * steps
    f32, b16 = jnp.float32, jnp.bfloat16
    dma = pltpu.SemaphoreType.DMA
    change = pl.pallas_call(
        functools.partial(kernel, (nt, ns, steps, width, own)),
        out_shape=jax.ShapeDtypeStruct(state.shape, f32),
        in_specs=[far] * 5 + [pl.BlockSpec(memory_space=pltpu.SMEM)] + [far] * 2,
        out_specs=pl.BlockSpec(memory_space=pltpu.VMEM),
        scratch_shapes=[
            pltpu.VMEM(state.shape, f32),
            pltpu.VMEM(state.shape, f32),
            pltpu.VMEM(initial.shape, f32),
            pltpu.VMEM((slots, own, size, size), b16),
            pltpu.VMEM((own, size, size), b16),
            pltpu.VMEM(matrix.shape, f32),
            pltpu.VMEM(factor.shape, f32),
            pltpu.VMEM((nt, rows, size), b16),
            pltpu.VMEM((2, 2 * steps, size), b16),
            pltpu.VMEM((width, steps, size), f32),
            pltpu.VMEM((nt, rows, size), b16),
            pltpu.VMEM((nt, own, steps, size), f32),
            pltpu.VMEM((nt, 2 * steps, size), b16),
            pltpu.VMEM((own + 4, total, size), b16),
            pltpu.VMEM((own + 4, total, size), b16),
            pltpu.VMEM((own, total, size), f32),
            pltpu.VMEM((width, steps, size), f32),
            dma((7,)),
            dma((nt,)),
            dma((nt,)),
            dma((nt,)),
            dma((nt,)),
            dma((2,)),
            dma((nt,)),
            dma((2,)),
            dma((2,)),
            dma((nt,)),
            dma((nt,)),
        ],
        compiler_params=pltpu.CompilerParams(
            collective_id=0, has_side_effects=True, vmem_limit_bytes=60 * 1024 * 1024
        ),
    )(state, forcing, initial, blocks, precond, couple.T, matrix, factor)
    return state + change


def on_device(state, forcing, initial, blocks, precond, couple):
    nt = lax.axis_size("tm")
    steps, width, _ = state.shape
    own = width // nt
    even_cut = width % nt == 0 and own >= 2 and 2 * own <= steps and steps % 8 == 0
    power = nt > 1 and nt & nt - 1 == 0 and nt * steps % 16 == 0
    if power and even_cut and (own + 5) * steps % 16 == 0:
        return on_device_blocks(state, forcing, initial, blocks, precond, couple)
    return on_device_steps(state, forcing, initial, blocks, precond, couple)


def solution(mesh):
    placed = (
        P("tm", "space", None),
        P("tm", "space", None),
        P("space", None),
        P(None, "space", None, None),
        P("space", None, None),
        P("space", None),
    )
    return jax.shard_map(
        on_device, mesh=mesh, in_specs=placed, out_specs=P("tm", "space", None), check_vma=False
    )
```

```python
import functools
import math

import jax
import jax.numpy as jnp
import numpy as np
from jax import lax
from jax.experimental import pallas as pl
from jax.experimental.pallas import tpu as pltpu
from jax.sharding import PartitionSpec as P

SWEEPS = 2


alpha_rate = 0.5
time_step = 0.5
relaxation = 0.7


def from_behind(block, axis, distance):
    devices = range(lax.axis_size(axis))
    route = [(i - distance, i) for i in devices if i - distance in devices]
    return lax.ppermute(block, axis, route)


def extended(block, sides, width):
    for axis, dim in sides:
        count = lax.axis_size(axis)
        forward = [(i, i + 1) for i in range(count - 1)]
        backward = [(target, source) for source, target in forward]
        low = lax.ppermute(
            lax.slice_in_dim(block, block.shape[dim] - width, None, axis=dim), axis, forward
        )
        high = lax.ppermute(lax.slice_in_dim(block, 0, width, axis=dim), axis, backward)
        block = jnp.concatenate([low, block, high], axis=dim)
    return block


def from_partner(block, axis, stride):
    count = lax.axis_size(axis)
    route = []
    for low in range(count):
        high = low | 1 << stride
        if high != low and high < count:
            route += [(low, high), (high, low)]
    return lax.ppermute(block, axis, route)


def apply_padded(padded, blocks, couple):
    width = padded.shape[1] - 4
    total = None
    for column in range(5):
        chosen = padded[:, 2 : 2 + width]
        for offset in range(-2, 3):
            picked = (couple[:, column] == offset)[None, :, None]
            chosen = jnp.where(picked, padded[:, 2 + offset : 2 + offset + width], chosen)
        term = jnp.einsum(
            "fbj,bij->fbi", chosen, blocks[column], preferred_element_type=jnp.float32
        )
        total = term if total is None else total + term
    return total


def on_device_steps(state, forcing, initial, blocks, precond, couple):
    local_steps = state.shape[0]
    devices_tm = lax.axis_size("tm")
    position = lax.axis_index("tm")
    total_steps = local_steps * devices_tm
    level_count = devices_tm.bit_length() - 1
    highest = lax.Precision.HIGHEST
    last_step = from_behind(state[-1:], "tm", 1)
    first_prev = jnp.where(position == 0, initial[None], last_step)
    previous = jnp.concatenate([first_prev, state[:-1]], 0)
    squares = (0.5 * state * state).astype(jnp.bfloat16)
    padded = extended(squares, (("space", 1),), 2)
    flux = apply_padded(padded, blocks, couple)
    residual = forcing - state + previous - time_step * flux
    steps_global = position * local_steps + jnp.arange(local_steps, dtype=jnp.int32)
    log_rate = math.log(alpha_rate) / total_steps
    scaled = residual * jnp.exp(steps_global.astype(jnp.float32) * log_rate)[:, None, None]
    cur_re = scaled
    cur_im = jnp.zeros_like(scaled)
    for level in range(level_count):
        bit_number = level_count - 1 - level
        half = 1 << bit_number
        other = from_partner(jnp.stack([cur_re, cur_im]), "tm", bit_number)
        upper = position >> bit_number & 1 == 1
        angle = -2.0 * math.pi * (position % half).astype(jnp.float32) / (2 * half)
        tw_re = jnp.cos(angle)
        tw_im = jnp.sin(angle)
        diff_re = other[0] - cur_re
        diff_im = other[1] - cur_im
        new_re = jnp.where(upper, diff_re * tw_re - diff_im * tw_im, cur_re + other[0])
        new_im = jnp.where(upper, diff_re * tw_im + diff_im * tw_re, cur_im + other[1])
        cur_re, cur_im = (new_re, new_im)
    freq_base = jnp.zeros((), jnp.int32)
    for level in range(level_count):
        freq_base = freq_base + (position >> level & 1) * (1 << level_count - 1 - level)
    part_re, part_im = (cur_re, cur_im)
    local_index = jnp.arange(local_steps, dtype=jnp.int32)
    freq = freq_base + devices_tm * local_index
    product = freq[:, None] * local_index[None, :] % total_steps
    angle_table = 2.0 * math.pi * product.astype(jnp.float32) / total_steps
    table_re = jnp.cos(angle_table)
    table_im = -jnp.sin(angle_table)
    spec_re = jnp.einsum("qm,mbc->qbc", table_re, part_re, precision=highest) - jnp.einsum(
        "qm,mbc->qbc", table_im, part_im, precision=highest
    )
    spec_im = jnp.einsum("qm,mbc->qbc", table_re, part_im, precision=highest) + jnp.einsum(
        "qm,mbc->qbc", table_im, part_re, precision=highest
    )
    theta = 2.0 * math.pi * freq.astype(jnp.float32) / total_steps
    rate = math.exp(log_rate)
    lam_re = (1.0 - rate * jnp.cos(theta))[:, None, None]
    lam_im = (rate * jnp.sin(theta))[:, None, None]
    denom = (1.0 + lam_re) ** 2 + lam_im**2
    coef_re = (1.0 + lam_re) / denom
    coef_im = -lam_im / denom
    sol_re = None
    sol_im = None
    for sweep in range(SWEEPS):
        if sweep == 0:
            res_re, res_im = (spec_re, spec_im)
        else:
            stacked = jnp.concatenate([sol_re, sol_im], 0).astype(jnp.bfloat16)
            padded_sol = extended(stacked, (("space", 1),), 2)
            applied = apply_padded(padded_sol, blocks, couple)
            res_re = (
                spec_re - (lam_re * sol_re - lam_im * sol_im) - time_step * applied[:local_steps]
            )
            res_im = (
                spec_im - (lam_re * sol_im + lam_im * sol_re) - time_step * applied[local_steps:]
            )
        rounded = jnp.concatenate([res_re, res_im], 0).astype(jnp.bfloat16)
        gres = jnp.einsum("fbj,bij->fbi", rounded, precond, preferred_element_type=jnp.float32)
        g_re = gres[:local_steps]
        g_im = gres[local_steps:]
        step_re = relaxation * (coef_re * g_re - coef_im * g_im)
        step_im = relaxation * (coef_re * g_im + coef_im * g_re)
        if sweep == 0:
            sol_re, sol_im = (step_re, step_im)
        else:
            sol_re = sol_re + step_re
            sol_im = sol_im + step_im
    back_re = (
        jnp.einsum("qm,qbc->mbc", table_re, sol_re, precision=highest)
        + jnp.einsum("qm,qbc->mbc", table_im, sol_im, precision=highest)
    ) / local_steps
    back_im = (
        jnp.einsum("qm,qbc->mbc", table_re, sol_im, precision=highest)
        - jnp.einsum("qm,qbc->mbc", table_im, sol_re, precision=highest)
    ) / local_steps
    cur_re, cur_im = (back_re, back_im)
    for bit_number in range(level_count):
        half = 1 << bit_number
        other = from_partner(jnp.stack([cur_re, cur_im]), "tm", bit_number)
        upper = position >> bit_number & 1 == 1
        angle = -2.0 * math.pi * (position % half).astype(jnp.float32) / (2 * half)
        conj_re = jnp.cos(angle)
        conj_im = -jnp.sin(angle)
        other_tw_re = other[0] * conj_re - other[1] * conj_im
        other_tw_im = other[0] * conj_im + other[1] * conj_re
        mine_tw_re = cur_re * conj_re - cur_im * conj_im
        mine_tw_im = cur_re * conj_im + cur_im * conj_re
        new_re = jnp.where(upper, 0.5 * (other[0] - mine_tw_re), 0.5 * (cur_re + other_tw_re))
        new_im = jnp.where(upper, 0.5 * (other[1] - mine_tw_im), 0.5 * (cur_im + other_tw_im))
        cur_re, cur_im = (new_re, new_im)
    change = cur_re * jnp.exp(-steps_global.astype(jnp.float32) * log_rate)[:, None, None]
    return state + change


MESH = pl.DeviceIdType.MESH
NT_DIMS = (((1,), (1,)), ((), ()))
HIGHEST = lax.Precision.HIGHEST


def tables(steps):
    half = steps // 2
    rate = math.exp(math.log(alpha_rate) / steps)
    step = np.arange(steps)
    freq = np.arange(half)
    angle = 2.0 * np.pi * ((freq[:, None] * step[None, :]) % steps) / steps
    cosine, sine = np.cos(angle), np.sin(angle)
    nyquist = 1.0 - 2.0 * (step % 2)
    forward = np.concatenate([cosine, nyquist[None], -sine[1:]], 0) * rate**step
    inverse = np.concatenate([2.0 * cosine, nyquist[None], -2.0 * sine[1:]], 0)
    inverse[0] = 1.0
    inverse = inverse.T / steps * (rate ** (-step))[:, None]
    theta = 2.0 * np.pi * np.arange(half + 1) / steps
    lam = 1.0 - rate * np.exp(-1j * theta)
    lam[half] = lam[half].real
    coef = relaxation / (1.0 + lam)

    def columns(factor):
        real = np.concatenate([factor.real[:half], factor.real[half:], factor.real[1:half]])
        imag = np.concatenate([[0.0], factor.imag[1:half]])
        return real, np.concatenate([-imag, imag])

    coef_own, coef_swap = columns(coef)
    lam_own, lam_swap = columns(lam * coef)
    swap = np.roll(np.eye(steps), half, 1)
    inverse = inverse @ (np.diag(coef_own) + np.diag(coef_swap) @ swap)
    lanes = -(-steps // 128) * 128
    factors = np.zeros((steps, lanes), np.float32)
    for place, column in enumerate((coef_own, coef_swap, lam_own, lam_swap)):
        factors[:, place] = column
    matrices = np.stack([np.tile(matrix, 2) for matrix in (forward, inverse)])
    return matrices.astype(np.float32), factors


def halves(field, axis):
    high = field.astype(jnp.bfloat16)
    low = (field - high.astype(jnp.float32)).astype(jnp.bfloat16)
    return jnp.concatenate([high, low], axis)


def transformed(matrix, field):
    both = halves(field, 0)
    return jnp.dot(
        halves(matrix, 1),
        jnp.concatenate([both, both], 0),
        preferred_element_type=jnp.float32,
    )


def bits_of(number, count):
    return [lax.rem(lax.div(number, 1 << i), 2) for i in range(count)]


def number_of(bits):
    return sum(bit * (1 << i) for i, bit in enumerate(bits))


def flipped(bits, mask):
    return [1 - bit if mask >> i & 1 else bit for i, bit in enumerate(bits)]


def differ(a, b):
    return a + b - 2 * a * b


def rank_at(bits, odd):
    bits = list(bits)
    for i in reversed(range(len(bits) - 1)):
        bits[i] = differ(bits[i], bits[i + 1])
    return number_of([differ(bit, odd) for bit in bits])


def position_at(rank, odd, count):
    bits = [differ(bit, odd) for bit in bits_of(rank, count)]
    for i in range(count - 1):
        bits[i] = differ(bits[i], bits[i + 1])
    return number_of(bits)


def kernel(
    sizes,
    state_h,
    forcing_h,
    initial_h,
    blocks_h,
    precond_h,
    couple_h,
    matrix_h,
    factor_h,
    out_ref,
    state_v,
    forcing_v,
    initial_v,
    wb,
    wp,
    matrix_v,
    factor_v,
    couple_s,
    chunk,
    edge,
    diff,
    rq,
    rd,
    redge,
    xsq,
    xsol,
    back,
    rback,
    local_sem,
    q_send,
    q_recv,
    d_send,
    d_recv,
    edge_send,
    edge_recv,
    halo_send,
    halo_recv,
    b_send,
    b_recv,
):
    nt, ns, steps, width, own = sizes
    total = nt * steps
    half = total // 2
    t = lax.axis_index("tm")
    s = lax.axis_index("space")
    level = nt.bit_length() - 1
    odd = lax.rem(s, 2)
    place_bits = bits_of(t, level)
    rank = rank_at(place_bits, odd)
    first, last = rank == 0, rank == nt - 1
    targets = [number_of(flipped(place_bits, o)) for o in range(nt)]
    ranks = [rank_at(flipped(place_bits, o), odd) for o in range(nt)]
    order = range(nt - 1, 0, -1)
    top = nt // 2
    first_place = odd * top, (1 - odd) * top
    last_place = first_place[1], first_place[0]
    below, above = s > 0, s < ns - 1
    lower, upper = jnp.maximum(s - 1, 0), jnp.minimum(s + 1, ns - 1)
    low_edge = jnp.logical_and(first, below)
    high_edge = jnp.logical_and(last, above)

    barrier = pltpu.get_barrier_semaphore()
    for o in order:
        pl.semaphore_signal(barrier, inc=1, device_id=(targets[o], s), device_id_type=MESH)

    @pl.when(low_edge)
    def _():
        for o in range(nt):
            pl.semaphore_signal(barrier, inc=1, device_id=(o, lower), device_id_type=MESH)

    @pl.when(high_edge)
    def _():
        for o in range(nt):
            pl.semaphore_signal(barrier, inc=1, device_id=(o, upper), device_id_type=MESH)

    start = rank * own
    loads = [
        pltpu.make_async_copy(source, target, local_sem.at[place])
        for place, (source, target) in enumerate(
            (
                (state_h, state_v),
                (forcing_h, forcing_v),
                (initial_h, initial_v),
                (blocks_h.at[:, pl.ds(start, own)], wb),
                (matrix_h, matrix_v),
                (factor_h, factor_v),
                (precond_h.at[pl.ds(start, own)], wp),
                (couple_h, couple_s),
            )
        )
    ]
    for load in loads:
        load.start()

    loads[0].wait()
    state = state_v[...]
    by_block = jnp.swapaxes(state, 0, 1)
    squares = 0.5 * by_block * by_block
    blank = jnp.zeros((steps, squares.shape[2]), jnp.float32)
    for target in range(nt):
        parts = []
        for j in range(own * target - 2, own * (target + 1) + 2):
            parts.append(squares[j] if 0 <= j < width else blank)
        tail = state[steps - 1, own * target : own * (target + 1)]
        tail_hi = tail.astype(jnp.bfloat16).astype(jnp.float32)
        parts += [tail_hi, tail - tail_hi]
        if steps > 2 * own:
            parts.append(blank[: steps - 2 * own])
        chunk[target] = jnp.concatenate(parts, 0).astype(jnp.bfloat16)
    edge[0] = jnp.concatenate([squares[width - 2], squares[width - 1]], 0).astype(jnp.bfloat16)
    edge[1] = jnp.concatenate([squares[0], squares[1]], 0).astype(jnp.bfloat16)

    signals = nt - 1 + jnp.where(below, 1, 0) + jnp.where(above, 1, 0)
    pl.semaphore_wait(barrier, signals)

    edge_up = pltpu.make_async_remote_copy(
        src_ref=edge.at[0],
        dst_ref=redge.at[t],
        send_sem=edge_send.at[0],
        recv_sem=edge_recv.at[t],
        device_id=(first_place[1], upper),
        device_id_type=MESH,
    )
    edge_down = pltpu.make_async_remote_copy(
        src_ref=edge.at[1],
        dst_ref=redge.at[t],
        send_sem=edge_send.at[1],
        recv_sem=edge_recv.at[t],
        device_id=(last_place[1], lower),
        device_id_type=MESH,
    )

    @pl.when(above)
    def _():
        edge_up.start()

    @pl.when(below)
    def _():
        edge_down.start()

    q_copies = []
    for o in order:
        target = targets[o]
        q_copies.append(
            pltpu.make_async_remote_copy(
                src_ref=chunk.at[ranks[o]],
                dst_ref=rq.at[t],
                send_sem=q_send.at[o],
                recv_sem=q_recv.at[o],
                device_id=(target, s),
                device_id_type=MESH,
            )
        )
    for copy in q_copies:
        copy.start()

    loads[1].wait()
    loads[2].wait()
    forcing = forcing_v[...]
    initial = jnp.where(t == 0, initial_v[...], 0.0)
    previous = jnp.concatenate([initial[None], state[:-1]], 0)
    diff[...] = jnp.swapaxes(forcing - state + previous, 0, 1)
    d_copies = []
    for o in order:
        target = targets[o]
        d_copies.append(
            pltpu.make_async_remote_copy(
                src_ref=diff.at[pl.ds(ranks[o] * own, own)],
                dst_ref=rd.at[t],
                send_sem=d_send.at[o],
                recv_sem=d_recv.at[o],
                device_id=(target, s),
                device_id_type=MESH,
            )
        )
    for copy in d_copies:
        copy.start()
    rq[t] = chunk[rank]
    rd[t] = diff[pl.ds(start, own)]

    for copy in q_copies:
        copy.wait_recv()
    got = [rq[source].astype(jnp.float32) for source in range(nt)]
    for e in range(own + 4):
        xsq[e] = jnp.concatenate(
            [part[e * steps : (e + 1) * steps] for part in got], 0
        ).astype(jnp.bfloat16)
    lead = (own + 4) * steps
    tails = [
        part[lead : lead + own] + part[lead + own : lead + 2 * own] for part in got[:-1]
    ]

    def take_edge(place):
        for source in range(nt):
            pltpu.make_async_remote_copy(
                src_ref=edge.at[0],
                dst_ref=redge.at[source],
                send_sem=edge_send.at[0],
                recv_sem=edge_recv.at[source],
                device_id=(0, 0),
                device_id_type=MESH,
            ).wait_recv()
        edges = [redge[source].astype(jnp.float32) for source in range(nt)]
        for e in range(2):
            xsq[place + e] = jnp.concatenate(
                [part[e * steps : (e + 1) * steps] for part in edges], 0
            ).astype(jnp.bfloat16)

    @pl.when(low_edge)
    def _():
        take_edge(0)

    @pl.when(high_edge)
    def _():
        take_edge(own + 2)

    loads[3].wait()
    loads[7].wait()

    def coupled(field, e):
        slots = wb.shape[0]
        rows = [field[e + 2 + couple_s[slot, start + e]] for slot in range(slots)]
        weights = [wb[slot, e] for slot in range(slots)]
        return lax.dot_general(
            jnp.concatenate(rows, 1),
            jnp.concatenate(weights, 1),
            NT_DIMS,
            preferred_element_type=jnp.float32,
        )

    def conditioned(rounded):
        size = wp.shape[1]
        return jnp.concatenate(
            [
                lax.dot_general(
                    rounded[:, e * size : (e + 1) * size],
                    wp[e],
                    NT_DIMS,
                    preferred_element_type=jnp.float32,
                )
                for e in range(own)
            ],
            1,
        )

    flux = [coupled(xsq, e) for e in range(own)]
    for copy in d_copies:
        copy.wait_recv()
    leading = lax.broadcasted_iota(jnp.int32, blank.shape, 0) == 0
    residual = []
    for e in range(own):
        parts = [rd[0, e]]
        for source in range(1, nt):
            carried = jnp.broadcast_to(tails[source - 1][e : e + 1], blank.shape)
            parts.append(rd[source, e] + jnp.where(leading, carried, 0.0))
        residual.append(jnp.concatenate(parts, 0) - time_step * flux[e])
    loads[4].wait()
    spectrum = transformed(matrix_v[0], jnp.concatenate(residual, 1))

    loads[5].wait()
    loads[6].wait()
    first_step = conditioned(spectrum.astype(jnp.bfloat16))
    swapped = jnp.concatenate([first_step[half:], first_step[:half]], 0)
    factors = factor_v[...]
    sol = factors[:, 0:1] * first_step + factors[:, 1:2] * swapped
    size = wp.shape[1]
    for e in range(own):
        xsol[2 + e] = sol[:, e * size : (e + 1) * size].astype(jnp.bfloat16)

    has_down = jnp.logical_or(rank > 0, below)
    has_up = jnp.logical_or(rank < nt - 1, above)
    down_s = jnp.where(first, lower, s)
    before = position_at(jnp.maximum(rank - 1, 0), odd, level)
    down_t = jnp.where(first, last_place[1], before)
    up_s = jnp.where(last, upper, s)
    after = position_at(jnp.minimum(rank + 1, nt - 1), odd, level)
    up_t = jnp.where(last, first_place[1], after)
    halo_down = pltpu.make_async_remote_copy(
        src_ref=xsol.at[pl.ds(2, 2)],
        dst_ref=xsol.at[pl.ds(own + 2, 2)],
        send_sem=halo_send.at[0],
        recv_sem=halo_recv.at[0],
        device_id=(down_t, down_s),
        device_id_type=MESH,
    )
    halo_up = pltpu.make_async_remote_copy(
        src_ref=xsol.at[pl.ds(own, 2)],
        dst_ref=xsol.at[pl.ds(0, 2)],
        send_sem=halo_send.at[1],
        recv_sem=halo_recv.at[1],
        device_id=(up_t, up_s),
        device_id_type=MESH,
    )

    @pl.when(has_down)
    def _():
        halo_down.start()

    @pl.when(has_up)
    def _():
        halo_up.start()

    @pl.when(jnp.logical_not(has_down))
    def _():
        xsol[0:2] = jnp.zeros((2,) + xsol.shape[1:], jnp.bfloat16)

    @pl.when(jnp.logical_not(has_up))
    def _():
        xsol[own + 2 : own + 4] = jnp.zeros((2,) + xsol.shape[1:], jnp.bfloat16)

    left = spectrum - (factors[:, 2:3] * first_step + factors[:, 3:4] * swapped)

    @pl.when(has_down)
    def _():
        halo_up.wait_recv()

    @pl.when(has_up)
    def _():
        halo_down.wait_recv()

    applied = jnp.concatenate([coupled(xsol, e) for e in range(own)], 1)
    left = left - time_step * applied
    steps_sum = first_step + conditioned(left.astype(jnp.bfloat16))
    change = transformed(matrix_v[1], steps_sum)
    for e in range(own):
        back[e] = change[:, e * size : (e + 1) * size]
    b_copies = []
    for o in order:
        target = targets[o]
        b_copies.append(
            pltpu.make_async_remote_copy(
                src_ref=back.at[:, pl.ds(pl.multiple_of(target * steps, steps), steps)],
                dst_ref=rback.at[pl.ds(start, own)],
                send_sem=b_send.at[o],
                recv_sem=b_recv.at[o],
                device_id=(target, s),
                device_id_type=MESH,
            )
        )
    for copy in b_copies:
        copy.start()
    rback[pl.ds(start, own)] = back[:, pl.ds(pl.multiple_of(t * steps, steps), steps)]
    for copy in b_copies:
        copy.wait_recv()
    out_ref[...] = state_v[...] + jnp.swapaxes(rback[...], 0, 1)

    for copy in q_copies + d_copies + b_copies:
        copy.wait_send()

    @pl.when(above)
    def _():
        edge_up.wait_send()

    @pl.when(below)
    def _():
        edge_down.wait_send()

    @pl.when(has_down)
    def _():
        halo_down.wait_send()

    @pl.when(has_up)
    def _():
        halo_up.wait_send()


def on_device_blocks(state, forcing, initial, blocks, precond, couple):
    nt, ns = lax.axis_size("tm"), lax.axis_size("space")
    steps, width, size = state.shape
    own = width // nt
    total = nt * steps
    slots = blocks.shape[0]
    matrix, factor = (jnp.asarray(table) for table in tables(total))
    far = pl.BlockSpec(memory_space=pltpu.HBM)
    rows = (own + 5) * steps
    f32, b16 = jnp.float32, jnp.bfloat16
    dma = pltpu.SemaphoreType.DMA
    return pl.pallas_call(
        functools.partial(kernel, (nt, ns, steps, width, own)),
        out_shape=jax.ShapeDtypeStruct(state.shape, f32),
        in_specs=[far] * 8,
        out_specs=pl.BlockSpec(memory_space=pltpu.VMEM),
        scratch_shapes=[
            pltpu.VMEM(state.shape, f32),
            pltpu.VMEM(state.shape, f32),
            pltpu.VMEM(initial.shape, f32),
            pltpu.VMEM((slots, own, size, size), b16),
            pltpu.VMEM((own, size, size), b16),
            pltpu.VMEM(matrix.shape, f32),
            pltpu.VMEM(factor.shape, f32),
            pltpu.SMEM(couple.shape[::-1], jnp.int32),
            pltpu.VMEM((nt, rows, size), b16),
            pltpu.VMEM((2, 2 * steps, size), b16),
            pltpu.VMEM((width, steps, size), f32),
            pltpu.VMEM((nt, rows, size), b16),
            pltpu.VMEM((nt, own, steps, size), f32),
            pltpu.VMEM((nt, 2 * steps, size), b16),
            pltpu.VMEM((own + 4, total, size), b16),
            pltpu.VMEM((own + 4, total, size), b16),
            pltpu.VMEM((own, total, size), f32),
            pltpu.VMEM((width, steps, size), f32),
            dma((8,)),
            dma((nt,)),
            dma((nt,)),
            dma((nt,)),
            dma((nt,)),
            dma((2,)),
            dma((nt,)),
            dma((2,)),
            dma((2,)),
            dma((nt,)),
            dma((nt,)),
        ],
        compiler_params=pltpu.CompilerParams(
            collective_id=0, has_side_effects=True, vmem_limit_bytes=60 * 1024 * 1024
        ),
    )(state, forcing, initial, blocks, precond, couple.T, matrix, factor)


def on_device(state, forcing, initial, blocks, precond, couple):
    nt = lax.axis_size("tm")
    steps, width, _ = state.shape
    own = width // nt
    even_cut = width % nt == 0 and own >= 2 and 2 * own <= steps and steps % 8 == 0
    power = nt > 1 and nt & nt - 1 == 0 and nt * steps % 16 == 0
    if power and even_cut and (own + 5) * steps % 16 == 0:
        return on_device_blocks(state, forcing, initial, blocks, precond, couple)
    return on_device_steps(state, forcing, initial, blocks, precond, couple)


def solution(mesh):
    placed = (
        P("tm", "space", None),
        P("tm", "space", None),
        P("space", None),
        P(None, "space", None, None),
        P("space", None, None),
        P("space", None),
    )
    return jax.shard_map(
        on_device, mesh=mesh, in_specs=placed, out_specs=P("tm", "space", None), check_vma=False
    )
```

```python
import functools
import math

import jax
import jax.numpy as jnp
import numpy as np
from jax import lax
from jax.experimental import pallas as pl
from jax.experimental.pallas import tpu as pltpu
from jax.sharding import PartitionSpec as P

SWEEPS = 2


alpha_rate = 0.5
time_step = 0.5
relaxation = 0.7


def from_behind(block, axis, distance):
    devices = range(lax.axis_size(axis))
    route = [(i - distance, i) for i in devices if i - distance in devices]
    return lax.ppermute(block, axis, route)


def extended(block, sides, width):
    for axis, dim in sides:
        count = lax.axis_size(axis)
        forward = [(i, i + 1) for i in range(count - 1)]
        backward = [(target, source) for source, target in forward]
        low = lax.ppermute(
            lax.slice_in_dim(block, block.shape[dim] - width, None, axis=dim), axis, forward
        )
        high = lax.ppermute(lax.slice_in_dim(block, 0, width, axis=dim), axis, backward)
        block = jnp.concatenate([low, block, high], axis=dim)
    return block


def from_partner(block, axis, stride):
    count = lax.axis_size(axis)
    route = []
    for low in range(count):
        high = low | 1 << stride
        if high != low and high < count:
            route += [(low, high), (high, low)]
    return lax.ppermute(block, axis, route)


def apply_padded(padded, blocks, couple):
    width = padded.shape[1] - 4
    total = None
    for column in range(5):
        chosen = padded[:, 2 : 2 + width]
        for offset in range(-2, 3):
            picked = (couple[:, column] == offset)[None, :, None]
            chosen = jnp.where(picked, padded[:, 2 + offset : 2 + offset + width], chosen)
        term = jnp.einsum(
            "fbj,bij->fbi", chosen, blocks[column], preferred_element_type=jnp.float32
        )
        total = term if total is None else total + term
    return total


def on_device_steps(state, forcing, initial, blocks, precond, couple):
    local_steps = state.shape[0]
    devices_tm = lax.axis_size("tm")
    position = lax.axis_index("tm")
    total_steps = local_steps * devices_tm
    level_count = devices_tm.bit_length() - 1
    highest = lax.Precision.HIGHEST
    last_step = from_behind(state[-1:], "tm", 1)
    first_prev = jnp.where(position == 0, initial[None], last_step)
    previous = jnp.concatenate([first_prev, state[:-1]], 0)
    squares = (0.5 * state * state).astype(jnp.bfloat16)
    padded = extended(squares, (("space", 1),), 2)
    flux = apply_padded(padded, blocks, couple)
    residual = forcing - state + previous - time_step * flux
    steps_global = position * local_steps + jnp.arange(local_steps, dtype=jnp.int32)
    log_rate = math.log(alpha_rate) / total_steps
    scaled = residual * jnp.exp(steps_global.astype(jnp.float32) * log_rate)[:, None, None]
    cur_re = scaled
    cur_im = jnp.zeros_like(scaled)
    for level in range(level_count):
        bit_number = level_count - 1 - level
        half = 1 << bit_number
        other = from_partner(jnp.stack([cur_re, cur_im]), "tm", bit_number)
        upper = position >> bit_number & 1 == 1
        angle = -2.0 * math.pi * (position % half).astype(jnp.float32) / (2 * half)
        tw_re = jnp.cos(angle)
        tw_im = jnp.sin(angle)
        diff_re = other[0] - cur_re
        diff_im = other[1] - cur_im
        new_re = jnp.where(upper, diff_re * tw_re - diff_im * tw_im, cur_re + other[0])
        new_im = jnp.where(upper, diff_re * tw_im + diff_im * tw_re, cur_im + other[1])
        cur_re, cur_im = (new_re, new_im)
    freq_base = jnp.zeros((), jnp.int32)
    for level in range(level_count):
        freq_base = freq_base + (position >> level & 1) * (1 << level_count - 1 - level)
    part_re, part_im = (cur_re, cur_im)
    local_index = jnp.arange(local_steps, dtype=jnp.int32)
    freq = freq_base + devices_tm * local_index
    product = freq[:, None] * local_index[None, :] % total_steps
    angle_table = 2.0 * math.pi * product.astype(jnp.float32) / total_steps
    table_re = jnp.cos(angle_table)
    table_im = -jnp.sin(angle_table)
    spec_re = jnp.einsum("qm,mbc->qbc", table_re, part_re, precision=highest) - jnp.einsum(
        "qm,mbc->qbc", table_im, part_im, precision=highest
    )
    spec_im = jnp.einsum("qm,mbc->qbc", table_re, part_im, precision=highest) + jnp.einsum(
        "qm,mbc->qbc", table_im, part_re, precision=highest
    )
    theta = 2.0 * math.pi * freq.astype(jnp.float32) / total_steps
    rate = math.exp(log_rate)
    lam_re = (1.0 - rate * jnp.cos(theta))[:, None, None]
    lam_im = (rate * jnp.sin(theta))[:, None, None]
    denom = (1.0 + lam_re) ** 2 + lam_im**2
    coef_re = (1.0 + lam_re) / denom
    coef_im = -lam_im / denom
    sol_re = None
    sol_im = None
    for sweep in range(SWEEPS):
        if sweep == 0:
            res_re, res_im = (spec_re, spec_im)
        else:
            stacked = jnp.concatenate([sol_re, sol_im], 0).astype(jnp.bfloat16)
            padded_sol = extended(stacked, (("space", 1),), 2)
            applied = apply_padded(padded_sol, blocks, couple)
            res_re = (
                spec_re - (lam_re * sol_re - lam_im * sol_im) - time_step * applied[:local_steps]
            )
            res_im = (
                spec_im - (lam_re * sol_im + lam_im * sol_re) - time_step * applied[local_steps:]
            )
        rounded = jnp.concatenate([res_re, res_im], 0).astype(jnp.bfloat16)
        gres = jnp.einsum("fbj,bij->fbi", rounded, precond, preferred_element_type=jnp.float32)
        g_re = gres[:local_steps]
        g_im = gres[local_steps:]
        step_re = relaxation * (coef_re * g_re - coef_im * g_im)
        step_im = relaxation * (coef_re * g_im + coef_im * g_re)
        if sweep == 0:
            sol_re, sol_im = (step_re, step_im)
        else:
            sol_re = sol_re + step_re
            sol_im = sol_im + step_im
    back_re = (
        jnp.einsum("qm,qbc->mbc", table_re, sol_re, precision=highest)
        + jnp.einsum("qm,qbc->mbc", table_im, sol_im, precision=highest)
    ) / local_steps
    back_im = (
        jnp.einsum("qm,qbc->mbc", table_re, sol_im, precision=highest)
        - jnp.einsum("qm,qbc->mbc", table_im, sol_re, precision=highest)
    ) / local_steps
    cur_re, cur_im = (back_re, back_im)
    for bit_number in range(level_count):
        half = 1 << bit_number
        other = from_partner(jnp.stack([cur_re, cur_im]), "tm", bit_number)
        upper = position >> bit_number & 1 == 1
        angle = -2.0 * math.pi * (position % half).astype(jnp.float32) / (2 * half)
        conj_re = jnp.cos(angle)
        conj_im = -jnp.sin(angle)
        other_tw_re = other[0] * conj_re - other[1] * conj_im
        other_tw_im = other[0] * conj_im + other[1] * conj_re
        mine_tw_re = cur_re * conj_re - cur_im * conj_im
        mine_tw_im = cur_re * conj_im + cur_im * conj_re
        new_re = jnp.where(upper, 0.5 * (other[0] - mine_tw_re), 0.5 * (cur_re + other_tw_re))
        new_im = jnp.where(upper, 0.5 * (other[1] - mine_tw_im), 0.5 * (cur_im + other_tw_im))
        cur_re, cur_im = (new_re, new_im)
    change = cur_re * jnp.exp(-steps_global.astype(jnp.float32) * log_rate)[:, None, None]
    return state + change


MESH = pl.DeviceIdType.MESH
NT_DIMS = (((1,), (1,)), ((), ()))
HIGHEST = lax.Precision.HIGHEST


def tables(steps):
    half = steps // 2
    rate = math.exp(math.log(alpha_rate) / steps)
    step = np.arange(steps)
    freq = np.arange(half)
    angle = 2.0 * np.pi * ((freq[:, None] * step[None, :]) % steps) / steps
    cosine, sine = np.cos(angle), np.sin(angle)
    nyquist = 1.0 - 2.0 * (step % 2)
    forward = np.concatenate([cosine, nyquist[None], -sine[1:]], 0) * rate**step
    inverse = np.concatenate([2.0 * cosine, nyquist[None], -2.0 * sine[1:]], 0)
    inverse[0] = 1.0
    inverse = inverse.T / steps * (rate ** (-step))[:, None]
    theta = 2.0 * np.pi * np.arange(half + 1) / steps
    lam = 1.0 - rate * np.exp(-1j * theta)
    lam[half] = lam[half].real
    coef = relaxation / (1.0 + lam)

    def columns(factor):
        real = np.concatenate([factor.real[:half], factor.real[half:], factor.real[1:half]])
        imag = np.concatenate([[0.0], factor.imag[1:half]])
        return real, np.concatenate([-imag, imag])

    coef_own, coef_swap = columns(coef)
    lam_own, lam_swap = columns(lam * coef)
    swap = np.roll(np.eye(steps), half, 1)
    inverse = inverse @ (np.diag(coef_own) + np.diag(coef_swap) @ swap)
    lanes = -(-steps // 128) * 128
    factors = np.zeros((steps, lanes), np.float32)
    for place, column in enumerate((coef_own, coef_swap, lam_own, lam_swap)):
        factors[:, place] = column
    matrices = np.stack([np.tile(matrix, 2) for matrix in (forward, inverse)])
    return matrices.astype(np.float32), factors


def halves(field, axis):
    high = field.astype(jnp.bfloat16)
    low = (field - high.astype(jnp.float32)).astype(jnp.bfloat16)
    return jnp.concatenate([high, low], axis)


def transformed(matrix, field):
    both = halves(field, 0)
    return jnp.dot(
        halves(matrix, 1),
        jnp.concatenate([both, both], 0),
        preferred_element_type=jnp.float32,
    )


def bits_of(number, count):
    return [lax.rem(lax.div(number, 1 << i), 2) for i in range(count)]


def number_of(bits):
    return sum(bit * (1 << i) for i, bit in enumerate(bits))


def flipped(bits, mask):
    return [1 - bit if mask >> i & 1 else bit for i, bit in enumerate(bits)]


def differ(a, b):
    return a + b - 2 * a * b


def rank_at(bits, odd):
    bits = list(bits)
    for i in reversed(range(len(bits) - 1)):
        bits[i] = differ(bits[i], bits[i + 1])
    return number_of([differ(bit, odd) for bit in bits])


def position_at(rank, odd, count):
    bits = [differ(bit, odd) for bit in bits_of(rank, count)]
    for i in range(count - 1):
        bits[i] = differ(bits[i], bits[i + 1])
    return number_of(bits)


def kernel(
    sizes,
    state_h,
    forcing_h,
    initial_h,
    blocks_h,
    precond_h,
    couple_h,
    matrix_h,
    factor_h,
    out_ref,
    state_v,
    forcing_v,
    initial_v,
    wb,
    wp,
    matrix_v,
    factor_v,
    couple_s,
    chunk,
    edge,
    diff,
    rq,
    rd,
    redge,
    xsq,
    xsol,
    back,
    rback,
    local_sem,
    q_send,
    q_recv,
    d_send,
    d_recv,
    edge_send,
    edge_recv,
    halo_send,
    halo_recv,
    b_send,
    b_recv,
):
    nt, ns, steps, width, own = sizes
    total = nt * steps
    half = total // 2
    t = lax.axis_index("tm")
    s = lax.axis_index("space")
    level = nt.bit_length() - 1
    odd = lax.rem(s, 2)
    place_bits = bits_of(t, level)
    rank = rank_at(place_bits, odd)
    first, last = rank == 0, rank == nt - 1
    targets = [number_of(flipped(place_bits, o)) for o in range(nt)]
    ranks = [rank_at(flipped(place_bits, o), odd) for o in range(nt)]
    order = range(nt - 1, 0, -1)
    top = nt // 2
    first_place = odd * top, (1 - odd) * top
    last_place = first_place[1], first_place[0]
    below, above = s > 0, s < ns - 1
    lower, upper = jnp.maximum(s - 1, 0), jnp.minimum(s + 1, ns - 1)
    low_edge = jnp.logical_and(first, below)
    high_edge = jnp.logical_and(last, above)

    barrier = pltpu.get_barrier_semaphore()
    for o in order:
        pl.semaphore_signal(barrier, inc=1, device_id=(targets[o], s), device_id_type=MESH)

    @pl.when(low_edge)
    def _():
        for o in range(nt):
            pl.semaphore_signal(barrier, inc=1, device_id=(o, lower), device_id_type=MESH)

    @pl.when(high_edge)
    def _():
        for o in range(nt):
            pl.semaphore_signal(barrier, inc=1, device_id=(o, upper), device_id_type=MESH)

    start = rank * own
    loads = [
        pltpu.make_async_copy(source, target, local_sem.at[place])
        for place, (source, target) in enumerate(
            (
                (state_h, state_v),
                (forcing_h, forcing_v),
                (initial_h, initial_v),
                (blocks_h.at[:, pl.ds(start, own)], wb),
                (matrix_h, matrix_v),
                (factor_h, factor_v),
                (precond_h.at[pl.ds(start, own)], wp),
                (couple_h, couple_s),
            )
        )
    ]
    for load in loads:
        load.start()

    loads[0].wait()
    state = state_v[...]
    by_block = jnp.swapaxes(state, 0, 1)
    squares = 0.5 * by_block * by_block
    blank = jnp.zeros((steps, squares.shape[2]), jnp.float32)
    for target in range(nt):
        parts = []
        for j in range(own * target - 2, own * (target + 1) + 2):
            parts.append(squares[j] if 0 <= j < width else blank)
        tail = state[steps - 1, own * target : own * (target + 1)]
        tail_hi = tail.astype(jnp.bfloat16).astype(jnp.float32)
        parts += [tail_hi, tail - tail_hi]
        if steps > 2 * own:
            parts.append(blank[: steps - 2 * own])
        chunk[target] = jnp.concatenate(parts, 0).astype(jnp.bfloat16)
    edge[0] = jnp.concatenate([squares[width - 2], squares[width - 1]], 0).astype(jnp.bfloat16)
    edge[1] = jnp.concatenate([squares[0], squares[1]], 0).astype(jnp.bfloat16)

    signals = nt - 1 + jnp.where(below, 1, 0) + jnp.where(above, 1, 0)
    pl.semaphore_wait(barrier, signals)

    edge_up = pltpu.make_async_remote_copy(
        src_ref=edge.at[0],
        dst_ref=redge.at[t],
        send_sem=edge_send.at[0],
        recv_sem=edge_recv.at[t],
        device_id=(first_place[1], upper),
        device_id_type=MESH,
    )
    edge_down = pltpu.make_async_remote_copy(
        src_ref=edge.at[1],
        dst_ref=redge.at[t],
        send_sem=edge_send.at[1],
        recv_sem=edge_recv.at[t],
        device_id=(last_place[1], lower),
        device_id_type=MESH,
    )

    @pl.when(above)
    def _():
        edge_up.start()

    @pl.when(below)
    def _():
        edge_down.start()

    q_copies = []
    for o in order:
        target = targets[o]
        q_copies.append(
            pltpu.make_async_remote_copy(
                src_ref=chunk.at[ranks[o]],
                dst_ref=rq.at[t],
                send_sem=q_send.at[o],
                recv_sem=q_recv.at[o],
                device_id=(target, s),
                device_id_type=MESH,
            )
        )
    for copy in q_copies:
        copy.start()

    loads[1].wait()
    loads[2].wait()
    forcing = forcing_v[...]
    initial = jnp.where(t == 0, initial_v[...], 0.0)
    previous = jnp.concatenate([initial[None], state[:-1]], 0)
    diff[...] = jnp.swapaxes(forcing - state + previous, 0, 1)
    d_copies = []
    for o in order:
        target = targets[o]
        d_copies.append(
            pltpu.make_async_remote_copy(
                src_ref=diff.at[pl.ds(ranks[o] * own, own)],
                dst_ref=rd.at[t],
                send_sem=d_send.at[o],
                recv_sem=d_recv.at[o],
                device_id=(target, s),
                device_id_type=MESH,
            )
        )
    for copy in d_copies:
        copy.start()
    rq[t] = chunk[rank]
    rd[t] = diff[pl.ds(start, own)]

    for copy in q_copies:
        copy.wait_recv()
    got = [rq[source].astype(jnp.float32) for source in range(nt)]
    for e in range(own + 4):
        xsq[e] = jnp.concatenate(
            [part[e * steps : (e + 1) * steps] for part in got], 0
        ).astype(jnp.bfloat16)
    lead = (own + 4) * steps
    tails = [
        part[lead : lead + own] + part[lead + own : lead + 2 * own] for part in got[:-1]
    ]

    def take_edge(place):
        for source in range(nt):
            pltpu.make_async_remote_copy(
                src_ref=edge.at[0],
                dst_ref=redge.at[source],
                send_sem=edge_send.at[0],
                recv_sem=edge_recv.at[source],
                device_id=(0, 0),
                device_id_type=MESH,
            ).wait_recv()
        edges = [redge[source].astype(jnp.float32) for source in range(nt)]
        for e in range(2):
            xsq[place + e] = jnp.concatenate(
                [part[e * steps : (e + 1) * steps] for part in edges], 0
            ).astype(jnp.bfloat16)

    @pl.when(low_edge)
    def _():
        take_edge(0)

    @pl.when(high_edge)
    def _():
        take_edge(own + 2)

    loads[3].wait()
    loads[7].wait()

    def coupled(field, e):
        slots = wb.shape[0]
        rows = [field[e + 2 + couple_s[slot, start + e]] for slot in range(slots)]
        weights = [wb[slot, e] for slot in range(slots)]
        return lax.dot_general(
            jnp.concatenate(rows, 1),
            jnp.concatenate(weights, 1),
            NT_DIMS,
            preferred_element_type=jnp.float32,
        )

    def conditioned(rounded):
        size = wp.shape[1]
        return jnp.concatenate(
            [
                lax.dot_general(
                    rounded[:, e * size : (e + 1) * size],
                    wp[e],
                    NT_DIMS,
                    preferred_element_type=jnp.float32,
                )
                for e in range(own)
            ],
            1,
        )

    flux = [coupled(xsq, e) for e in range(own)]
    for copy in d_copies:
        copy.wait_recv()
    leading = lax.broadcasted_iota(jnp.int32, blank.shape, 0) == 0
    residual = []
    for e in range(own):
        parts = [rd[0, e]]
        for source in range(1, nt):
            carried = jnp.broadcast_to(tails[source - 1][e : e + 1], blank.shape)
            parts.append(rd[source, e] + jnp.where(leading, carried, 0.0))
        residual.append(jnp.concatenate(parts, 0) - time_step * flux[e])
    loads[4].wait()
    spectrum = transformed(matrix_v[0], jnp.concatenate(residual, 1))

    loads[5].wait()
    loads[6].wait()
    first_step = conditioned(spectrum.astype(jnp.bfloat16))
    swapped = jnp.concatenate([first_step[half:], first_step[:half]], 0)
    factors = factor_v[...]
    sol = factors[:, 0:1] * first_step + factors[:, 1:2] * swapped
    size = wp.shape[1]
    for e in range(own):
        xsol[2 + e] = sol[:, e * size : (e + 1) * size].astype(jnp.bfloat16)

    has_down = jnp.logical_or(rank > 0, below)
    has_up = jnp.logical_or(rank < nt - 1, above)
    down_s = jnp.where(first, lower, s)
    before = position_at(jnp.maximum(rank - 1, 0), odd, level)
    down_t = jnp.where(first, last_place[1], before)
    up_s = jnp.where(last, upper, s)
    after = position_at(jnp.minimum(rank + 1, nt - 1), odd, level)
    up_t = jnp.where(last, first_place[1], after)
    halo_down = pltpu.make_async_remote_copy(
        src_ref=xsol.at[pl.ds(2, 2)],
        dst_ref=xsol.at[pl.ds(own + 2, 2)],
        send_sem=halo_send.at[0],
        recv_sem=halo_recv.at[0],
        device_id=(down_t, down_s),
        device_id_type=MESH,
    )
    halo_up = pltpu.make_async_remote_copy(
        src_ref=xsol.at[pl.ds(own, 2)],
        dst_ref=xsol.at[pl.ds(0, 2)],
        send_sem=halo_send.at[1],
        recv_sem=halo_recv.at[1],
        device_id=(up_t, up_s),
        device_id_type=MESH,
    )

    @pl.when(has_down)
    def _():
        halo_down.start()

    @pl.when(has_up)
    def _():
        halo_up.start()

    @pl.when(jnp.logical_not(has_down))
    def _():
        xsol[0:2] = jnp.zeros((2,) + xsol.shape[1:], jnp.bfloat16)

    @pl.when(jnp.logical_not(has_up))
    def _():
        xsol[own + 2 : own + 4] = jnp.zeros((2,) + xsol.shape[1:], jnp.bfloat16)

    left = spectrum - (factors[:, 2:3] * first_step + factors[:, 3:4] * swapped)

    @pl.when(has_down)
    def _():
        halo_up.wait_recv()

    @pl.when(has_up)
    def _():
        halo_down.wait_recv()

    applied = jnp.concatenate([coupled(xsol, e) for e in range(own)], 1)
    left = left - time_step * applied
    steps_sum = first_step + conditioned(left.astype(jnp.bfloat16))
    change = transformed(matrix_v[1], steps_sum)
    for e in range(own):
        back[e] = change[:, e * size : (e + 1) * size]
    b_copies = []
    for o in order:
        target = targets[o]
        b_copies.append(
            pltpu.make_async_remote_copy(
                src_ref=back.at[:, pl.ds(pl.multiple_of(target * steps, steps), steps)],
                dst_ref=rback.at[pl.ds(start, own)],
                send_sem=b_send.at[o],
                recv_sem=b_recv.at[o],
                device_id=(target, s),
                device_id_type=MESH,
            )
        )
    for copy in b_copies:
        copy.start()
    rback[pl.ds(start, own)] = back[:, pl.ds(pl.multiple_of(t * steps, steps), steps)]
    for copy in b_copies:
        copy.wait_recv()
    out_ref[...] = state_v[...] + jnp.swapaxes(rback[...], 0, 1)

    for copy in q_copies + d_copies + b_copies:
        copy.wait_send()

    @pl.when(above)
    def _():
        edge_up.wait_send()

    @pl.when(below)
    def _():
        edge_down.wait_send()

    @pl.when(has_down)
    def _():
        halo_down.wait_send()

    @pl.when(has_up)
    def _():
        halo_up.wait_send()


def on_device_blocks(state, forcing, initial, blocks, precond, couple):
    nt, ns = lax.axis_size("tm"), lax.axis_size("space")
    steps, width, size = state.shape
    own = width // nt
    total = nt * steps
    slots = blocks.shape[0]
    matrix, factor = (jnp.asarray(table) for table in tables(total))
    far = pl.BlockSpec(memory_space=pltpu.HBM)
    rows = (own + 5) * steps
    f32, b16 = jnp.float32, jnp.bfloat16
    dma = pltpu.SemaphoreType.DMA
    return pl.pallas_call(
        functools.partial(kernel, (nt, ns, steps, width, own)),
        out_shape=pltpu.VMEM(state.shape, f32),
        in_specs=[far] * 8,
        out_specs=pl.BlockSpec(memory_space=pltpu.VMEM),
        scratch_shapes=[
            pltpu.VMEM(state.shape, f32),
            pltpu.VMEM(state.shape, f32),
            pltpu.VMEM(initial.shape, f32),
            pltpu.VMEM((slots, own, size, size), b16),
            pltpu.VMEM((own, size, size), b16),
            pltpu.VMEM(matrix.shape, f32),
            pltpu.VMEM(factor.shape, f32),
            pltpu.SMEM(couple.shape[::-1], jnp.int32),
            pltpu.VMEM((nt, rows, size), b16),
            pltpu.VMEM((2, 2 * steps, size), b16),
            pltpu.VMEM((width, steps, size), f32),
            pltpu.VMEM((nt, rows, size), b16),
            pltpu.VMEM((nt, own, steps, size), f32),
            pltpu.VMEM((nt, 2 * steps, size), b16),
            pltpu.VMEM((own + 4, total, size), b16),
            pltpu.VMEM((own + 4, total, size), b16),
            pltpu.VMEM((own, total, size), f32),
            pltpu.VMEM((width, steps, size), f32),
            dma((8,)),
            dma((nt,)),
            dma((nt,)),
            dma((nt,)),
            dma((nt,)),
            dma((2,)),
            dma((nt,)),
            dma((2,)),
            dma((2,)),
            dma((nt,)),
            dma((nt,)),
        ],
        compiler_params=pltpu.CompilerParams(
            collective_id=0, has_side_effects=True, vmem_limit_bytes=60 * 1024 * 1024
        ),
    )(state, forcing, initial, blocks, precond, couple.T, matrix, factor)


def on_device(state, forcing, initial, blocks, precond, couple):
    nt = lax.axis_size("tm")
    steps, width, _ = state.shape
    own = width // nt
    even_cut = width % nt == 0 and own >= 2 and 2 * own <= steps and steps % 8 == 0
    power = nt > 1 and nt & nt - 1 == 0 and nt * steps % 16 == 0
    if power and even_cut and (own + 5) * steps % 16 == 0:
        return on_device_blocks(state, forcing, initial, blocks, precond, couple)
    return on_device_steps(state, forcing, initial, blocks, precond, couple)


def solution(mesh):
    placed = (
        P("tm", "space", None),
        P("tm", "space", None),
        P("space", None),
        P(None, "space", None, None),
        P("space", None, None),
        P("space", None),
    )
    return jax.shard_map(
        on_device, mesh=mesh, in_specs=placed, out_specs=P("tm", "space", None), check_vma=False
    )
```

```python
import functools
import math

import jax
import jax.numpy as jnp
import numpy as np
from jax import lax
from jax.experimental import pallas as pl
from jax.experimental.pallas import tpu as pltpu
from jax.sharding import PartitionSpec as P

SWEEPS = 2


alpha_rate = 0.5
time_step = 0.5
relaxation = 0.7


def from_behind(block, axis, distance):
    devices = range(lax.axis_size(axis))
    route = [(i - distance, i) for i in devices if i - distance in devices]
    return lax.ppermute(block, axis, route)


def extended(block, sides, width):
    for axis, dim in sides:
        count = lax.axis_size(axis)
        forward = [(i, i + 1) for i in range(count - 1)]
        backward = [(target, source) for source, target in forward]
        low = lax.ppermute(
            lax.slice_in_dim(block, block.shape[dim] - width, None, axis=dim), axis, forward
        )
        high = lax.ppermute(lax.slice_in_dim(block, 0, width, axis=dim), axis, backward)
        block = jnp.concatenate([low, block, high], axis=dim)
    return block


def from_partner(block, axis, stride):
    count = lax.axis_size(axis)
    route = []
    for low in range(count):
        high = low | 1 << stride
        if high != low and high < count:
            route += [(low, high), (high, low)]
    return lax.ppermute(block, axis, route)


def apply_padded(padded, blocks, couple):
    width = padded.shape[1] - 4
    total = None
    for column in range(5):
        chosen = padded[:, 2 : 2 + width]
        for offset in range(-2, 3):
            picked = (couple[:, column] == offset)[None, :, None]
            chosen = jnp.where(picked, padded[:, 2 + offset : 2 + offset + width], chosen)
        term = jnp.einsum(
            "fbj,bij->fbi", chosen, blocks[column], preferred_element_type=jnp.float32
        )
        total = term if total is None else total + term
    return total


def on_device_steps(state, forcing, initial, blocks, precond, couple):
    local_steps = state.shape[0]
    devices_tm = lax.axis_size("tm")
    position = lax.axis_index("tm")
    total_steps = local_steps * devices_tm
    level_count = devices_tm.bit_length() - 1
    highest = lax.Precision.HIGHEST
    last_step = from_behind(state[-1:], "tm", 1)
    first_prev = jnp.where(position == 0, initial[None], last_step)
    previous = jnp.concatenate([first_prev, state[:-1]], 0)
    squares = (0.5 * state * state).astype(jnp.bfloat16)
    padded = extended(squares, (("space", 1),), 2)
    flux = apply_padded(padded, blocks, couple)
    residual = forcing - state + previous - time_step * flux
    steps_global = position * local_steps + jnp.arange(local_steps, dtype=jnp.int32)
    log_rate = math.log(alpha_rate) / total_steps
    scaled = residual * jnp.exp(steps_global.astype(jnp.float32) * log_rate)[:, None, None]
    cur_re = scaled
    cur_im = jnp.zeros_like(scaled)
    for level in range(level_count):
        bit_number = level_count - 1 - level
        half = 1 << bit_number
        other = from_partner(jnp.stack([cur_re, cur_im]), "tm", bit_number)
        upper = position >> bit_number & 1 == 1
        angle = -2.0 * math.pi * (position % half).astype(jnp.float32) / (2 * half)
        tw_re = jnp.cos(angle)
        tw_im = jnp.sin(angle)
        diff_re = other[0] - cur_re
        diff_im = other[1] - cur_im
        new_re = jnp.where(upper, diff_re * tw_re - diff_im * tw_im, cur_re + other[0])
        new_im = jnp.where(upper, diff_re * tw_im + diff_im * tw_re, cur_im + other[1])
        cur_re, cur_im = (new_re, new_im)
    freq_base = jnp.zeros((), jnp.int32)
    for level in range(level_count):
        freq_base = freq_base + (position >> level & 1) * (1 << level_count - 1 - level)
    part_re, part_im = (cur_re, cur_im)
    local_index = jnp.arange(local_steps, dtype=jnp.int32)
    freq = freq_base + devices_tm * local_index
    product = freq[:, None] * local_index[None, :] % total_steps
    angle_table = 2.0 * math.pi * product.astype(jnp.float32) / total_steps
    table_re = jnp.cos(angle_table)
    table_im = -jnp.sin(angle_table)
    spec_re = jnp.einsum("qm,mbc->qbc", table_re, part_re, precision=highest) - jnp.einsum(
        "qm,mbc->qbc", table_im, part_im, precision=highest
    )
    spec_im = jnp.einsum("qm,mbc->qbc", table_re, part_im, precision=highest) + jnp.einsum(
        "qm,mbc->qbc", table_im, part_re, precision=highest
    )
    theta = 2.0 * math.pi * freq.astype(jnp.float32) / total_steps
    rate = math.exp(log_rate)
    lam_re = (1.0 - rate * jnp.cos(theta))[:, None, None]
    lam_im = (rate * jnp.sin(theta))[:, None, None]
    denom = (1.0 + lam_re) ** 2 + lam_im**2
    coef_re = (1.0 + lam_re) / denom
    coef_im = -lam_im / denom
    sol_re = None
    sol_im = None
    for sweep in range(SWEEPS):
        if sweep == 0:
            res_re, res_im = (spec_re, spec_im)
        else:
            stacked = jnp.concatenate([sol_re, sol_im], 0).astype(jnp.bfloat16)
            padded_sol = extended(stacked, (("space", 1),), 2)
            applied = apply_padded(padded_sol, blocks, couple)
            res_re = (
                spec_re - (lam_re * sol_re - lam_im * sol_im) - time_step * applied[:local_steps]
            )
            res_im = (
                spec_im - (lam_re * sol_im + lam_im * sol_re) - time_step * applied[local_steps:]
            )
        rounded = jnp.concatenate([res_re, res_im], 0).astype(jnp.bfloat16)
        gres = jnp.einsum("fbj,bij->fbi", rounded, precond, preferred_element_type=jnp.float32)
        g_re = gres[:local_steps]
        g_im = gres[local_steps:]
        step_re = relaxation * (coef_re * g_re - coef_im * g_im)
        step_im = relaxation * (coef_re * g_im + coef_im * g_re)
        if sweep == 0:
            sol_re, sol_im = (step_re, step_im)
        else:
            sol_re = sol_re + step_re
            sol_im = sol_im + step_im
    back_re = (
        jnp.einsum("qm,qbc->mbc", table_re, sol_re, precision=highest)
        + jnp.einsum("qm,qbc->mbc", table_im, sol_im, precision=highest)
    ) / local_steps
    back_im = (
        jnp.einsum("qm,qbc->mbc", table_re, sol_im, precision=highest)
        - jnp.einsum("qm,qbc->mbc", table_im, sol_re, precision=highest)
    ) / local_steps
    cur_re, cur_im = (back_re, back_im)
    for bit_number in range(level_count):
        half = 1 << bit_number
        other = from_partner(jnp.stack([cur_re, cur_im]), "tm", bit_number)
        upper = position >> bit_number & 1 == 1
        angle = -2.0 * math.pi * (position % half).astype(jnp.float32) / (2 * half)
        conj_re = jnp.cos(angle)
        conj_im = -jnp.sin(angle)
        other_tw_re = other[0] * conj_re - other[1] * conj_im
        other_tw_im = other[0] * conj_im + other[1] * conj_re
        mine_tw_re = cur_re * conj_re - cur_im * conj_im
        mine_tw_im = cur_re * conj_im + cur_im * conj_re
        new_re = jnp.where(upper, 0.5 * (other[0] - mine_tw_re), 0.5 * (cur_re + other_tw_re))
        new_im = jnp.where(upper, 0.5 * (other[1] - mine_tw_im), 0.5 * (cur_im + other_tw_im))
        cur_re, cur_im = (new_re, new_im)
    change = cur_re * jnp.exp(-steps_global.astype(jnp.float32) * log_rate)[:, None, None]
    return state + change


MESH = pl.DeviceIdType.MESH


def tables(steps):
    half = steps // 2
    rate = math.exp(math.log(alpha_rate) / steps)
    step = np.arange(steps)
    freq = np.arange(half)
    angle = 2.0 * np.pi * ((freq[:, None] * step[None, :]) % steps) / steps
    cosine, sine = np.cos(angle), np.sin(angle)
    nyquist = 1.0 - 2.0 * (step % 2)
    forward = np.concatenate([cosine, nyquist[None], -sine[1:]], 0) * rate**step
    inverse = np.concatenate([2.0 * cosine, nyquist[None], -2.0 * sine[1:]], 0)
    inverse[0] = 1.0
    inverse = inverse.T / steps * (rate ** (-step))[:, None]
    theta = 2.0 * np.pi * np.arange(half + 1) / steps
    lam = 1.0 - rate * np.exp(-1j * theta)
    lam[half] = lam[half].real
    coef = relaxation / (1.0 + lam)

    def columns(factor):
        real = np.concatenate([factor.real[:half], factor.real[half:], factor.real[1:half]])
        imag = np.concatenate([[0.0], factor.imag[1:half]])
        return real, np.concatenate([-imag, imag])

    coef_own, coef_swap = columns(coef)
    lam_own, lam_swap = columns(lam * coef)
    swap = np.roll(np.eye(steps), half, 1)
    inverse = inverse @ (np.diag(coef_own) + np.diag(coef_swap) @ swap)
    lanes = -(-steps // 128) * 128
    factors = np.zeros((steps, lanes), np.float32)
    for place, column in enumerate((coef_own, coef_swap, lam_own, lam_swap)):
        factors[:, place] = column
    matrices = np.stack([np.tile(matrix, 2) for matrix in (forward, inverse)])
    return matrices.astype(np.float32), factors


def halves(field, axis):
    high = field.astype(jnp.bfloat16)
    low = (field - high.astype(jnp.float32)).astype(jnp.bfloat16)
    return jnp.concatenate([high, low], axis)


def transformed(matrix, field):
    both = halves(field, 0)
    return jnp.dot(
        halves(matrix, 1),
        jnp.concatenate([both, both], 0),
        preferred_element_type=jnp.float32,
    )


def bits_of(number, count):
    return [lax.rem(lax.div(number, 1 << i), 2) for i in range(count)]


def number_of(bits):
    return sum(bit * (1 << i) for i, bit in enumerate(bits))


def flipped(bits, mask):
    return [1 - bit if mask >> i & 1 else bit for i, bit in enumerate(bits)]


def differ(a, b):
    return a + b - 2 * a * b


def rank_at(bits, odd):
    bits = list(bits)
    for i in reversed(range(len(bits) - 1)):
        bits[i] = differ(bits[i], bits[i + 1])
    return number_of([differ(bit, odd) for bit in bits])


def position_at(rank, odd, count):
    bits = [differ(bit, odd) for bit in bits_of(rank, count)]
    for i in range(count - 1):
        bits[i] = differ(bits[i], bits[i + 1])
    return number_of(bits)


def kernel(
    sizes,
    state_h,
    forcing_h,
    initial_h,
    blocks_h,
    precond_h,
    couple_h,
    matrix_h,
    factor_h,
    out_ref,
    state_v,
    forcing_v,
    initial_v,
    wb,
    wp,
    wbt,
    wpt,
    matrix_v,
    factor_v,
    couple_s,
    chunk,
    edge,
    diff,
    rq,
    rd,
    redge,
    xsq,
    xsol,
    back,
    rback,
    local_sem,
    q_send,
    q_recv,
    d_send,
    d_recv,
    edge_send,
    edge_recv,
    halo_send,
    halo_recv,
    b_send,
    b_recv,
):
    nt, ns, steps, width, own = sizes
    total = nt * steps
    half = total // 2
    t = lax.axis_index("tm")
    s = lax.axis_index("space")
    level = nt.bit_length() - 1
    odd = lax.rem(s, 2)
    place_bits = bits_of(t, level)
    rank = rank_at(place_bits, odd)
    first, last = rank == 0, rank == nt - 1
    targets = [number_of(flipped(place_bits, o)) for o in range(nt)]
    ranks = [rank_at(flipped(place_bits, o), odd) for o in range(nt)]
    order = range(nt - 1, 0, -1)
    top = nt // 2
    first_place = odd * top, (1 - odd) * top
    last_place = first_place[1], first_place[0]
    below, above = s > 0, s < ns - 1
    lower, upper = jnp.maximum(s - 1, 0), jnp.minimum(s + 1, ns - 1)
    low_edge = jnp.logical_and(first, below)
    high_edge = jnp.logical_and(last, above)

    start = rank * own
    loads = [
        pltpu.make_async_copy(source, target, local_sem.at[place])
        for place, (source, target) in enumerate(
            (
                (state_h, state_v),
                (forcing_h, forcing_v),
                (initial_h, initial_v),
                (blocks_h.at[:, pl.ds(start, own)], wb),
                (matrix_h, matrix_v),
                (factor_h, factor_v),
                (precond_h.at[pl.ds(start, own)], wp),
                (couple_h, couple_s),
            )
        )
    ]
    for load in loads[:3]:
        load.start()

    barrier = pltpu.get_barrier_semaphore()
    for o in order:
        pl.semaphore_signal(barrier, inc=1, device_id=(targets[o], s), device_id_type=MESH)

    @pl.when(low_edge)
    def _():
        for o in range(nt):
            pl.semaphore_signal(barrier, inc=1, device_id=(o, lower), device_id_type=MESH)

    @pl.when(high_edge)
    def _():
        for o in range(nt):
            pl.semaphore_signal(barrier, inc=1, device_id=(o, upper), device_id_type=MESH)

    for load in loads[3:]:
        load.start()

    loads[0].wait()
    state = state_v[...]
    by_block = jnp.swapaxes(state, 0, 1)
    squares = 0.5 * by_block * by_block
    blank = jnp.zeros((steps, squares.shape[2]), jnp.float32)
    for target in range(nt):
        parts = []
        for j in range(own * target - 2, own * (target + 1) + 2):
            parts.append(squares[j] if 0 <= j < width else blank)
        tail = state[steps - 1, own * target : own * (target + 1)]
        tail_hi = tail.astype(jnp.bfloat16).astype(jnp.float32)
        parts += [tail_hi, tail - tail_hi]
        if steps > 2 * own:
            parts.append(blank[: steps - 2 * own])
        chunk[target] = jnp.concatenate(parts, 0).astype(jnp.bfloat16)
    edge[0] = jnp.concatenate([squares[width - 2], squares[width - 1]], 0).astype(jnp.bfloat16)
    edge[1] = jnp.concatenate([squares[0], squares[1]], 0).astype(jnp.bfloat16)

    signals = nt - 1 + jnp.where(below, 1, 0) + jnp.where(above, 1, 0)
    pl.semaphore_wait(barrier, signals)

    edge_up = pltpu.make_async_remote_copy(
        src_ref=edge.at[0],
        dst_ref=redge.at[t],
        send_sem=edge_send.at[0],
        recv_sem=edge_recv.at[t],
        device_id=(first_place[1], upper),
        device_id_type=MESH,
    )
    edge_down = pltpu.make_async_remote_copy(
        src_ref=edge.at[1],
        dst_ref=redge.at[t],
        send_sem=edge_send.at[1],
        recv_sem=edge_recv.at[t],
        device_id=(last_place[1], lower),
        device_id_type=MESH,
    )

    @pl.when(above)
    def _():
        edge_up.start()

    @pl.when(below)
    def _():
        edge_down.start()

    q_copies = []
    for o in order:
        target = targets[o]
        q_copies.append(
            pltpu.make_async_remote_copy(
                src_ref=chunk.at[ranks[o]],
                dst_ref=rq.at[t],
                send_sem=q_send.at[o],
                recv_sem=q_recv.at[o],
                device_id=(target, s),
                device_id_type=MESH,
            )
        )
    for copy in q_copies:
        copy.start()

    loads[1].wait()
    loads[2].wait()
    forcing = forcing_v[...]
    initial = jnp.where(t == 0, initial_v[...], 0.0)
    previous = jnp.concatenate([initial[None], state[:-1]], 0)
    diff[...] = jnp.swapaxes(forcing - state + previous, 0, 1)
    d_copies = []
    for o in order:
        target = targets[o]
        d_copies.append(
            pltpu.make_async_remote_copy(
                src_ref=diff.at[pl.ds(ranks[o] * own, own)],
                dst_ref=rd.at[t],
                send_sem=d_send.at[o],
                recv_sem=d_recv.at[o],
                device_id=(target, s),
                device_id_type=MESH,
            )
        )
    for copy in d_copies:
        copy.start()
    rq[t] = chunk[rank]
    rd[t] = diff[pl.ds(start, own)]

    loads[3].wait()
    slots, size = wb.shape[0], wb.shape[2]
    for e in range(own):
        for slot in range(slots):
            wbt[e, slot * size : (slot + 1) * size] = wb[slot, e].T
    loads[6].wait()
    for e in range(own):
        wpt[e] = wp[e].T

    for copy in q_copies:
        copy.wait_recv()
    got = [rq[source].astype(jnp.float32) for source in range(nt)]
    for e in range(own + 4):
        xsq[e] = jnp.concatenate(
            [part[e * steps : (e + 1) * steps] for part in got], 0
        ).astype(jnp.bfloat16)
    lead = (own + 4) * steps
    tails = [
        part[lead : lead + own] + part[lead + own : lead + 2 * own] for part in got[:-1]
    ]

    def take_edge(place):
        for source in range(nt):
            pltpu.make_async_remote_copy(
                src_ref=edge.at[0],
                dst_ref=redge.at[source],
                send_sem=edge_send.at[0],
                recv_sem=edge_recv.at[source],
                device_id=(0, 0),
                device_id_type=MESH,
            ).wait_recv()
        edges = [redge[source].astype(jnp.float32) for source in range(nt)]
        for e in range(2):
            xsq[place + e] = jnp.concatenate(
                [part[e * steps : (e + 1) * steps] for part in edges], 0
            ).astype(jnp.bfloat16)

    @pl.when(low_edge)
    def _():
        take_edge(0)

    @pl.when(high_edge)
    def _():
        take_edge(own + 2)

    loads[7].wait()

    def coupled(field, e):
        rows = [field[e + 2 + couple_s[slot, start + e]] for slot in range(slots)]
        return jnp.dot(
            jnp.concatenate(rows, 1), wbt[e], preferred_element_type=jnp.float32
        )

    def conditioned(rounded):
        return jnp.concatenate(
            [
                jnp.dot(
                    rounded[:, e * size : (e + 1) * size],
                    wpt[e],
                    preferred_element_type=jnp.float32,
                )
                for e in range(own)
            ],
            1,
        )

    flux = [coupled(xsq, e) for e in range(own)]
    for copy in d_copies:
        copy.wait_recv()
    leading = lax.broadcasted_iota(jnp.int32, blank.shape, 0) == 0
    residual = []
    for e in range(own):
        parts = [rd[0, e]]
        for source in range(1, nt):
            carried = jnp.broadcast_to(tails[source - 1][e : e + 1], blank.shape)
            parts.append(rd[source, e] + jnp.where(leading, carried, 0.0))
        residual.append(jnp.concatenate(parts, 0) - time_step * flux[e])
    loads[4].wait()
    spectrum = transformed(matrix_v[0], jnp.concatenate(residual, 1))

    loads[5].wait()
    first_step = conditioned(spectrum.astype(jnp.bfloat16))
    swapped = jnp.concatenate([first_step[half:], first_step[:half]], 0)
    factors = factor_v[...]
    sol = factors[:, 0:1] * first_step + factors[:, 1:2] * swapped
    for e in range(own):
        xsol[2 + e] = sol[:, e * size : (e + 1) * size].astype(jnp.bfloat16)

    has_down = jnp.logical_or(rank > 0, below)
    has_up = jnp.logical_or(rank < nt - 1, above)
    down_s = jnp.where(first, lower, s)
    before = position_at(jnp.maximum(rank - 1, 0), odd, level)
    down_t = jnp.where(first, last_place[1], before)
    up_s = jnp.where(last, upper, s)
    after = position_at(jnp.minimum(rank + 1, nt - 1), odd, level)
    up_t = jnp.where(last, first_place[1], after)
    halo_down = pltpu.make_async_remote_copy(
        src_ref=xsol.at[pl.ds(2, 2)],
        dst_ref=xsol.at[pl.ds(own + 2, 2)],
        send_sem=halo_send.at[0],
        recv_sem=halo_recv.at[0],
        device_id=(down_t, down_s),
        device_id_type=MESH,
    )
    halo_up = pltpu.make_async_remote_copy(
        src_ref=xsol.at[pl.ds(own, 2)],
        dst_ref=xsol.at[pl.ds(0, 2)],
        send_sem=halo_send.at[1],
        recv_sem=halo_recv.at[1],
        device_id=(up_t, up_s),
        device_id_type=MESH,
    )

    @pl.when(has_down)
    def _():
        halo_down.start()

    @pl.when(has_up)
    def _():
        halo_up.start()

    @pl.when(jnp.logical_not(has_down))
    def _():
        xsol[0:2] = jnp.zeros((2,) + xsol.shape[1:], jnp.bfloat16)

    @pl.when(jnp.logical_not(has_up))
    def _():
        xsol[own + 2 : own + 4] = jnp.zeros((2,) + xsol.shape[1:], jnp.bfloat16)

    left = spectrum - (factors[:, 2:3] * first_step + factors[:, 3:4] * swapped)

    @pl.when(has_down)
    def _():
        halo_up.wait_recv()

    @pl.when(has_up)
    def _():
        halo_down.wait_recv()

    applied = jnp.concatenate([coupled(xsol, e) for e in range(own)], 1)
    left = left - time_step * applied
    steps_sum = first_step + conditioned(left.astype(jnp.bfloat16))
    change = transformed(matrix_v[1], steps_sum)
    for e in range(own):
        back[e] = change[:, e * size : (e + 1) * size]
    b_copies = []
    for o in order:
        target = targets[o]
        b_copies.append(
            pltpu.make_async_remote_copy(
                src_ref=back.at[:, pl.ds(pl.multiple_of(target * steps, steps), steps)],
                dst_ref=rback.at[pl.ds(start, own)],
                send_sem=b_send.at[o],
                recv_sem=b_recv.at[o],
                device_id=(target, s),
                device_id_type=MESH,
            )
        )
    for copy in b_copies:
        copy.start()
    rback[pl.ds(start, own)] = back[:, pl.ds(pl.multiple_of(t * steps, steps), steps)]
    for copy in b_copies:
        copy.wait_recv()
    out_ref[...] = state_v[...] + jnp.swapaxes(rback[...], 0, 1)

    for copy in q_copies + d_copies + b_copies:
        copy.wait_send()

    @pl.when(above)
    def _():
        edge_up.wait_send()

    @pl.when(below)
    def _():
        edge_down.wait_send()

    @pl.when(has_down)
    def _():
        halo_down.wait_send()

    @pl.when(has_up)
    def _():
        halo_up.wait_send()


def on_device_blocks(state, forcing, initial, blocks, precond, couple):
    nt, ns = lax.axis_size("tm"), lax.axis_size("space")
    steps, width, size = state.shape
    own = width // nt
    total = nt * steps
    slots = blocks.shape[0]
    matrix, factor = (jnp.asarray(table) for table in tables(total))
    far = pl.BlockSpec(memory_space=pltpu.HBM)
    rows = (own + 5) * steps
    f32, b16 = jnp.float32, jnp.bfloat16
    dma = pltpu.SemaphoreType.DMA
    return pl.pallas_call(
        functools.partial(kernel, (nt, ns, steps, width, own)),
        out_shape=pltpu.VMEM(state.shape, f32),
        in_specs=[far] * 8,
        out_specs=pl.BlockSpec(memory_space=pltpu.VMEM),
        scratch_shapes=[
            pltpu.VMEM(state.shape, f32),
            pltpu.VMEM(state.shape, f32),
            pltpu.VMEM(initial.shape, f32),
            pltpu.VMEM((slots, own, size, size), b16),
            pltpu.VMEM((own, size, size), b16),
            pltpu.VMEM((own, slots * size, size), b16),
            pltpu.VMEM((own, size, size), b16),
            pltpu.VMEM(matrix.shape, f32),
            pltpu.VMEM(factor.shape, f32),
            pltpu.SMEM(couple.shape[::-1], jnp.int32),
            pltpu.VMEM((nt, rows, size), b16),
            pltpu.VMEM((2, 2 * steps, size), b16),
            pltpu.VMEM((width, steps, size), f32),
            pltpu.VMEM((nt, rows, size), b16),
            pltpu.VMEM((nt, own, steps, size), f32),
            pltpu.VMEM((nt, 2 * steps, size), b16),
            pltpu.VMEM((own + 4, total, size), b16),
            pltpu.VMEM((own + 4, total, size), b16),
            pltpu.VMEM((own, total, size), f32),
            pltpu.VMEM((width, steps, size), f32),
            dma((8,)),
            dma((nt,)),
            dma((nt,)),
            dma((nt,)),
            dma((nt,)),
            dma((2,)),
            dma((nt,)),
            dma((2,)),
            dma((2,)),
            dma((nt,)),
            dma((nt,)),
        ],
        compiler_params=pltpu.CompilerParams(
            collective_id=0, has_side_effects=True, vmem_limit_bytes=60 * 1024 * 1024
        ),
    )(state, forcing, initial, blocks, precond, couple.T, matrix, factor)


def on_device(state, forcing, initial, blocks, precond, couple):
    nt = lax.axis_size("tm")
    steps, width, _ = state.shape
    own = width // nt
    even_cut = width % nt == 0 and own >= 2 and 2 * own <= steps and steps % 8 == 0
    power = nt > 1 and nt & nt - 1 == 0 and nt * steps % 16 == 0
    if power and even_cut and (own + 5) * steps % 16 == 0:
        return on_device_blocks(state, forcing, initial, blocks, precond, couple)
    return on_device_steps(state, forcing, initial, blocks, precond, couple)


def solution(mesh):
    placed = (
        P("tm", "space", None),
        P("tm", "space", None),
        P("space", None),
        P(None, "space", None, None),
        P("space", None, None),
        P("space", None),
    )
    return jax.shard_map(
        on_device, mesh=mesh, in_specs=placed, out_specs=P("tm", "space", None), check_vma=False
    )
```

```python
import functools
import math

import jax
import jax.numpy as jnp
import numpy as np
from jax import lax
from jax.experimental import pallas as pl
from jax.experimental.pallas import tpu as pltpu
from jax.sharding import PartitionSpec as P

SWEEPS = 2


alpha_rate = 0.5
time_step = 0.5
relaxation = 0.7


def from_behind(block, axis, distance):
    devices = range(lax.axis_size(axis))
    route = [(i - distance, i) for i in devices if i - distance in devices]
    return lax.ppermute(block, axis, route)


def extended(block, sides, width):
    for axis, dim in sides:
        count = lax.axis_size(axis)
        forward = [(i, i + 1) for i in range(count - 1)]
        backward = [(target, source) for source, target in forward]
        low = lax.ppermute(
            lax.slice_in_dim(block, block.shape[dim] - width, None, axis=dim), axis, forward
        )
        high = lax.ppermute(lax.slice_in_dim(block, 0, width, axis=dim), axis, backward)
        block = jnp.concatenate([low, block, high], axis=dim)
    return block


def from_partner(block, axis, stride):
    count = lax.axis_size(axis)
    route = []
    for low in range(count):
        high = low | 1 << stride
        if high != low and high < count:
            route += [(low, high), (high, low)]
    return lax.ppermute(block, axis, route)


def apply_padded(padded, blocks, couple):
    width = padded.shape[1] - 4
    total = None
    for column in range(5):
        chosen = padded[:, 2 : 2 + width]
        for offset in range(-2, 3):
            picked = (couple[:, column] == offset)[None, :, None]
            chosen = jnp.where(picked, padded[:, 2 + offset : 2 + offset + width], chosen)
        term = jnp.einsum(
            "fbj,bij->fbi", chosen, blocks[column], preferred_element_type=jnp.float32
        )
        total = term if total is None else total + term
    return total


def on_device_steps(state, forcing, initial, blocks, precond, couple):
    local_steps = state.shape[0]
    devices_tm = lax.axis_size("tm")
    position = lax.axis_index("tm")
    total_steps = local_steps * devices_tm
    level_count = devices_tm.bit_length() - 1
    highest = lax.Precision.HIGHEST
    last_step = from_behind(state[-1:], "tm", 1)
    first_prev = jnp.where(position == 0, initial[None], last_step)
    previous = jnp.concatenate([first_prev, state[:-1]], 0)
    squares = (0.5 * state * state).astype(jnp.bfloat16)
    padded = extended(squares, (("space", 1),), 2)
    flux = apply_padded(padded, blocks, couple)
    residual = forcing - state + previous - time_step * flux
    steps_global = position * local_steps + jnp.arange(local_steps, dtype=jnp.int32)
    log_rate = math.log(alpha_rate) / total_steps
    scaled = residual * jnp.exp(steps_global.astype(jnp.float32) * log_rate)[:, None, None]
    cur_re = scaled
    cur_im = jnp.zeros_like(scaled)
    for level in range(level_count):
        bit_number = level_count - 1 - level
        half = 1 << bit_number
        other = from_partner(jnp.stack([cur_re, cur_im]), "tm", bit_number)
        upper = position >> bit_number & 1 == 1
        angle = -2.0 * math.pi * (position % half).astype(jnp.float32) / (2 * half)
        tw_re = jnp.cos(angle)
        tw_im = jnp.sin(angle)
        diff_re = other[0] - cur_re
        diff_im = other[1] - cur_im
        new_re = jnp.where(upper, diff_re * tw_re - diff_im * tw_im, cur_re + other[0])
        new_im = jnp.where(upper, diff_re * tw_im + diff_im * tw_re, cur_im + other[1])
        cur_re, cur_im = (new_re, new_im)
    freq_base = jnp.zeros((), jnp.int32)
    for level in range(level_count):
        freq_base = freq_base + (position >> level & 1) * (1 << level_count - 1 - level)
    part_re, part_im = (cur_re, cur_im)
    local_index = jnp.arange(local_steps, dtype=jnp.int32)
    freq = freq_base + devices_tm * local_index
    product = freq[:, None] * local_index[None, :] % total_steps
    angle_table = 2.0 * math.pi * product.astype(jnp.float32) / total_steps
    table_re = jnp.cos(angle_table)
    table_im = -jnp.sin(angle_table)
    spec_re = jnp.einsum("qm,mbc->qbc", table_re, part_re, precision=highest) - jnp.einsum(
        "qm,mbc->qbc", table_im, part_im, precision=highest
    )
    spec_im = jnp.einsum("qm,mbc->qbc", table_re, part_im, precision=highest) + jnp.einsum(
        "qm,mbc->qbc", table_im, part_re, precision=highest
    )
    theta = 2.0 * math.pi * freq.astype(jnp.float32) / total_steps
    rate = math.exp(log_rate)
    lam_re = (1.0 - rate * jnp.cos(theta))[:, None, None]
    lam_im = (rate * jnp.sin(theta))[:, None, None]
    denom = (1.0 + lam_re) ** 2 + lam_im**2
    coef_re = (1.0 + lam_re) / denom
    coef_im = -lam_im / denom
    sol_re = None
    sol_im = None
    for sweep in range(SWEEPS):
        if sweep == 0:
            res_re, res_im = (spec_re, spec_im)
        else:
            stacked = jnp.concatenate([sol_re, sol_im], 0).astype(jnp.bfloat16)
            padded_sol = extended(stacked, (("space", 1),), 2)
            applied = apply_padded(padded_sol, blocks, couple)
            res_re = (
                spec_re - (lam_re * sol_re - lam_im * sol_im) - time_step * applied[:local_steps]
            )
            res_im = (
                spec_im - (lam_re * sol_im + lam_im * sol_re) - time_step * applied[local_steps:]
            )
        rounded = jnp.concatenate([res_re, res_im], 0).astype(jnp.bfloat16)
        gres = jnp.einsum("fbj,bij->fbi", rounded, precond, preferred_element_type=jnp.float32)
        g_re = gres[:local_steps]
        g_im = gres[local_steps:]
        step_re = relaxation * (coef_re * g_re - coef_im * g_im)
        step_im = relaxation * (coef_re * g_im + coef_im * g_re)
        if sweep == 0:
            sol_re, sol_im = (step_re, step_im)
        else:
            sol_re = sol_re + step_re
            sol_im = sol_im + step_im
    back_re = (
        jnp.einsum("qm,qbc->mbc", table_re, sol_re, precision=highest)
        + jnp.einsum("qm,qbc->mbc", table_im, sol_im, precision=highest)
    ) / local_steps
    back_im = (
        jnp.einsum("qm,qbc->mbc", table_re, sol_im, precision=highest)
        - jnp.einsum("qm,qbc->mbc", table_im, sol_re, precision=highest)
    ) / local_steps
    cur_re, cur_im = (back_re, back_im)
    for bit_number in range(level_count):
        half = 1 << bit_number
        other = from_partner(jnp.stack([cur_re, cur_im]), "tm", bit_number)
        upper = position >> bit_number & 1 == 1
        angle = -2.0 * math.pi * (position % half).astype(jnp.float32) / (2 * half)
        conj_re = jnp.cos(angle)
        conj_im = -jnp.sin(angle)
        other_tw_re = other[0] * conj_re - other[1] * conj_im
        other_tw_im = other[0] * conj_im + other[1] * conj_re
        mine_tw_re = cur_re * conj_re - cur_im * conj_im
        mine_tw_im = cur_re * conj_im + cur_im * conj_re
        new_re = jnp.where(upper, 0.5 * (other[0] - mine_tw_re), 0.5 * (cur_re + other_tw_re))
        new_im = jnp.where(upper, 0.5 * (other[1] - mine_tw_im), 0.5 * (cur_im + other_tw_im))
        cur_re, cur_im = (new_re, new_im)
    change = cur_re * jnp.exp(-steps_global.astype(jnp.float32) * log_rate)[:, None, None]
    return state + change


MESH = pl.DeviceIdType.MESH


def tables(steps):
    half = steps // 2
    rate = math.exp(math.log(alpha_rate) / steps)
    step = np.arange(steps)
    freq = np.arange(half)
    angle = 2.0 * np.pi * ((freq[:, None] * step[None, :]) % steps) / steps
    cosine, sine = np.cos(angle), np.sin(angle)
    nyquist = 1.0 - 2.0 * (step % 2)
    forward = np.concatenate([cosine, nyquist[None], -sine[1:]], 0) * rate**step
    inverse = np.concatenate([2.0 * cosine, nyquist[None], -2.0 * sine[1:]], 0)
    inverse[0] = 1.0
    inverse = inverse.T / steps * (rate ** (-step))[:, None]
    theta = 2.0 * np.pi * np.arange(half + 1) / steps
    lam = 1.0 - rate * np.exp(-1j * theta)
    lam[half] = lam[half].real
    coef = relaxation / (1.0 + lam)

    def columns(factor):
        real = np.concatenate([factor.real[:half], factor.real[half:], factor.real[1:half]])
        imag = np.concatenate([[0.0], factor.imag[1:half]])
        return real, np.concatenate([-imag, imag])

    coef_own, coef_swap = columns(coef)
    lam_own, lam_swap = columns(lam * coef)
    swap = np.roll(np.eye(steps), half, 1)
    inverse = inverse @ (np.diag(coef_own) + np.diag(coef_swap) @ swap)
    lanes = -(-steps // 128) * 128
    factors = np.zeros((steps, lanes), np.float32)
    for place, column in enumerate((coef_own, coef_swap, lam_own, lam_swap)):
        factors[:, place] = column
    matrices = np.stack([np.tile(matrix, 2) for matrix in (forward, inverse)])
    return matrices.astype(np.float32), factors


def halves(field, axis):
    high = field.astype(jnp.bfloat16)
    low = (field - high.astype(jnp.float32)).astype(jnp.bfloat16)
    return jnp.concatenate([high, low], axis)


def transformed(matrix, field):
    both = halves(field, 0)
    return jnp.dot(
        halves(matrix, 1),
        jnp.concatenate([both, both], 0),
        preferred_element_type=jnp.float32,
    )


def bits_of(number, count):
    return [lax.rem(lax.div(number, 1 << i), 2) for i in range(count)]


def number_of(bits):
    return sum(bit * (1 << i) for i, bit in enumerate(bits))


def flipped(bits, mask):
    return [1 - bit if mask >> i & 1 else bit for i, bit in enumerate(bits)]


def differ(a, b):
    return a + b - 2 * a * b


def rank_at(bits, odd):
    bits = list(bits)
    for i in reversed(range(len(bits) - 1)):
        bits[i] = differ(bits[i], bits[i + 1])
    return number_of([differ(bit, odd) for bit in bits])


def position_at(rank, odd, count):
    bits = [differ(bit, odd) for bit in bits_of(rank, count)]
    for i in range(count - 1):
        bits[i] = differ(bits[i], bits[i + 1])
    return number_of(bits)


def kernel(
    sizes,
    state_h,
    forcing_h,
    initial_h,
    blocks_h,
    precond_h,
    couple_h,
    matrix_h,
    factor_h,
    out_ref,
    state_v,
    forcing_v,
    initial_v,
    wb,
    wp,
    wbt,
    wpt,
    matrix_v,
    factor_v,
    couple_s,
    chunk,
    edge,
    diff,
    rq,
    rd,
    redge,
    xsq,
    xsol,
    back,
    rback,
    local_sem,
    q_send,
    q_recv,
    d_send,
    d_recv,
    edge_send,
    edge_recv,
    halo_send,
    halo_recv,
    b_send,
    b_recv,
):
    nt, ns, steps, width, own = sizes
    total = nt * steps
    half = total // 2
    t = lax.axis_index("tm")
    s = lax.axis_index("space")
    level = nt.bit_length() - 1
    odd = lax.rem(s, 2)
    place_bits = bits_of(t, level)
    rank = rank_at(place_bits, odd)
    first, last = rank == 0, rank == nt - 1
    targets = [number_of(flipped(place_bits, o)) for o in range(nt)]
    ranks = [rank_at(flipped(place_bits, o), odd) for o in range(nt)]
    order = sorted(range(1, nt), key=lambda o: (o < 2, -(o % 2), -o))
    top = nt // 2
    first_place = odd * top, (1 - odd) * top
    last_place = first_place[1], first_place[0]
    below, above = s > 0, s < ns - 1
    lower, upper = jnp.maximum(s - 1, 0), jnp.minimum(s + 1, ns - 1)
    low_edge = jnp.logical_and(first, below)
    high_edge = jnp.logical_and(last, above)

    start = rank * own
    loads = [
        pltpu.make_async_copy(source, target, local_sem.at[place])
        for place, (source, target) in enumerate(
            (
                (state_h, state_v),
                (forcing_h, forcing_v),
                (initial_h, initial_v),
                (blocks_h.at[:, pl.ds(start, own)], wb),
                (matrix_h, matrix_v),
                (factor_h, factor_v),
                (precond_h.at[pl.ds(start, own)], wp),
                (couple_h, couple_s),
            )
        )
    ]
    for load in loads[:3]:
        load.start()

    barrier = pltpu.get_barrier_semaphore()
    for o in order:
        pl.semaphore_signal(barrier, inc=1, device_id=(targets[o], s), device_id_type=MESH)

    @pl.when(low_edge)
    def _():
        for o in range(nt):
            pl.semaphore_signal(barrier, inc=1, device_id=(o, lower), device_id_type=MESH)

    @pl.when(high_edge)
    def _():
        for o in range(nt):
            pl.semaphore_signal(barrier, inc=1, device_id=(o, upper), device_id_type=MESH)

    for load in loads[3:]:
        load.start()

    loads[0].wait()
    state = state_v[...]
    by_block = jnp.swapaxes(state, 0, 1)
    squares = 0.5 * by_block * by_block
    blank = jnp.zeros((steps, squares.shape[2]), jnp.float32)
    for target in range(nt):
        parts = []
        for j in range(own * target - 2, own * (target + 1) + 2):
            parts.append(squares[j] if 0 <= j < width else blank)
        tail = state[steps - 1, own * target : own * (target + 1)]
        tail_hi = tail.astype(jnp.bfloat16).astype(jnp.float32)
        parts += [tail_hi, tail - tail_hi]
        if steps > 2 * own:
            parts.append(blank[: steps - 2 * own])
        chunk[target] = jnp.concatenate(parts, 0).astype(jnp.bfloat16)
    edge[0] = jnp.concatenate([squares[width - 2], squares[width - 1]], 0).astype(jnp.bfloat16)
    edge[1] = jnp.concatenate([squares[0], squares[1]], 0).astype(jnp.bfloat16)

    signals = nt - 1 + jnp.where(below, 1, 0) + jnp.where(above, 1, 0)
    pl.semaphore_wait(barrier, signals)

    edge_up = pltpu.make_async_remote_copy(
        src_ref=edge.at[0],
        dst_ref=redge.at[t],
        send_sem=edge_send.at[0],
        recv_sem=edge_recv.at[t],
        device_id=(first_place[1], upper),
        device_id_type=MESH,
    )
    edge_down = pltpu.make_async_remote_copy(
        src_ref=edge.at[1],
        dst_ref=redge.at[t],
        send_sem=edge_send.at[1],
        recv_sem=edge_recv.at[t],
        device_id=(last_place[1], lower),
        device_id_type=MESH,
    )

    @pl.when(above)
    def _():
        edge_up.start()

    @pl.when(below)
    def _():
        edge_down.start()

    q_copies = []
    for o in order:
        target = targets[o]
        q_copies.append(
            pltpu.make_async_remote_copy(
                src_ref=chunk.at[ranks[o]],
                dst_ref=rq.at[t],
                send_sem=q_send.at[o],
                recv_sem=q_recv.at[o],
                device_id=(target, s),
                device_id_type=MESH,
            )
        )
    for copy in q_copies:
        copy.start()

    loads[1].wait()
    loads[2].wait()
    forcing = forcing_v[...]
    initial = jnp.where(t == 0, initial_v[...], 0.0)
    previous = jnp.concatenate([initial[None], state[:-1]], 0)
    diff[...] = jnp.swapaxes(forcing - state + previous, 0, 1)
    d_copies = []
    for o in order:
        target = targets[o]
        d_copies.append(
            pltpu.make_async_remote_copy(
                src_ref=diff.at[pl.ds(ranks[o] * own, own)],
                dst_ref=rd.at[t],
                send_sem=d_send.at[o],
                recv_sem=d_recv.at[o],
                device_id=(target, s),
                device_id_type=MESH,
            )
        )
    for copy in d_copies:
        copy.start()
    rq[t] = chunk[rank]
    rd[t] = diff[pl.ds(start, own)]

    loads[3].wait()
    slots, size = wb.shape[0], wb.shape[2]
    for e in range(own):
        for slot in range(slots):
            wbt[e, slot * size : (slot + 1) * size] = wb[slot, e].T
    loads[6].wait()
    for e in range(own):
        wpt[e] = wp[e].T

    for copy in q_copies:
        copy.wait_recv()
    got = [rq[source].astype(jnp.float32) for source in range(nt)]
    for e in range(own + 4):
        xsq[e] = jnp.concatenate(
            [part[e * steps : (e + 1) * steps] for part in got], 0
        ).astype(jnp.bfloat16)
    lead = (own + 4) * steps
    tails = [
        part[lead : lead + own] + part[lead + own : lead + 2 * own] for part in got[:-1]
    ]

    def take_edge(place):
        for source in range(nt):
            pltpu.make_async_remote_copy(
                src_ref=edge.at[0],
                dst_ref=redge.at[source],
                send_sem=edge_send.at[0],
                recv_sem=edge_recv.at[source],
                device_id=(0, 0),
                device_id_type=MESH,
            ).wait_recv()
        edges = [redge[source].astype(jnp.float32) for source in range(nt)]
        for e in range(2):
            xsq[place + e] = jnp.concatenate(
                [part[e * steps : (e + 1) * steps] for part in edges], 0
            ).astype(jnp.bfloat16)

    @pl.when(low_edge)
    def _():
        take_edge(0)

    @pl.when(high_edge)
    def _():
        take_edge(own + 2)

    loads[7].wait()

    def coupled(field, e):
        rows = [field[e + 2 + couple_s[slot, start + e]] for slot in range(slots)]
        return jnp.dot(
            jnp.concatenate(rows, 1), wbt[e], preferred_element_type=jnp.float32
        )

    def conditioned(rounded):
        return jnp.concatenate(
            [
                jnp.dot(
                    rounded[:, e * size : (e + 1) * size],
                    wpt[e],
                    preferred_element_type=jnp.float32,
                )
                for e in range(own)
            ],
            1,
        )

    flux = [coupled(xsq, e) for e in range(own)]
    for copy in d_copies:
        copy.wait_recv()
    leading = lax.broadcasted_iota(jnp.int32, blank.shape, 0) == 0
    residual = []
    for e in range(own):
        parts = [rd[0, e]]
        for source in range(1, nt):
            carried = jnp.broadcast_to(tails[source - 1][e : e + 1], blank.shape)
            parts.append(rd[source, e] + jnp.where(leading, carried, 0.0))
        residual.append(jnp.concatenate(parts, 0) - time_step * flux[e])
    loads[4].wait()
    spectrum = transformed(matrix_v[0], jnp.concatenate(residual, 1))

    loads[5].wait()
    first_step = conditioned(spectrum.astype(jnp.bfloat16))
    swapped = jnp.concatenate([first_step[half:], first_step[:half]], 0)
    factors = factor_v[...]
    sol = factors[:, 0:1] * first_step + factors[:, 1:2] * swapped
    for e in range(own):
        xsol[2 + e] = sol[:, e * size : (e + 1) * size].astype(jnp.bfloat16)

    has_down = jnp.logical_or(rank > 0, below)
    has_up = jnp.logical_or(rank < nt - 1, above)
    down_s = jnp.where(first, lower, s)
    before = position_at(jnp.maximum(rank - 1, 0), odd, level)
    down_t = jnp.where(first, last_place[1], before)
    up_s = jnp.where(last, upper, s)
    after = position_at(jnp.minimum(rank + 1, nt - 1), odd, level)
    up_t = jnp.where(last, first_place[1], after)
    halo_down = pltpu.make_async_remote_copy(
        src_ref=xsol.at[pl.ds(2, 2)],
        dst_ref=xsol.at[pl.ds(own + 2, 2)],
        send_sem=halo_send.at[0],
        recv_sem=halo_recv.at[0],
        device_id=(down_t, down_s),
        device_id_type=MESH,
    )
    halo_up = pltpu.make_async_remote_copy(
        src_ref=xsol.at[pl.ds(own, 2)],
        dst_ref=xsol.at[pl.ds(0, 2)],
        send_sem=halo_send.at[1],
        recv_sem=halo_recv.at[1],
        device_id=(up_t, up_s),
        device_id_type=MESH,
    )

    @pl.when(has_down)
    def _():
        halo_down.start()

    @pl.when(has_up)
    def _():
        halo_up.start()

    @pl.when(jnp.logical_not(has_down))
    def _():
        xsol[0:2] = jnp.zeros((2,) + xsol.shape[1:], jnp.bfloat16)

    @pl.when(jnp.logical_not(has_up))
    def _():
        xsol[own + 2 : own + 4] = jnp.zeros((2,) + xsol.shape[1:], jnp.bfloat16)

    left = spectrum - (factors[:, 2:3] * first_step + factors[:, 3:4] * swapped)

    @pl.when(has_down)
    def _():
        halo_up.wait_recv()

    @pl.when(has_up)
    def _():
        halo_down.wait_recv()

    applied = jnp.concatenate([coupled(xsol, e) for e in range(own)], 1)
    left = left - time_step * applied
    steps_sum = first_step + conditioned(left.astype(jnp.bfloat16))
    change = transformed(matrix_v[1], steps_sum)
    for e in range(own):
        back[e] = change[:, e * size : (e + 1) * size]
    b_copies = []
    for o in order:
        target = targets[o]
        b_copies.append(
            pltpu.make_async_remote_copy(
                src_ref=back.at[:, pl.ds(pl.multiple_of(target * steps, steps), steps)],
                dst_ref=rback.at[pl.ds(start, own)],
                send_sem=b_send.at[o],
                recv_sem=b_recv.at[o],
                device_id=(target, s),
                device_id_type=MESH,
            )
        )
    for copy in b_copies:
        copy.start()
    rback[pl.ds(start, own)] = back[:, pl.ds(pl.multiple_of(t * steps, steps), steps)]
    for copy in q_copies + d_copies:
        copy.wait_send()

    @pl.when(above)
    def _():
        edge_up.wait_send()

    @pl.when(below)
    def _():
        edge_down.wait_send()

    @pl.when(has_down)
    def _():
        halo_down.wait_send()

    @pl.when(has_up)
    def _():
        halo_up.wait_send()

    for copy in b_copies:
        copy.wait_send()
    for copy in b_copies:
        copy.wait_recv()
    out_ref[...] = state_v[...] + jnp.swapaxes(rback[...], 0, 1)


def on_device_blocks(state, forcing, initial, blocks, precond, couple):
    nt, ns = lax.axis_size("tm"), lax.axis_size("space")
    steps, width, size = state.shape
    own = width // nt
    total = nt * steps
    slots = blocks.shape[0]
    matrix, factor = (jnp.asarray(table) for table in tables(total))
    far = pl.BlockSpec(memory_space=pltpu.HBM)
    rows = (own + 5) * steps
    f32, b16 = jnp.float32, jnp.bfloat16
    dma = pltpu.SemaphoreType.DMA
    return pl.pallas_call(
        functools.partial(kernel, (nt, ns, steps, width, own)),
        out_shape=pltpu.VMEM(state.shape, f32),
        in_specs=[far] * 8,
        out_specs=pl.BlockSpec(memory_space=pltpu.VMEM),
        scratch_shapes=[
            pltpu.VMEM(state.shape, f32),
            pltpu.VMEM(state.shape, f32),
            pltpu.VMEM(initial.shape, f32),
            pltpu.VMEM((slots, own, size, size), b16),
            pltpu.VMEM((own, size, size), b16),
            pltpu.VMEM((own, slots * size, size), b16),
            pltpu.VMEM((own, size, size), b16),
            pltpu.VMEM(matrix.shape, f32),
            pltpu.VMEM(factor.shape, f32),
            pltpu.SMEM(couple.shape[::-1], jnp.int32),
            pltpu.VMEM((nt, rows, size), b16),
            pltpu.VMEM((2, 2 * steps, size), b16),
            pltpu.VMEM((width, steps, size), f32),
            pltpu.VMEM((nt, rows, size), b16),
            pltpu.VMEM((nt, own, steps, size), f32),
            pltpu.VMEM((nt, 2 * steps, size), b16),
            pltpu.VMEM((own + 4, total, size), b16),
            pltpu.VMEM((own + 4, total, size), b16),
            pltpu.VMEM((own, total, size), f32),
            pltpu.VMEM((width, steps, size), f32),
            dma((8,)),
            dma((nt,)),
            dma((nt,)),
            dma((nt,)),
            dma((nt,)),
            dma((2,)),
            dma((nt,)),
            dma((2,)),
            dma((2,)),
            dma((nt,)),
            dma((nt,)),
        ],
        compiler_params=pltpu.CompilerParams(
            collective_id=0, has_side_effects=True, vmem_limit_bytes=60 * 1024 * 1024
        ),
    )(state, forcing, initial, blocks, precond, couple.T, matrix, factor)


def on_device(state, forcing, initial, blocks, precond, couple):
    nt = lax.axis_size("tm")
    steps, width, _ = state.shape
    own = width // nt
    even_cut = width % nt == 0 and own >= 2 and 2 * own <= steps and steps % 8 == 0
    power = nt > 1 and nt & nt - 1 == 0 and nt * steps % 16 == 0
    if power and even_cut and (own + 5) * steps % 16 == 0:
        return on_device_blocks(state, forcing, initial, blocks, precond, couple)
    return on_device_steps(state, forcing, initial, blocks, precond, couple)


def solution(mesh):
    placed = (
        P("tm", "space", None),
        P("tm", "space", None),
        P("space", None),
        P(None, "space", None, None),
        P("space", None, None),
        P("space", None),
    )
    return jax.shard_map(
        on_device, mesh=mesh, in_specs=placed, out_specs=P("tm", "space", None), check_vma=False
    )
```

```python
import functools
import math

import jax
import jax.numpy as jnp
import numpy as np
from jax import lax
from jax.experimental import pallas as pl
from jax.experimental.pallas import tpu as pltpu
from jax.sharding import PartitionSpec as P

SWEEPS = 2


alpha_rate = 0.5
time_step = 0.5
relaxation = 0.7


def from_behind(block, axis, distance):
    devices = range(lax.axis_size(axis))
    route = [(i - distance, i) for i in devices if i - distance in devices]
    return lax.ppermute(block, axis, route)


def extended(block, sides, width):
    for axis, dim in sides:
        count = lax.axis_size(axis)
        forward = [(i, i + 1) for i in range(count - 1)]
        backward = [(target, source) for source, target in forward]
        low = lax.ppermute(
            lax.slice_in_dim(block, block.shape[dim] - width, None, axis=dim), axis, forward
        )
        high = lax.ppermute(lax.slice_in_dim(block, 0, width, axis=dim), axis, backward)
        block = jnp.concatenate([low, block, high], axis=dim)
    return block


def from_partner(block, axis, stride):
    count = lax.axis_size(axis)
    route = []
    for low in range(count):
        high = low | 1 << stride
        if high != low and high < count:
            route += [(low, high), (high, low)]
    return lax.ppermute(block, axis, route)


def apply_padded(padded, blocks, couple):
    width = padded.shape[1] - 4
    total = None
    for column in range(5):
        chosen = padded[:, 2 : 2 + width]
        for offset in range(-2, 3):
            picked = (couple[:, column] == offset)[None, :, None]
            chosen = jnp.where(picked, padded[:, 2 + offset : 2 + offset + width], chosen)
        term = jnp.einsum(
            "fbj,bij->fbi", chosen, blocks[column], preferred_element_type=jnp.float32
        )
        total = term if total is None else total + term
    return total


def on_device_steps(state, forcing, initial, blocks, precond, couple):
    local_steps = state.shape[0]
    devices_tm = lax.axis_size("tm")
    position = lax.axis_index("tm")
    total_steps = local_steps * devices_tm
    level_count = devices_tm.bit_length() - 1
    highest = lax.Precision.HIGHEST
    last_step = from_behind(state[-1:], "tm", 1)
    first_prev = jnp.where(position == 0, initial[None], last_step)
    previous = jnp.concatenate([first_prev, state[:-1]], 0)
    squares = (0.5 * state * state).astype(jnp.bfloat16)
    padded = extended(squares, (("space", 1),), 2)
    flux = apply_padded(padded, blocks, couple)
    residual = forcing - state + previous - time_step * flux
    steps_global = position * local_steps + jnp.arange(local_steps, dtype=jnp.int32)
    log_rate = math.log(alpha_rate) / total_steps
    scaled = residual * jnp.exp(steps_global.astype(jnp.float32) * log_rate)[:, None, None]
    cur_re = scaled
    cur_im = jnp.zeros_like(scaled)
    for level in range(level_count):
        bit_number = level_count - 1 - level
        half = 1 << bit_number
        other = from_partner(jnp.stack([cur_re, cur_im]), "tm", bit_number)
        upper = position >> bit_number & 1 == 1
        angle = -2.0 * math.pi * (position % half).astype(jnp.float32) / (2 * half)
        tw_re = jnp.cos(angle)
        tw_im = jnp.sin(angle)
        diff_re = other[0] - cur_re
        diff_im = other[1] - cur_im
        new_re = jnp.where(upper, diff_re * tw_re - diff_im * tw_im, cur_re + other[0])
        new_im = jnp.where(upper, diff_re * tw_im + diff_im * tw_re, cur_im + other[1])
        cur_re, cur_im = (new_re, new_im)
    freq_base = jnp.zeros((), jnp.int32)
    for level in range(level_count):
        freq_base = freq_base + (position >> level & 1) * (1 << level_count - 1 - level)
    part_re, part_im = (cur_re, cur_im)
    local_index = jnp.arange(local_steps, dtype=jnp.int32)
    freq = freq_base + devices_tm * local_index
    product = freq[:, None] * local_index[None, :] % total_steps
    angle_table = 2.0 * math.pi * product.astype(jnp.float32) / total_steps
    table_re = jnp.cos(angle_table)
    table_im = -jnp.sin(angle_table)
    spec_re = jnp.einsum("qm,mbc->qbc", table_re, part_re, precision=highest) - jnp.einsum(
        "qm,mbc->qbc", table_im, part_im, precision=highest
    )
    spec_im = jnp.einsum("qm,mbc->qbc", table_re, part_im, precision=highest) + jnp.einsum(
        "qm,mbc->qbc", table_im, part_re, precision=highest
    )
    theta = 2.0 * math.pi * freq.astype(jnp.float32) / total_steps
    rate = math.exp(log_rate)
    lam_re = (1.0 - rate * jnp.cos(theta))[:, None, None]
    lam_im = (rate * jnp.sin(theta))[:, None, None]
    denom = (1.0 + lam_re) ** 2 + lam_im**2
    coef_re = (1.0 + lam_re) / denom
    coef_im = -lam_im / denom
    sol_re = None
    sol_im = None
    for sweep in range(SWEEPS):
        if sweep == 0:
            res_re, res_im = (spec_re, spec_im)
        else:
            stacked = jnp.concatenate([sol_re, sol_im], 0).astype(jnp.bfloat16)
            padded_sol = extended(stacked, (("space", 1),), 2)
            applied = apply_padded(padded_sol, blocks, couple)
            res_re = (
                spec_re - (lam_re * sol_re - lam_im * sol_im) - time_step * applied[:local_steps]
            )
            res_im = (
                spec_im - (lam_re * sol_im + lam_im * sol_re) - time_step * applied[local_steps:]
            )
        rounded = jnp.concatenate([res_re, res_im], 0).astype(jnp.bfloat16)
        gres = jnp.einsum("fbj,bij->fbi", rounded, precond, preferred_element_type=jnp.float32)
        g_re = gres[:local_steps]
        g_im = gres[local_steps:]
        step_re = relaxation * (coef_re * g_re - coef_im * g_im)
        step_im = relaxation * (coef_re * g_im + coef_im * g_re)
        if sweep == 0:
            sol_re, sol_im = (step_re, step_im)
        else:
            sol_re = sol_re + step_re
            sol_im = sol_im + step_im
    back_re = (
        jnp.einsum("qm,qbc->mbc", table_re, sol_re, precision=highest)
        + jnp.einsum("qm,qbc->mbc", table_im, sol_im, precision=highest)
    ) / local_steps
    back_im = (
        jnp.einsum("qm,qbc->mbc", table_re, sol_im, precision=highest)
        - jnp.einsum("qm,qbc->mbc", table_im, sol_re, precision=highest)
    ) / local_steps
    cur_re, cur_im = (back_re, back_im)
    for bit_number in range(level_count):
        half = 1 << bit_number
        other = from_partner(jnp.stack([cur_re, cur_im]), "tm", bit_number)
        upper = position >> bit_number & 1 == 1
        angle = -2.0 * math.pi * (position % half).astype(jnp.float32) / (2 * half)
        conj_re = jnp.cos(angle)
        conj_im = -jnp.sin(angle)
        other_tw_re = other[0] * conj_re - other[1] * conj_im
        other_tw_im = other[0] * conj_im + other[1] * conj_re
        mine_tw_re = cur_re * conj_re - cur_im * conj_im
        mine_tw_im = cur_re * conj_im + cur_im * conj_re
        new_re = jnp.where(upper, 0.5 * (other[0] - mine_tw_re), 0.5 * (cur_re + other_tw_re))
        new_im = jnp.where(upper, 0.5 * (other[1] - mine_tw_im), 0.5 * (cur_im + other_tw_im))
        cur_re, cur_im = (new_re, new_im)
    change = cur_re * jnp.exp(-steps_global.astype(jnp.float32) * log_rate)[:, None, None]
    return state + change


MESH = pl.DeviceIdType.MESH


def tables(steps):
    half = steps // 2
    rate = math.exp(math.log(alpha_rate) / steps)
    step = np.arange(steps)
    freq = np.arange(half)
    angle = 2.0 * np.pi * ((freq[:, None] * step[None, :]) % steps) / steps
    cosine, sine = np.cos(angle), np.sin(angle)
    nyquist = 1.0 - 2.0 * (step % 2)
    forward = np.concatenate([cosine, nyquist[None], -sine[1:]], 0) * rate**step
    inverse = np.concatenate([2.0 * cosine, nyquist[None], -2.0 * sine[1:]], 0)
    inverse[0] = 1.0
    inverse = inverse.T / steps * (rate ** (-step))[:, None]
    theta = 2.0 * np.pi * np.arange(half + 1) / steps
    lam = 1.0 - rate * np.exp(-1j * theta)
    lam[half] = lam[half].real
    coef = relaxation / (1.0 + lam)

    def columns(factor):
        real = np.concatenate([factor.real[:half], factor.real[half:], factor.real[1:half]])
        imag = np.concatenate([[0.0], factor.imag[1:half]])
        return real, np.concatenate([-imag, imag])

    coef_own, coef_swap = columns(coef)
    lam_own, lam_swap = columns(lam * coef)
    swap = np.roll(np.eye(steps), half, 1)
    inverse = inverse @ (np.diag(coef_own) + np.diag(coef_swap) @ swap)
    lanes = -(-steps // 128) * 128
    factors = np.zeros((steps, lanes), np.float32)
    for place, column in enumerate((coef_own, coef_swap, lam_own, lam_swap)):
        factors[:, place] = column
    matrices = np.stack([np.tile(matrix, 2) for matrix in (forward, inverse)])
    return matrices.astype(np.float32), factors


def halves(field, axis):
    high = field.astype(jnp.bfloat16)
    low = (field - high.astype(jnp.float32)).astype(jnp.bfloat16)
    return jnp.concatenate([high, low], axis)


def transformed(matrix, field):
    both = halves(field, 0)
    return jnp.dot(
        halves(matrix, 1),
        jnp.concatenate([both, both], 0),
        preferred_element_type=jnp.float32,
    )


def bits_of(number, count):
    return [lax.rem(lax.div(number, 1 << i), 2) for i in range(count)]


def number_of(bits):
    return sum(bit * (1 << i) for i, bit in enumerate(bits))


def flipped(bits, mask):
    return [1 - bit if mask >> i & 1 else bit for i, bit in enumerate(bits)]


def differ(a, b):
    return a + b - 2 * a * b


def rank_at(bits, odd):
    bits = list(bits)
    for i in reversed(range(len(bits) - 1)):
        bits[i] = differ(bits[i], bits[i + 1])
    return number_of([differ(bit, odd) for bit in bits])


def position_at(rank, odd, count):
    bits = [differ(bit, odd) for bit in bits_of(rank, count)]
    for i in range(count - 1):
        bits[i] = differ(bits[i], bits[i + 1])
    return number_of(bits)


def kernel(
    sizes,
    state_h,
    forcing_h,
    initial_h,
    blocks_h,
    precond_h,
    couple_h,
    matrix_h,
    factor_h,
    out_ref,
    state_v,
    forcing_v,
    initial_v,
    wb,
    wp,
    wbt,
    wpt,
    matrix_v,
    factor_v,
    couple_s,
    chunk,
    edge,
    diff,
    rq,
    rd,
    redge,
    xsq,
    xsol,
    back,
    rback,
    local_sem,
    q_send,
    q_recv,
    d_send,
    d_recv,
    edge_send,
    edge_recv,
    halo_send,
    halo_recv,
    b_send,
    b_recv,
):
    nt, ns, steps, width, own = sizes
    total = nt * steps
    half = total // 2
    t = lax.axis_index("tm")
    s = lax.axis_index("space")
    level = nt.bit_length() - 1
    odd = lax.rem(s, 2)
    place_bits = bits_of(t, level)
    rank = rank_at(place_bits, odd)
    first, last = rank == 0, rank == nt - 1
    targets = [number_of(flipped(place_bits, o)) for o in range(nt)]
    ranks = [rank_at(flipped(place_bits, o), odd) for o in range(nt)]
    order = sorted(range(1, nt), key=lambda o: (o < 2, -(o % 2), -o))
    top = nt // 2
    first_place = odd * top, (1 - odd) * top
    last_place = first_place[1], first_place[0]
    below, above = s > 0, s < ns - 1
    lower, upper = jnp.maximum(s - 1, 0), jnp.minimum(s + 1, ns - 1)
    low_edge = jnp.logical_and(first, below)
    high_edge = jnp.logical_and(last, above)

    start = rank * own
    loads = [
        pltpu.make_async_copy(source, target, local_sem.at[place])
        for place, (source, target) in enumerate(
            (
                (state_h, state_v),
                (forcing_h, forcing_v),
                (initial_h, initial_v),
                (blocks_h.at[:, pl.ds(start, own)], wb),
                (matrix_h, matrix_v),
                (factor_h, factor_v),
                (precond_h.at[pl.ds(start, own)], wp),
                (couple_h, couple_s),
            )
        )
    ]
    for load in loads[:3]:
        load.start()

    barrier = pltpu.get_barrier_semaphore()
    for o in order:
        pl.semaphore_signal(barrier, inc=1, device_id=(targets[o], s), device_id_type=MESH)

    @pl.when(low_edge)
    def _():
        for o in range(nt):
            pl.semaphore_signal(barrier, inc=1, device_id=(o, lower), device_id_type=MESH)

    @pl.when(high_edge)
    def _():
        for o in range(nt):
            pl.semaphore_signal(barrier, inc=1, device_id=(o, upper), device_id_type=MESH)

    for load in loads[3:]:
        load.start()

    loads[0].wait()
    squares = []
    for j in range(width):
        block = state_v[pl.ds(j, steps, stride=width)]
        squares.append(0.5 * block * block)
    blank = jnp.zeros((steps, state_v.shape[1]), jnp.float32)
    final = state_v[(steps - 1) * width :]
    for target in range(nt):
        parts = []
        for j in range(own * target - 2, own * (target + 1) + 2):
            parts.append(squares[j] if 0 <= j < width else blank)
        tail = final[own * target : own * (target + 1)]
        tail_hi = tail.astype(jnp.bfloat16).astype(jnp.float32)
        parts += [tail_hi, tail - tail_hi]
        if steps > 2 * own:
            parts.append(blank[: steps - 2 * own])
        chunk[target] = jnp.concatenate(parts, 0).astype(jnp.bfloat16)
    edge[0] = jnp.concatenate([squares[width - 2], squares[width - 1]], 0).astype(jnp.bfloat16)
    edge[1] = jnp.concatenate([squares[0], squares[1]], 0).astype(jnp.bfloat16)

    signals = nt - 1 + jnp.where(below, 1, 0) + jnp.where(above, 1, 0)
    pl.semaphore_wait(barrier, signals)

    edge_up = pltpu.make_async_remote_copy(
        src_ref=edge.at[0],
        dst_ref=redge.at[t],
        send_sem=edge_send.at[0],
        recv_sem=edge_recv.at[t],
        device_id=(first_place[1], upper),
        device_id_type=MESH,
    )
    edge_down = pltpu.make_async_remote_copy(
        src_ref=edge.at[1],
        dst_ref=redge.at[t],
        send_sem=edge_send.at[1],
        recv_sem=edge_recv.at[t],
        device_id=(last_place[1], lower),
        device_id_type=MESH,
    )

    @pl.when(above)
    def _():
        edge_up.start()

    @pl.when(below)
    def _():
        edge_down.start()

    q_copies = []
    for o in order:
        target = targets[o]
        q_copies.append(
            pltpu.make_async_remote_copy(
                src_ref=chunk.at[ranks[o]],
                dst_ref=rq.at[t],
                send_sem=q_send.at[o],
                recv_sem=q_recv.at[o],
                device_id=(target, s),
                device_id_type=MESH,
            )
        )
    for copy in q_copies:
        copy.start()

    loads[1].wait()
    loads[2].wait()
    initial = jnp.where(t == 0, initial_v[...], 0.0)
    state = state_v[...]
    previous = jnp.concatenate([initial, state[:-width]], 0)
    forcing_v[...] = forcing_v[...] - state + previous
    for j in range(width):
        diff[j] = forcing_v[pl.ds(j, steps, stride=width)]
    d_copies = []
    for o in order:
        target = targets[o]
        d_copies.append(
            pltpu.make_async_remote_copy(
                src_ref=diff.at[pl.ds(ranks[o] * own, own)],
                dst_ref=rd.at[t],
                send_sem=d_send.at[o],
                recv_sem=d_recv.at[o],
                device_id=(target, s),
                device_id_type=MESH,
            )
        )
    for copy in d_copies:
        copy.start()
    rq[t] = chunk[rank]
    rd[t] = diff[pl.ds(start, own)]

    loads[3].wait()
    slots, size = wb.shape[0], wb.shape[2]
    for e in range(own):
        for slot in range(slots):
            wbt[e, slot * size : (slot + 1) * size] = wb[slot, e].T
    loads[6].wait()
    for e in range(own):
        wpt[e] = wp[e].T

    for copy in q_copies:
        copy.wait_recv()
    got = [rq[source].astype(jnp.float32) for source in range(nt)]
    for e in range(own + 4):
        xsq[e] = jnp.concatenate(
            [part[e * steps : (e + 1) * steps] for part in got], 0
        ).astype(jnp.bfloat16)
    lead = (own + 4) * steps
    tails = [
        part[lead : lead + own] + part[lead + own : lead + 2 * own] for part in got[:-1]
    ]

    def take_edge(place):
        for source in range(nt):
            pltpu.make_async_remote_copy(
                src_ref=edge.at[0],
                dst_ref=redge.at[source],
                send_sem=edge_send.at[0],
                recv_sem=edge_recv.at[source],
                device_id=(0, 0),
                device_id_type=MESH,
            ).wait_recv()
        edges = [redge[source].astype(jnp.float32) for source in range(nt)]
        for e in range(2):
            xsq[place + e] = jnp.concatenate(
                [part[e * steps : (e + 1) * steps] for part in edges], 0
            ).astype(jnp.bfloat16)

    @pl.when(low_edge)
    def _():
        take_edge(0)

    @pl.when(high_edge)
    def _():
        take_edge(own + 2)

    loads[7].wait()

    def coupled(field, e):
        rows = [field[e + 2 + couple_s[slot, start + e]] for slot in range(slots)]
        return jnp.dot(
            jnp.concatenate(rows, 1), wbt[e], preferred_element_type=jnp.float32
        )

    def conditioned(rounded):
        return jnp.concatenate(
            [
                jnp.dot(
                    rounded[:, e * size : (e + 1) * size],
                    wpt[e],
                    preferred_element_type=jnp.float32,
                )
                for e in range(own)
            ],
            1,
        )

    flux = [coupled(xsq, e) for e in range(own)]
    for copy in d_copies:
        copy.wait_recv()
    leading = lax.broadcasted_iota(jnp.int32, blank.shape, 0) == 0
    residual = []
    for e in range(own):
        parts = [rd[0, e]]
        for source in range(1, nt):
            carried = jnp.broadcast_to(tails[source - 1][e : e + 1], blank.shape)
            parts.append(rd[source, e] + jnp.where(leading, carried, 0.0))
        residual.append(jnp.concatenate(parts, 0) - time_step * flux[e])
    loads[4].wait()
    spectrum = transformed(matrix_v[0], jnp.concatenate(residual, 1))

    loads[5].wait()
    first_step = conditioned(spectrum.astype(jnp.bfloat16))
    swapped = jnp.concatenate([first_step[half:], first_step[:half]], 0)
    factors = factor_v[...]
    sol = factors[:, 0:1] * first_step + factors[:, 1:2] * swapped
    for e in range(own):
        xsol[2 + e] = sol[:, e * size : (e + 1) * size].astype(jnp.bfloat16)

    has_down = jnp.logical_or(rank > 0, below)
    has_up = jnp.logical_or(rank < nt - 1, above)
    down_s = jnp.where(first, lower, s)
    before = position_at(jnp.maximum(rank - 1, 0), odd, level)
    down_t = jnp.where(first, last_place[1], before)
    up_s = jnp.where(last, upper, s)
    after = position_at(jnp.minimum(rank + 1, nt - 1), odd, level)
    up_t = jnp.where(last, first_place[1], after)
    halo_down = pltpu.make_async_remote_copy(
        src_ref=xsol.at[pl.ds(2, 2)],
        dst_ref=xsol.at[pl.ds(own + 2, 2)],
        send_sem=halo_send.at[0],
        recv_sem=halo_recv.at[0],
        device_id=(down_t, down_s),
        device_id_type=MESH,
    )
    halo_up = pltpu.make_async_remote_copy(
        src_ref=xsol.at[pl.ds(own, 2)],
        dst_ref=xsol.at[pl.ds(0, 2)],
        send_sem=halo_send.at[1],
        recv_sem=halo_recv.at[1],
        device_id=(up_t, up_s),
        device_id_type=MESH,
    )

    @pl.when(has_down)
    def _():
        halo_down.start()

    @pl.when(has_up)
    def _():
        halo_up.start()

    @pl.when(jnp.logical_not(has_down))
    def _():
        xsol[0:2] = jnp.zeros((2,) + xsol.shape[1:], jnp.bfloat16)

    @pl.when(jnp.logical_not(has_up))
    def _():
        xsol[own + 2 : own + 4] = jnp.zeros((2,) + xsol.shape[1:], jnp.bfloat16)

    left = spectrum - (factors[:, 2:3] * first_step + factors[:, 3:4] * swapped)

    @pl.when(has_down)
    def _():
        halo_up.wait_recv()

    @pl.when(has_up)
    def _():
        halo_down.wait_recv()

    applied = jnp.concatenate([coupled(xsol, e) for e in range(own)], 1)
    left = left - time_step * applied
    steps_sum = first_step + conditioned(left.astype(jnp.bfloat16))
    change = transformed(matrix_v[1], steps_sum)
    for e in range(own):
        back[e] = change[:, e * size : (e + 1) * size]
    b_copies = []
    for o in order:
        target = targets[o]
        b_copies.append(
            pltpu.make_async_remote_copy(
                src_ref=back.at[:, pl.ds(pl.multiple_of(target * steps, steps), steps)],
                dst_ref=rback.at[pl.ds(start, own)],
                send_sem=b_send.at[o],
                recv_sem=b_recv.at[o],
                device_id=(target, s),
                device_id_type=MESH,
            )
        )
    for copy in b_copies:
        copy.start()
    rback[pl.ds(start, own)] = back[:, pl.ds(pl.multiple_of(t * steps, steps), steps)]
    for copy in q_copies + d_copies:
        copy.wait_send()

    @pl.when(above)
    def _():
        edge_up.wait_send()

    @pl.when(below)
    def _():
        edge_down.wait_send()

    @pl.when(has_down)
    def _():
        halo_down.wait_send()

    @pl.when(has_up)
    def _():
        halo_up.wait_send()

    for copy in b_copies:
        copy.wait_send()
    for copy in b_copies:
        copy.wait_recv()
    for j in range(width):
        rows = pl.ds(j, steps, stride=width)
        out_ref[rows] = state_v[rows] + rback[j]


def on_device_blocks(state, forcing, initial, blocks, precond, couple):
    nt, ns = lax.axis_size("tm"), lax.axis_size("space")
    steps, width, size = state.shape
    own = width // nt
    total = nt * steps
    slots = blocks.shape[0]
    matrix, factor = (jnp.asarray(table) for table in tables(total))
    far = pl.BlockSpec(memory_space=pltpu.HBM)
    rows = (own + 5) * steps
    f32, b16 = jnp.float32, jnp.bfloat16
    dma = pltpu.SemaphoreType.DMA
    flat = steps * width, size
    corrected = pl.pallas_call(
        functools.partial(kernel, (nt, ns, steps, width, own)),
        out_shape=pltpu.VMEM(flat, f32),
        in_specs=[far] * 8,
        out_specs=pl.BlockSpec(memory_space=pltpu.VMEM),
        scratch_shapes=[
            pltpu.VMEM(flat, f32),
            pltpu.VMEM(flat, f32),
            pltpu.VMEM(initial.shape, f32),
            pltpu.VMEM((slots, own, size, size), b16),
            pltpu.VMEM((own, size, size), b16),
            pltpu.VMEM((own, slots * size, size), b16),
            pltpu.VMEM((own, size, size), b16),
            pltpu.VMEM(matrix.shape, f32),
            pltpu.VMEM(factor.shape, f32),
            pltpu.SMEM(couple.shape[::-1], jnp.int32),
            pltpu.VMEM((nt, rows, size), b16),
            pltpu.VMEM((2, 2 * steps, size), b16),
            pltpu.VMEM((width, steps, size), f32),
            pltpu.VMEM((nt, rows, size), b16),
            pltpu.VMEM((nt, own, steps, size), f32),
            pltpu.VMEM((nt, 2 * steps, size), b16),
            pltpu.VMEM((own + 4, total, size), b16),
            pltpu.VMEM((own + 4, total, size), b16),
            pltpu.VMEM((own, total, size), f32),
            pltpu.VMEM((width, steps, size), f32),
            dma((8,)),
            dma((nt,)),
            dma((nt,)),
            dma((nt,)),
            dma((nt,)),
            dma((2,)),
            dma((nt,)),
            dma((2,)),
            dma((2,)),
            dma((nt,)),
            dma((nt,)),
        ],
        compiler_params=pltpu.CompilerParams(
            collective_id=0, has_side_effects=True, vmem_limit_bytes=60 * 1024 * 1024
        ),
    )(
        state.reshape(flat),
        forcing.reshape(flat),
        initial,
        blocks,
        precond,
        couple.T,
        matrix,
        factor,
    )
    return corrected.reshape(state.shape)


def on_device(state, forcing, initial, blocks, precond, couple):
    nt = lax.axis_size("tm")
    steps, width, _ = state.shape
    own = width // nt
    even_cut = width % nt == 0 and own >= 2 and 2 * own <= steps and steps % 8 == 0
    power = nt > 1 and nt & nt - 1 == 0 and nt * steps % 16 == 0
    if power and even_cut and (own + 5) * steps % 16 == 0:
        return on_device_blocks(state, forcing, initial, blocks, precond, couple)
    return on_device_steps(state, forcing, initial, blocks, precond, couple)


def solution(mesh):
    placed = (
        P("tm", "space", None),
        P("tm", "space", None),
        P("space", None),
        P(None, "space", None, None),
        P("space", None, None),
        P("space", None),
    )
    return jax.shard_map(
        on_device, mesh=mesh, in_specs=placed, out_specs=P("tm", "space", None), check_vma=False
    )
```

```python
import functools
import math

import jax
import jax.numpy as jnp
import numpy as np
from jax import lax
from jax.experimental import pallas as pl
from jax.experimental.pallas import tpu as pltpu
from jax.sharding import PartitionSpec as P

SWEEPS = 2


alpha_rate = 0.5
time_step = 0.5
relaxation = 0.7


def from_behind(block, axis, distance):
    devices = range(lax.axis_size(axis))
    route = [(i - distance, i) for i in devices if i - distance in devices]
    return lax.ppermute(block, axis, route)


def extended(block, sides, width):
    for axis, dim in sides:
        count = lax.axis_size(axis)
        forward = [(i, i + 1) for i in range(count - 1)]
        backward = [(target, source) for source, target in forward]
        low = lax.ppermute(
            lax.slice_in_dim(block, block.shape[dim] - width, None, axis=dim), axis, forward
        )
        high = lax.ppermute(lax.slice_in_dim(block, 0, width, axis=dim), axis, backward)
        block = jnp.concatenate([low, block, high], axis=dim)
    return block


def from_partner(block, axis, stride):
    count = lax.axis_size(axis)
    route = []
    for low in range(count):
        high = low | 1 << stride
        if high != low and high < count:
            route += [(low, high), (high, low)]
    return lax.ppermute(block, axis, route)


def apply_padded(padded, blocks, couple):
    width = padded.shape[1] - 4
    total = None
    for column in range(5):
        chosen = padded[:, 2 : 2 + width]
        for offset in range(-2, 3):
            picked = (couple[:, column] == offset)[None, :, None]
            chosen = jnp.where(picked, padded[:, 2 + offset : 2 + offset + width], chosen)
        term = jnp.einsum(
            "fbj,bij->fbi", chosen, blocks[column], preferred_element_type=jnp.float32
        )
        total = term if total is None else total + term
    return total


def on_device_steps(state, forcing, initial, blocks, precond, couple):
    local_steps = state.shape[0]
    devices_tm = lax.axis_size("tm")
    position = lax.axis_index("tm")
    total_steps = local_steps * devices_tm
    level_count = devices_tm.bit_length() - 1
    highest = lax.Precision.HIGHEST
    last_step = from_behind(state[-1:], "tm", 1)
    first_prev = jnp.where(position == 0, initial[None], last_step)
    previous = jnp.concatenate([first_prev, state[:-1]], 0)
    squares = (0.5 * state * state).astype(jnp.bfloat16)
    padded = extended(squares, (("space", 1),), 2)
    flux = apply_padded(padded, blocks, couple)
    residual = forcing - state + previous - time_step * flux
    steps_global = position * local_steps + jnp.arange(local_steps, dtype=jnp.int32)
    log_rate = math.log(alpha_rate) / total_steps
    scaled = residual * jnp.exp(steps_global.astype(jnp.float32) * log_rate)[:, None, None]
    cur_re = scaled
    cur_im = jnp.zeros_like(scaled)
    for level in range(level_count):
        bit_number = level_count - 1 - level
        half = 1 << bit_number
        other = from_partner(jnp.stack([cur_re, cur_im]), "tm", bit_number)
        upper = position >> bit_number & 1 == 1
        angle = -2.0 * math.pi * (position % half).astype(jnp.float32) / (2 * half)
        tw_re = jnp.cos(angle)
        tw_im = jnp.sin(angle)
        diff_re = other[0] - cur_re
        diff_im = other[1] - cur_im
        new_re = jnp.where(upper, diff_re * tw_re - diff_im * tw_im, cur_re + other[0])
        new_im = jnp.where(upper, diff_re * tw_im + diff_im * tw_re, cur_im + other[1])
        cur_re, cur_im = (new_re, new_im)
    freq_base = jnp.zeros((), jnp.int32)
    for level in range(level_count):
        freq_base = freq_base + (position >> level & 1) * (1 << level_count - 1 - level)
    part_re, part_im = (cur_re, cur_im)
    local_index = jnp.arange(local_steps, dtype=jnp.int32)
    freq = freq_base + devices_tm * local_index
    product = freq[:, None] * local_index[None, :] % total_steps
    angle_table = 2.0 * math.pi * product.astype(jnp.float32) / total_steps
    table_re = jnp.cos(angle_table)
    table_im = -jnp.sin(angle_table)
    spec_re = jnp.einsum("qm,mbc->qbc", table_re, part_re, precision=highest) - jnp.einsum(
        "qm,mbc->qbc", table_im, part_im, precision=highest
    )
    spec_im = jnp.einsum("qm,mbc->qbc", table_re, part_im, precision=highest) + jnp.einsum(
        "qm,mbc->qbc", table_im, part_re, precision=highest
    )
    theta = 2.0 * math.pi * freq.astype(jnp.float32) / total_steps
    rate = math.exp(log_rate)
    lam_re = (1.0 - rate * jnp.cos(theta))[:, None, None]
    lam_im = (rate * jnp.sin(theta))[:, None, None]
    denom = (1.0 + lam_re) ** 2 + lam_im**2
    coef_re = (1.0 + lam_re) / denom
    coef_im = -lam_im / denom
    sol_re = None
    sol_im = None
    for sweep in range(SWEEPS):
        if sweep == 0:
            res_re, res_im = (spec_re, spec_im)
        else:
            stacked = jnp.concatenate([sol_re, sol_im], 0).astype(jnp.bfloat16)
            padded_sol = extended(stacked, (("space", 1),), 2)
            applied = apply_padded(padded_sol, blocks, couple)
            res_re = (
                spec_re - (lam_re * sol_re - lam_im * sol_im) - time_step * applied[:local_steps]
            )
            res_im = (
                spec_im - (lam_re * sol_im + lam_im * sol_re) - time_step * applied[local_steps:]
            )
        rounded = jnp.concatenate([res_re, res_im], 0).astype(jnp.bfloat16)
        gres = jnp.einsum("fbj,bij->fbi", rounded, precond, preferred_element_type=jnp.float32)
        g_re = gres[:local_steps]
        g_im = gres[local_steps:]
        step_re = relaxation * (coef_re * g_re - coef_im * g_im)
        step_im = relaxation * (coef_re * g_im + coef_im * g_re)
        if sweep == 0:
            sol_re, sol_im = (step_re, step_im)
        else:
            sol_re = sol_re + step_re
            sol_im = sol_im + step_im
    back_re = (
        jnp.einsum("qm,qbc->mbc", table_re, sol_re, precision=highest)
        + jnp.einsum("qm,qbc->mbc", table_im, sol_im, precision=highest)
    ) / local_steps
    back_im = (
        jnp.einsum("qm,qbc->mbc", table_re, sol_im, precision=highest)
        - jnp.einsum("qm,qbc->mbc", table_im, sol_re, precision=highest)
    ) / local_steps
    cur_re, cur_im = (back_re, back_im)
    for bit_number in range(level_count):
        half = 1 << bit_number
        other = from_partner(jnp.stack([cur_re, cur_im]), "tm", bit_number)
        upper = position >> bit_number & 1 == 1
        angle = -2.0 * math.pi * (position % half).astype(jnp.float32) / (2 * half)
        conj_re = jnp.cos(angle)
        conj_im = -jnp.sin(angle)
        other_tw_re = other[0] * conj_re - other[1] * conj_im
        other_tw_im = other[0] * conj_im + other[1] * conj_re
        mine_tw_re = cur_re * conj_re - cur_im * conj_im
        mine_tw_im = cur_re * conj_im + cur_im * conj_re
        new_re = jnp.where(upper, 0.5 * (other[0] - mine_tw_re), 0.5 * (cur_re + other_tw_re))
        new_im = jnp.where(upper, 0.5 * (other[1] - mine_tw_im), 0.5 * (cur_im + other_tw_im))
        cur_re, cur_im = (new_re, new_im)
    change = cur_re * jnp.exp(-steps_global.astype(jnp.float32) * log_rate)[:, None, None]
    return state + change


MESH = pl.DeviceIdType.MESH


def tables(steps):
    half = steps // 2
    rate = math.exp(math.log(alpha_rate) / steps)
    step = np.arange(steps)
    freq = np.arange(half)
    angle = 2.0 * np.pi * ((freq[:, None] * step[None, :]) % steps) / steps
    cosine, sine = np.cos(angle), np.sin(angle)
    nyquist = 1.0 - 2.0 * (step % 2)
    forward = np.concatenate([cosine, nyquist[None], -sine[1:]], 0) * rate**step
    inverse = np.concatenate([2.0 * cosine, nyquist[None], -2.0 * sine[1:]], 0)
    inverse[0] = 1.0
    inverse = inverse.T / steps * (rate ** (-step))[:, None]
    theta = 2.0 * np.pi * np.arange(half + 1) / steps
    lam = 1.0 - rate * np.exp(-1j * theta)
    lam[half] = lam[half].real
    coef = relaxation / (1.0 + lam)

    def columns(factor):
        real = np.concatenate([factor.real[:half], factor.real[half:], factor.real[1:half]])
        imag = np.concatenate([[0.0], factor.imag[1:half]])
        return real, np.concatenate([-imag, imag])

    coef_own, coef_swap = columns(coef)
    lam_own, lam_swap = columns(lam * coef)
    swap = np.roll(np.eye(steps), half, 1)
    inverse = inverse @ (np.diag(coef_own) + np.diag(coef_swap) @ swap)
    lanes = -(-steps // 128) * 128
    factors = np.zeros((steps, lanes), np.float32)
    for place, column in enumerate((coef_own, coef_swap, lam_own, lam_swap)):
        factors[:, place] = column
    matrices = np.stack([np.tile(matrix, 2) for matrix in (forward, inverse)])
    return matrices.astype(np.float32), factors


def halves(field, axis):
    high = field.astype(jnp.bfloat16)
    low = (field - high.astype(jnp.float32)).astype(jnp.bfloat16)
    return jnp.concatenate([high, low], axis)


def transformed(matrix, field):
    both = halves(field, 0)
    return jnp.dot(
        halves(matrix, 1),
        jnp.concatenate([both, both], 0),
        preferred_element_type=jnp.float32,
    )


def bits_of(number, count):
    return [lax.rem(lax.div(number, 1 << i), 2) for i in range(count)]


def number_of(bits):
    return sum(bit * (1 << i) for i, bit in enumerate(bits))


def flipped(bits, mask):
    return [1 - bit if mask >> i & 1 else bit for i, bit in enumerate(bits)]


def differ(a, b):
    return a + b - 2 * a * b


def rank_at(bits, odd):
    bits = list(bits)
    for i in reversed(range(len(bits) - 1)):
        bits[i] = differ(bits[i], bits[i + 1])
    return number_of([differ(bit, odd) for bit in bits])


def position_at(rank, odd, count):
    bits = [differ(bit, odd) for bit in bits_of(rank, count)]
    for i in range(count - 1):
        bits[i] = differ(bits[i], bits[i + 1])
    return number_of(bits)


def kernel(
    sizes,
    state_h,
    forcing_h,
    initial_h,
    blocks_h,
    precond_h,
    couple_h,
    matrix_h,
    factor_h,
    out_ref,
    state_v,
    forcing_v,
    initial_v,
    wb,
    wp,
    wbt,
    wpt,
    matrix_v,
    factor_v,
    couple_s,
    chunk,
    edge,
    diff,
    rq,
    rd,
    redge,
    xsq,
    xsol,
    back,
    rback,
    local_sem,
    q_send,
    q_recv,
    d_send,
    d_recv,
    edge_send,
    edge_recv,
    halo_send,
    halo_recv,
    b_send,
    b_recv,
):
    nt, ns, steps, width, own = sizes
    total = nt * steps
    half = total // 2
    t = lax.axis_index("tm")
    s = lax.axis_index("space")
    level = nt.bit_length() - 1
    odd = lax.rem(s, 2)
    place_bits = bits_of(t, level)
    rank = rank_at(place_bits, odd)
    first, last = rank == 0, rank == nt - 1
    targets = [number_of(flipped(place_bits, o)) for o in range(nt)]
    ranks = [rank_at(flipped(place_bits, o), odd) for o in range(nt)]
    order = sorted(range(1, nt), key=lambda o: (o < 2, -(o % 2), -o))
    top = nt // 2
    first_place = odd * top, (1 - odd) * top
    last_place = first_place[1], first_place[0]
    below, above = s > 0, s < ns - 1
    lower, upper = jnp.maximum(s - 1, 0), jnp.minimum(s + 1, ns - 1)
    low_edge = jnp.logical_and(first, below)
    high_edge = jnp.logical_and(last, above)

    start = rank * own
    loads = [
        pltpu.make_async_copy(source, target, local_sem.at[place])
        for place, (source, target) in enumerate(
            (
                (state_h, state_v),
                (forcing_h, forcing_v),
                (initial_h, initial_v),
                (blocks_h.at[:, pl.ds(start, own)], wb),
                (matrix_h, matrix_v),
                (factor_h, factor_v),
                (precond_h.at[pl.ds(start, own)], wp),
                (couple_h, couple_s),
            )
        )
    ]
    for load in loads[:3]:
        load.start()

    barrier = pltpu.get_barrier_semaphore()
    for o in order:
        pl.semaphore_signal(barrier, inc=1, device_id=(targets[o], s), device_id_type=MESH)

    @pl.when(low_edge)
    def _():
        for o in range(nt):
            pl.semaphore_signal(barrier, inc=1, device_id=(o, lower), device_id_type=MESH)

    @pl.when(high_edge)
    def _():
        for o in range(nt):
            pl.semaphore_signal(barrier, inc=1, device_id=(o, upper), device_id_type=MESH)

    for load in loads[3:]:
        load.start()

    loads[0].wait()
    squares = []
    for j in range(width):
        block = state_v[pl.ds(j, steps, stride=width)]
        squares.append(0.5 * block * block)
    blank = jnp.zeros((steps, state_v.shape[1]), jnp.float32)
    final = state_v[(steps - 1) * width :]
    for target in range(nt):
        parts = []
        for j in range(own * target - 2, own * (target + 1) + 2):
            parts.append(squares[j] if 0 <= j < width else blank)
        tail = final[own * target : own * (target + 1)]
        tail_hi = tail.astype(jnp.bfloat16).astype(jnp.float32)
        parts += [tail_hi, tail - tail_hi]
        if steps > 2 * own:
            parts.append(blank[: steps - 2 * own])
        chunk[target] = jnp.concatenate(parts, 0).astype(jnp.bfloat16)
    edge[0] = jnp.concatenate([squares[width - 2], squares[width - 1]], 0).astype(jnp.bfloat16)
    edge[1] = jnp.concatenate([squares[0], squares[1]], 0).astype(jnp.bfloat16)

    signals = nt - 1 + jnp.where(below, 1, 0) + jnp.where(above, 1, 0)
    pl.semaphore_wait(barrier, signals)

    edge_up = pltpu.make_async_remote_copy(
        src_ref=edge.at[0],
        dst_ref=redge.at[t],
        send_sem=edge_send.at[0],
        recv_sem=edge_recv.at[t],
        device_id=(first_place[1], upper),
        device_id_type=MESH,
    )
    edge_down = pltpu.make_async_remote_copy(
        src_ref=edge.at[1],
        dst_ref=redge.at[t],
        send_sem=edge_send.at[1],
        recv_sem=edge_recv.at[t],
        device_id=(last_place[1], lower),
        device_id_type=MESH,
    )

    @pl.when(above)
    def _():
        edge_up.start()

    @pl.when(below)
    def _():
        edge_down.start()

    q_copies = []
    for o in order:
        target = targets[o]
        q_copies.append(
            pltpu.make_async_remote_copy(
                src_ref=chunk.at[ranks[o]],
                dst_ref=rq.at[t],
                send_sem=q_send.at[o],
                recv_sem=q_recv.at[o],
                device_id=(target, s),
                device_id_type=MESH,
            )
        )
    for copy in q_copies:
        copy.start()

    loads[1].wait()
    loads[2].wait()
    initial = jnp.where(t == 0, initial_v[...], 0.0)
    state = state_v[...]
    previous = jnp.concatenate([initial, state[:-width]], 0)
    forcing_v[...] = forcing_v[...] - state + previous
    for j in range(width):
        diff[j] = forcing_v[pl.ds(j, steps, stride=width)]
    d_copies = []
    for o in order:
        target = targets[o]
        d_copies.append(
            pltpu.make_async_remote_copy(
                src_ref=diff.at[pl.ds(ranks[o] * own, own)],
                dst_ref=rd.at[t],
                send_sem=d_send.at[o],
                recv_sem=d_recv.at[o],
                device_id=(target, s),
                device_id_type=MESH,
            )
        )
    for copy in d_copies:
        copy.start()
    rq[t] = chunk[rank]
    rd[t] = diff[pl.ds(start, own)]

    loads[3].wait()
    slots, size = wb.shape[0], wb.shape[2]
    for e in range(own):
        for slot in range(slots):
            wbt[e, slot * size : (slot + 1) * size] = wb[slot, e].T
    loads[6].wait()
    for e in range(own):
        wpt[e] = wp[e].T

    for copy in q_copies:
        copy.wait_recv()
    got = [rq[source].astype(jnp.float32) for source in range(nt)]
    for e in range(own + 4):
        xsq[e] = jnp.concatenate(
            [part[e * steps : (e + 1) * steps] for part in got], 0
        ).astype(jnp.bfloat16)
    lead = (own + 4) * steps
    tails = [
        part[lead : lead + own] + part[lead + own : lead + 2 * own] for part in got[:-1]
    ]

    def take_edge(place):
        for source in range(nt):
            pltpu.make_async_remote_copy(
                src_ref=edge.at[0],
                dst_ref=redge.at[source],
                send_sem=edge_send.at[0],
                recv_sem=edge_recv.at[source],
                device_id=(0, 0),
                device_id_type=MESH,
            ).wait_recv()
        edges = [redge[source].astype(jnp.float32) for source in range(nt)]
        for e in range(2):
            xsq[place + e] = jnp.concatenate(
                [part[e * steps : (e + 1) * steps] for part in edges], 0
            ).astype(jnp.bfloat16)

    @pl.when(low_edge)
    def _():
        take_edge(0)

    @pl.when(high_edge)
    def _():
        take_edge(own + 2)

    loads[7].wait()

    def coupled(field, e):
        rows = [field[e + 2 + couple_s[slot, start + e]] for slot in range(slots)]
        return jnp.dot(
            jnp.concatenate(rows, 1), wbt[e], preferred_element_type=jnp.float32
        )

    def conditioned(rounded):
        return jnp.concatenate(
            [
                jnp.dot(
                    rounded[:, e * size : (e + 1) * size],
                    wpt[e],
                    preferred_element_type=jnp.float32,
                )
                for e in range(own)
            ],
            1,
        )

    flux = [coupled(xsq, e) for e in range(own)]
    for copy in d_copies:
        copy.wait_recv()
    leading = lax.broadcasted_iota(jnp.int32, blank.shape, 0) == 0
    residual = []
    for e in range(own):
        parts = [rd[0, e]]
        for source in range(1, nt):
            carried = jnp.broadcast_to(tails[source - 1][e : e + 1], blank.shape)
            parts.append(rd[source, e] + jnp.where(leading, carried, 0.0))
        residual.append(jnp.concatenate(parts, 0) - time_step * flux[e])
    loads[4].wait()
    spectrum = transformed(matrix_v[0], jnp.concatenate(residual, 1))

    loads[5].wait()
    first_step = conditioned(spectrum.astype(jnp.bfloat16))
    swapped = jnp.concatenate([first_step[half:], first_step[:half]], 0)
    factors = factor_v[...]
    sol = factors[:, 0:1] * first_step + factors[:, 1:2] * swapped
    for e in range(own):
        xsol[2 + e] = sol[:, e * size : (e + 1) * size].astype(jnp.bfloat16)

    has_down = jnp.logical_or(rank > 0, below)
    has_up = jnp.logical_or(rank < nt - 1, above)
    down_s = jnp.where(first, lower, s)
    before = position_at(jnp.maximum(rank - 1, 0), odd, level)
    down_t = jnp.where(first, last_place[1], before)
    up_s = jnp.where(last, upper, s)
    after = position_at(jnp.minimum(rank + 1, nt - 1), odd, level)
    up_t = jnp.where(last, first_place[1], after)
    halo_down = pltpu.make_async_remote_copy(
        src_ref=xsol.at[pl.ds(2, 2)],
        dst_ref=xsol.at[pl.ds(own + 2, 2)],
        send_sem=halo_send.at[0],
        recv_sem=halo_recv.at[0],
        device_id=(down_t, down_s),
        device_id_type=MESH,
    )
    halo_up = pltpu.make_async_remote_copy(
        src_ref=xsol.at[pl.ds(own, 2)],
        dst_ref=xsol.at[pl.ds(0, 2)],
        send_sem=halo_send.at[1],
        recv_sem=halo_recv.at[1],
        device_id=(up_t, up_s),
        device_id_type=MESH,
    )

    @pl.when(has_down)
    def _():
        halo_down.start()

    @pl.when(has_up)
    def _():
        halo_up.start()

    @pl.when(jnp.logical_not(has_down))
    def _():
        xsol[0:2] = jnp.zeros((2,) + xsol.shape[1:], jnp.bfloat16)

    @pl.when(jnp.logical_not(has_up))
    def _():
        xsol[own + 2 : own + 4] = jnp.zeros((2,) + xsol.shape[1:], jnp.bfloat16)

    left = spectrum - (factors[:, 2:3] * first_step + factors[:, 3:4] * swapped)

    @pl.when(has_down)
    def _():
        halo_up.wait_recv()

    @pl.when(has_up)
    def _():
        halo_down.wait_recv()

    applied = jnp.concatenate([coupled(xsol, e) for e in range(own)], 1)
    left = left - time_step * applied
    rounded = left.astype(jnp.bfloat16)
    b_copies = []
    for e in range(own):
        columns = slice(e * size, (e + 1) * size)
        second_step = jnp.dot(rounded[:, columns], wpt[e], preferred_element_type=jnp.float32)
        back[e] = transformed(matrix_v[1], first_step[:, columns] + second_step)
        for o in order:
            piece = pl.ds(pl.multiple_of(targets[o] * steps, steps), steps)
            copy = pltpu.make_async_remote_copy(
                src_ref=back.at[e, piece],
                dst_ref=rback.at[start + e],
                send_sem=b_send.at[e, o],
                recv_sem=b_recv.at[e, o],
                device_id=(targets[o], s),
                device_id_type=MESH,
            )
            copy.start()
            b_copies.append(copy)
    rback[pl.ds(start, own)] = back[:, pl.ds(pl.multiple_of(t * steps, steps), steps)]
    for copy in q_copies + d_copies:
        copy.wait_send()

    @pl.when(above)
    def _():
        edge_up.wait_send()

    @pl.when(below)
    def _():
        edge_down.wait_send()

    @pl.when(has_down)
    def _():
        halo_down.wait_send()

    @pl.when(has_up)
    def _():
        halo_up.wait_send()

    for copy in b_copies:
        copy.wait_send()
    for copy in b_copies:
        copy.wait_recv()
    for j in range(width):
        rows = pl.ds(j, steps, stride=width)
        out_ref[rows] = state_v[rows] + rback[j]


def on_device_blocks(state, forcing, initial, blocks, precond, couple):
    nt, ns = lax.axis_size("tm"), lax.axis_size("space")
    steps, width, size = state.shape
    own = width // nt
    total = nt * steps
    slots = blocks.shape[0]
    matrix, factor = (jnp.asarray(table) for table in tables(total))
    far = pl.BlockSpec(memory_space=pltpu.HBM)
    rows = (own + 5) * steps
    f32, b16 = jnp.float32, jnp.bfloat16
    dma = pltpu.SemaphoreType.DMA
    flat = steps * width, size
    corrected = pl.pallas_call(
        functools.partial(kernel, (nt, ns, steps, width, own)),
        out_shape=pltpu.VMEM(flat, f32),
        in_specs=[far] * 8,
        out_specs=pl.BlockSpec(memory_space=pltpu.VMEM),
        scratch_shapes=[
            pltpu.VMEM(flat, f32),
            pltpu.VMEM(flat, f32),
            pltpu.VMEM(initial.shape, f32),
            pltpu.VMEM((slots, own, size, size), b16),
            pltpu.VMEM((own, size, size), b16),
            pltpu.VMEM((own, slots * size, size), b16),
            pltpu.VMEM((own, size, size), b16),
            pltpu.VMEM(matrix.shape, f32),
            pltpu.VMEM(factor.shape, f32),
            pltpu.SMEM(couple.shape[::-1], jnp.int32),
            pltpu.VMEM((nt, rows, size), b16),
            pltpu.VMEM((2, 2 * steps, size), b16),
            pltpu.VMEM((width, steps, size), f32),
            pltpu.VMEM((nt, rows, size), b16),
            pltpu.VMEM((nt, own, steps, size), f32),
            pltpu.VMEM((nt, 2 * steps, size), b16),
            pltpu.VMEM((own + 4, total, size), b16),
            pltpu.VMEM((own + 4, total, size), b16),
            pltpu.VMEM((own, total, size), f32),
            pltpu.VMEM((width, steps, size), f32),
            dma((8,)),
            dma((nt,)),
            dma((nt,)),
            dma((nt,)),
            dma((nt,)),
            dma((2,)),
            dma((nt,)),
            dma((2,)),
            dma((2,)),
            dma((own, nt)),
            dma((own, nt)),
        ],
        compiler_params=pltpu.CompilerParams(
            collective_id=0, has_side_effects=True, vmem_limit_bytes=60 * 1024 * 1024
        ),
    )(
        state.reshape(flat),
        forcing.reshape(flat),
        initial,
        blocks,
        precond,
        couple.T,
        matrix,
        factor,
    )
    return corrected.reshape(state.shape)


def on_device(state, forcing, initial, blocks, precond, couple):
    nt = lax.axis_size("tm")
    steps, width, _ = state.shape
    own = width // nt
    even_cut = width % nt == 0 and own >= 2 and 2 * own <= steps and steps % 8 == 0
    power = nt > 1 and nt & nt - 1 == 0 and nt * steps % 16 == 0
    if power and even_cut and (own + 5) * steps % 16 == 0:
        return on_device_blocks(state, forcing, initial, blocks, precond, couple)
    return on_device_steps(state, forcing, initial, blocks, precond, couple)


def solution(mesh):
    placed = (
        P("tm", "space", None),
        P("tm", "space", None),
        P("space", None),
        P(None, "space", None, None),
        P("space", None, None),
        P("space", None),
    )
    return jax.shard_map(
        on_device, mesh=mesh, in_specs=placed, out_specs=P("tm", "space", None), check_vma=False
    )
```
